256 devices in a mesh: tm: 128 (over x, y, z), chan: 2 (over core).
Axes of the slice: x: 4, y: 4, z: 8, core: 2. Of those that a mesh axis runs over, the one named last changes fastest.
Arguments:
- record: float32 [2048, 32768], P('chan', 'tm'), may hold values from -90 to 90
- gauge_table: float32 [6, 8], replicated, may hold values from 0.7 to 1.4
- gauge_index: int32 [6, 32], replicated, may hold values from 0 to 7
Outputs:
- denoised: float32 [2048, 32768], P('chan', 'tm')
The draws below stay inside these ranges and needn't reach their ends.
Inputs may be any that keep to these rules, and one draw needn't show every extreme that they name: gauge_index[l, b] picks the entry of gauge_table[l] for channel block b at level l.
All inputs are finite; a program needn't handle non-finite values.
Results may differ from the reference program's by a relative error of at most 0.0001.
Values sent between devices are 32-bit elements; how exact they have to be, the bound alone decides.
No kernel may reach another device: no remote copies, remote signals or barrier semaphores. Data moves between devices by JAX's collectives and lax.ppermute only.
A program may use at most 64 MiB of HBM per device.

```python
import math
import jax
import jax.numpy as jnp
from jax import lax

C = 2048
LEVELS = 6
COARSE = 6
GTAB = 8
S = 32768
NBLK = 32


def draw_record(key, part):
    key = jax.random.fold_in(key, 11)
    noise_key, chan_key, time_key = jax.random.split(key, 3)
    chan_scale = jnp.exp(jax.random.uniform(chan_key, (C, 1), jnp.float32, -1.15, 1.15))
    time_frac = lax.broadcasted_iota(jnp.float32, (1, S), 1) / S
    time_scale = jnp.exp(jax.random.uniform(time_key, (1, S), jnp.float32, -1.15, 1.15) + 1.1 * time_frac - 0.55)
    noise_field = jnp.clip(jax.random.normal(noise_key, (C, S), jnp.float32), -5.0, 5.0) + 0.3
    return noise_field * chan_scale * time_scale


def set_ends(values, key, low, largest):
    index_at = [jax.random.randint(jax.random.fold_in(key, axis), (), 0, length) for axis, length in enumerate(values.shape)]
    longest = values.shape.index(max(values.shape))
    next_to = index_at[:longest] + [(index_at[longest] + 1) % values.shape[longest]] + index_at[longest + 1:]
    return values.at[tuple(index_at)].set(low).at[tuple(next_to)].set(largest)


def setup_inputs(seed: int = 0) -> dict:
    splits = jax.random.split(jax.random.key(seed), 4)
    return {
        "record": draw_record(jax.random.fold_in(splits[3], 71), 0),
        "gauge_table": jnp.clip(jnp.exp(jax.random.uniform(splits[1], (LEVELS, GTAB), jnp.float32, math.log(0.7), math.log(1.4))), 0.7, 1.4),
        "gauge_index": set_ends(jax.random.randint(splits[2], (LEVELS, NBLK), 0, GTAB), jax.random.fold_in(splits[2], 1), 0, GTAB - 1).astype(jnp.int32),
    }


lift_predict_one = -1.586134342059924
lift_update_one = -0.052980118572961
lift_predict_two = 0.882911075530934
lift_update_two = 0.443506852043971
lift_scale = 1.149604398860241
noise_floor = 1e-06

def shifted(values, direction, forward, keep_mask):
    length = values.shape[direction]
    if forward:
        moved_values = jnp.concatenate((lax.slice_in_dim(values, 1, length, axis=direction), lax.slice_in_dim(values, length - 1, length, axis=direction)), axis=direction)
    else:
        moved_values = jnp.concatenate((lax.slice_in_dim(values, 0, 1, axis=direction), lax.slice_in_dim(values, 0, length - 1, axis=direction)), axis=direction)
    return jnp.where(keep_mask, values, moved_values)

def edge_masks(length, direction, low_edge, high_edge):
    extent_shape = (length, 1) if direction == 0 else (1, length)
    positions = lax.broadcasted_iota(jnp.int32, extent_shape, direction)
    return (jnp.logical_and(low_edge, positions == 2), jnp.logical_and(high_edge, positions == length - 3))

def center(values, direction):
    length = values.shape[direction]
    return lax.slice_in_dim(values, 2, length - 2, axis=direction)

def lift_forward(even_part, odd_part, weights, direction, low_edge, high_edge):
    low_mask, high_mask = edge_masks(even_part.shape[direction], direction, low_edge, high_edge)
    odd_part = odd_part + lift_predict_one * weights * (even_part + shifted(even_part, direction, True, high_mask))
    even_part = even_part + lift_update_one * weights * (shifted(odd_part, direction, False, low_mask) + odd_part)
    odd_part = odd_part + lift_predict_two * weights * (even_part + shifted(even_part, direction, True, high_mask))
    even_part = even_part + lift_update_two * weights * (shifted(odd_part, direction, False, low_mask) + odd_part)
    return (lift_scale * center(even_part, direction), center(odd_part, direction) / lift_scale)

def lift_inverse(low_band, high_band, weights, direction, low_edge, high_edge):
    low_mask, high_mask = edge_masks(low_band.shape[direction], direction, low_edge, high_edge)
    even_part = low_band / lift_scale
    odd_part = high_band * lift_scale
    even_part = even_part - lift_update_two * weights * (shifted(odd_part, direction, False, low_mask) + odd_part)
    odd_part = odd_part - lift_predict_two * weights * (even_part + shifted(even_part, direction, True, high_mask))
    even_part = even_part - lift_update_one * weights * (shifted(odd_part, direction, False, low_mask) + odd_part)
    odd_part = odd_part - lift_predict_one * weights * (even_part + shifted(even_part, direction, True, high_mask))
    return (center(even_part, direction), center(odd_part, direction))

def alternate(even_part, odd_part, direction):
    if direction == 0:
        return jnp.stack((even_part, odd_part), axis=1).reshape(2 * even_part.shape[0], even_part.shape[1])
    return jnp.stack((even_part, odd_part), axis=2).reshape(even_part.shape[0], 2 * even_part.shape[1])

def pad_pairs(values, direction):
    widths = ((2, 2), (0, 0)) if direction == 0 else ((0, 0), (2, 2))
    return jnp.pad(values, widths)

def split_pairs(values, direction):
    if direction == 0:
        return (values[0::2, :], values[1::2, :])
    return (values[:, 0::2], values[:, 1::2])

def full_forward(values, weights, direction):
    even_part, odd_part = split_pairs(values, direction)
    return lift_forward(pad_pairs(even_part, direction), pad_pairs(odd_part, direction), weights, direction, True, True)

def full_inverse(low_band, high_band, weights, direction):
    even_part, odd_part = lift_inverse(pad_pairs(low_band, direction), pad_pairs(high_band, direction), weights, direction, True, True)
    return alternate(even_part, odd_part, direction)

def level_weights(block_weights, level_index):
    pair_weights = jnp.repeat(block_weights[level_index], 2 ** (LEVELS - 1 - level_index))
    return jnp.pad(pair_weights, 2, mode='edge')

def shrink(band_values, limit_value):
    return band_values - jnp.clip(band_values, -limit_value, limit_value)

def squares(band_values):
    return jnp.sum(band_values * band_values)

def reference(record, gauge_table, gauge_index):
    matches = (gauge_index[:, :, None] == jnp.arange(GTAB, dtype=jnp.int32)[None, None, :]).astype(gauge_table.dtype)
    block_weights = lax.optimization_barrier(jnp.sum(matches * gauge_table[:, None, :], axis=2))
    current = record
    details = []
    level_sums = []
    for level_index in range(LEVELS):
        time_low, time_high = full_forward(current, 1.0, 1)
        half_width = time_low.shape[1]
        combined = jnp.concatenate((time_low, time_high), axis=1)
        chan_low, chan_high = full_forward(combined, level_weights(block_weights, level_index)[:, None], 0)
        level_bands = (chan_low[:, half_width:], chan_high[:, :half_width], chan_high[:, half_width:])
        details.append(level_bands)
        level_sums.append(squares(level_bands[0]) + squares(level_bands[1]) + squares(level_bands[2]))
        current = chan_low[:, :half_width]
    coarse_highs = []
    coarse_total = 0.0
    coarse_count = 0
    for coarse_step in range(COARSE):
        current, high_band = full_forward(current, 1.0, 1)
        coarse_highs.append(high_band)
        coarse_total = coarse_total + squares(high_band)
        coarse_count = coarse_count + high_band.size
    coarse_limit = jnp.sqrt(coarse_total / coarse_count + noise_floor)
    for coarse_step in reversed(range(COARSE)):
        current = full_inverse(current, shrink(coarse_highs[coarse_step], coarse_limit), 1.0, 1)
    for level_index in reversed(range(LEVELS)):
        level_bands = details[level_index]
        level_limit = jnp.sqrt(level_sums[level_index] / (3 * level_bands[0].size) + noise_floor)
        time_detail = shrink(level_bands[0], level_limit)
        channel_detail = shrink(level_bands[1], level_limit)
        both_detail = shrink(level_bands[2], level_limit)
        half_width = current.shape[1]
        chan_low = jnp.concatenate((current, time_detail), axis=1)
        chan_high = jnp.concatenate((channel_detail, both_detail), axis=1)
        combined = full_inverse(chan_low, chan_high, level_weights(block_weights, level_index)[:, None], 0)
        current = full_inverse(combined[:, :half_width], combined[:, half_width:], 1.0, 1)
    return current
```

```python
import functools

import jax
import jax.numpy as jnp
import ml_dtypes
import numpy as np
from jax import lax
from jax.experimental import pallas as pl
from jax.experimental.pallas import tpu as pltpu
from jax.sharding import PartitionSpec as P

LEVELS = 6
COARSE = 6
GTAB = 8
NBLK = 32
C = 2048
S = 32768
NT = 128
OWN = 1024
HALO = 512
SEG = 192
A1 = -1.586134342059924
B1 = -0.052980118572961
A2 = 0.882911075530934
B2 = 0.443506852043971
KS = 1.149604398860241
FLOOR = 1e-06
F32 = jnp.float32
BF16 = jnp.bfloat16


def _next(e):
    return np.concatenate((e[1:], e[-1:]))


def _prev(o):
    return np.concatenate((o[:1], o[:-1]))


def _lift(x):
    e, o = x[0::2], x[1::2]
    o = o + A1 * (e + _next(e))
    e = e + B1 * (_prev(o) + o)
    o = o + A2 * (e + _next(e))
    e = e + B2 * (_prev(o) + o)
    return KS * e, o / KS


def _unlift(low, high):
    e, o = low / KS, high * KS
    e = e - B2 * (_prev(o) + o)
    o = o - A2 * (e + _next(e))
    e = e - B1 * (_prev(o) + o)
    o = o - A1 * (e + _next(e))
    return np.stack((e, o), axis=1).reshape((2 * e.shape[0],) + e.shape[1:])


def _forward(inputs, lows, highs, rows, cols, start, stop, scale):
    pairs = list(lows) + list(highs)
    a = max(2 * min(pairs) - 16, start)
    b = min(2 * max(pairs) + 16, stop)
    low, high = _lift(np.eye(b - a))
    out = np.zeros((rows, cols))
    for band, places in ((low, lows), (high, highs)):
        for pair, col in places.items():
            if a <= 2 * pair < b:
                line = band[pair - a // 2]
                for i in np.nonzero(line)[0]:
                    out[inputs[a + int(i)], col] += scale * line[i]
    return out


def _inverse(lows, highs, outputs, rows, cols, start, stop, scale):
    a = max(2 * (min(outputs) // 2) - 16, start) // 2
    b = min(2 * (max(outputs) // 2) + 18, stop) // 2
    n = b - a
    eye, zero = np.eye(n), np.zeros((n, n))
    from_low, from_high = _unlift(eye, zero), _unlift(zero, eye)
    out = np.zeros((rows, cols))
    for sample, col in outputs.items():
        if 2 * a <= sample < 2 * b:
            for lines, places in ((from_low, lows), (from_high, highs)):
                line = lines[sample - 2 * a]
                for i in np.nonzero(line)[0]:
                    out[places[a + int(i)], col] += scale * line[i]
    return out


def _pair(m):
    hi = m.astype(ml_dtypes.bfloat16)
    lo = (m - hi.astype(np.float64)).astype(ml_dtypes.bfloat16)
    return np.stack((hi, lo))


def _run(first, last, at):
    return {k: at + k - first for k in range(first, last)}


OWN_LOW0 = _run(2, 126, 2)
OWN_HIGH0 = _run(2, 126, 130)
RIM_LOW0 = {**_run(-8, 2, 0), **_run(126, 137, 10)}
RIM_HIGH0 = {**_run(-2, 2, 32), **_run(126, 130, 36)}
RIM_IN0 = {**_run(0, 32, 0), **_run(-32, 0, 32), **_run(256, 288, 64), **_run(224, 256, 96)}
IN1 = {**OWN_LOW0, **{k: 128 + v for k, v in RIM_LOW0.items()}}
LOW1 = {**_run(0, 64, 0), **_run(-2, 0, 134), **_run(64, 67, 136)}
HIGH1 = {**_run(0, 64, 64), **_run(-3, 0, 128), **_run(64, 67, 131)}
IN2 = {**_run(0, 128, 0), **_run(-64, 0, 128), **_run(128, 192, 192), **_run(-128, -64, 256)}
LOW2 = _run(-52, 85, 0)
HIGH2 = _run(-3, 36, 140)
LOW3 = _run(-24, 41, 0)
HIGH3 = _run(-3, 20, 70)
LOW4 = _run(-10, 19, 0)
HIGH4 = _run(-3, 12, 40)
LOW5 = _run(-2, 8, 0)
HIGH5 = _run(-3, 8, 16)


def _edges(variants, width):
    far = 1 << 20
    if variants == 3:
        return ((0, far), (-far, far), (-far, width))
    return ((0, far), (-width, far), (-far, far), (-far, 2 * width), (-far, width))


def _table(build, variants, width):
    return np.stack([_pair(build(*edge)) for edge in _edges(variants, width)])


@functools.cache
def _tables():
    fw, inv = _forward, _inverse
    out = {}
    out["t0"] = _pair(fw(_run(0, 256, 0), OWN_LOW0, OWN_HIGH0, 256, 256, -(1 << 20), 1 << 20, 1.0))
    out["t0r"] = _table(lambda a, b: fw(RIM_IN0, RIM_LOW0, RIM_HIGH0, 128, 128, a, b, 1.0), 3, 256)
    out["t1"] = _table(lambda a, b: fw(IN1, LOW1, HIGH1, 256, 256, a, b, KS), 3, 128)
    out["t2"] = _table(lambda a, b: fw(IN2, LOW2, HIGH2, 384, 256, a, b, KS), 5, 64)
    out["t3"] = _table(lambda a, b: fw(LOW2, LOW3, HIGH3, 256, 128, a, b, KS), 5, 32)
    out["t4"] = _table(lambda a, b: fw(LOW3, LOW4, HIGH4, 128, 128, a, b, KS), 5, 16)

    def level5(a, b):
        m = fw(LOW4, LOW5, HIGH5, 128, 256, a, b, KS)
        for i in range(128):
            m[:, 128 + i] = m[:, LOW5[i % 4]]
        return m

    out["t5"] = _table(level5, 5, 8)

    def low_part(places, first, last):
        return {k: places[k] for k in range(first, last)}

    full0 = {**OWN_LOW0, **{k: 256 + v for k, v in RIM_LOW0.items() if -2 <= k < 2 or 126 <= k < 130}}
    high0 = {**OWN_HIGH0, **{k: 256 + v for k, v in RIM_HIGH0.items()}}
    out["s0"] = _table(lambda a, b: inv(full0, high0, _run(0, 256, 0), 384, 256, a, b, 1.0), 3, 256)
    out["s1"] = _table(
        lambda a, b: inv(LOW1, HIGH1, low_part(IN1, -1, 130), 256, 256, a, b, 1.0 / KS), 3, 128
    )
    out["s2"] = _table(
        lambda a, b: inv(low_part(LOW2, -2, 36), HIGH2, low_part(LOW1, -2, 67), 256, 256, a, b, 1.0 / KS),
        3,
        64,
    )
    out["s3"] = _table(
        lambda a, b: inv(low_part(LOW3, -2, 20), HIGH3, low_part(LOW2, -2, 36), 128, 128, a, b, 1.0 / KS),
        3,
        32,
    )
    out["s4"] = _table(
        lambda a, b: inv(low_part(LOW4, -2, 12), HIGH4, low_part(LOW3, -2, 20), 128, 128, a, b, 1.0 / KS),
        3,
        16,
    )
    out["s5"] = _table(
        lambda a, b: inv(low_part(LOW5, -2, 8), HIGH5, low_part(LOW4, -2, 12), 128, 128, a, b, 1.0 / KS),
        3,
        8,
    )
    n = S >> LEVELS
    bands = []
    current = np.eye(n)
    for _ in range(COARSE):
        current, high = _lift(current)
        bands.append(high)
    coarse = np.concatenate([current] + bands[::-1])
    order = (np.arange(n) % NT) * 4 + np.arange(n) // NT
    out["w"] = _pair((KS * coarse.T)[order])
    last = n >> COARSE
    current = np.eye(n)[:last]
    for step in range(COARSE):
        size = last << step
        current = _unlift(current, np.eye(n)[size : 2 * size])
    rebuilt = np.zeros((n + 32, n))
    rebuilt[2 : n + 2] = current / KS
    rebuilt = np.moveaxis(_pair(rebuilt), 0, 0)
    pieces = np.zeros((NT, 2, 16, n), ml_dtypes.bfloat16)
    for t in range(NT):
        pieces[t, :, :10] = rebuilt[:, 4 * t : 4 * t + 10]
    out["v"] = pieces
    return out


def _lane_mask(*places):
    row = np.zeros(128, np.float32)
    for lanes in places:
        row[list(lanes)] = 1.0
    return row


@functools.cache
def _lane_masks():
    def own(places, first, last, base):
        return [v - base for k, v in places.items() if first <= k < last and 0 <= v - base < 128]

    rows = []
    rows.append(_lane_mask(own(RIM_HIGH0, 0, 128, 0)))
    rows.append(_lane_mask(own(RIM_HIGH0, 0, 128, 0), own(RIM_LOW0, 0, 128, 0)))
    for low, high, n in ((LOW1, HIGH1, 64), (LOW2, HIGH2, 32), (LOW3, HIGH3, 16), (LOW4, HIGH4, 8), (LOW5, HIGH5, 4)):
        rows.append(_lane_mask(own(high, 0, n, 0)))
        rows.append(_lane_mask(own(high, 0, n, 0), own(low, 0, n, 0)))
    rows.append(_lane_mask(own(HIGH2, 0, 32, 128)))
    rows.append(_lane_mask(own(HIGH2, 0, 32, 128)))
    out = np.zeros((16, 128), np.float32)
    out[: len(rows)] = np.stack(rows)
    return out


def _dot3(x, t):
    hi = x.astype(BF16)
    lo = (x - hi.astype(F32)).astype(BF16)
    d = functools.partial(jnp.dot, preferred_element_type=F32)
    return d(hi, t[0]) + d(lo, t[0]) + d(hi, t[1])


def _time(load, count, t, store, step):
    for j in range(0, count, step):
        x = load(j, step)
        y = _dot3(x.reshape(step * 8, x.shape[2]), t)
        store(j, step, y.reshape(step, 8, y.shape[1]))


def _sublane(lanes):
    return lax.broadcasted_iota(jnp.int32, (8, lanes), 0)


def _lane(rows=8):
    return lax.broadcasted_iota(jnp.int32, (rows, 128), 1)


def _wide(v, lanes):
    return v if lanes == 128 else jnp.concatenate([v] * (lanes // 128), axis=1)


class _Wrap:
    def __init__(self, lanes):
        sub = _sublane(lanes)
        self.last, self.first = sub == 7, sub == 0

    def after(self, first, last):
        return jnp.where(self.last, last, pltpu.roll(first, 7, 0))

    def before(self, last, first):
        return jnp.where(self.first, first, pltpu.roll(last, 1, 0))


def _coefs(w_ref, level, lanes):
    return [[_wide(c * w_ref[level, q], lanes) for q in range(3)] for c in (A1, B1, A2, B2)]


def _chan_forward(get, n, w_ref, level, lanes, put_low, put_high):
    wrap = _Wrap(lanes)
    ca, cb, cc, cd = _coefs(w_ref, level, lanes)
    per = n // 3
    first = get(0)
    e, o1, e1, o2 = {0: first}, {}, {}, {}

    def high(k, v):
        o2[k] = v
        put_high(k, k // per, v)

    def low(k):
        put_low(k, k // per, e1[k] + cd[k // per] * (o2[k - 1] + o2[k]))

    for k in range(n):
        q = k // per
        e[k + 1] = get(2 * k + 2) if k + 1 < n else wrap.after(first, e[k])
        o1[k] = get(2 * k + 1) + ca[q] * (e[k] + e[k + 1])
        if k >= 1:
            e1[k] = e[k] + cb[q] * (o1[k - 1] + o1[k])
        if k >= 2:
            high(k - 1, o1[k - 1] + cc[(k - 1) // per] * (e1[k - 1] + e1[k]))
        if k >= 3:
            low(k - 1)
    e1[0] = first + cb[0] * (wrap.before(o1[n - 1], o1[0]) + o1[0])
    high(0, o1[0] + cc[0] * (e1[0] + e1[1]))
    high(n - 1, o1[n - 1] + cc[2] * (e1[n - 1] + wrap.after(e1[0], e1[n - 1])))
    o2[-1] = wrap.before(o2[n - 1], o2[0])
    for k in (0, 1, n - 1):
        low(k)


def _chan_inverse(get_low, get_high, n, w_ref, level, lanes, put):
    wrap = _Wrap(lanes)
    ca, cb, cc, cd = _coefs(w_ref, level, lanes)
    per = n // 3
    o = {0: get_high(0)}
    o[-1] = wrap.before(get_high(n - 1), o[0])
    e1, o1, e2 = {}, {}, {}

    def even(k):
        e2[k] = e1[k] - cb[k // per] * (o1[k - 1] + o1[k])
        put(2 * k, e2[k])

    def odd(k):
        put(2 * k + 1, o1[k] - ca[k // per] * (e2[k] + e2[k + 1]))

    for k in range(n):
        q = k // per
        if k:
            o[k] = get_high(k)
        e1[k] = get_low(k) - cd[q] * (o[k - 1] + o[k])
        if k >= 1:
            o1[k - 1] = o[k - 1] - cc[(k - 1) // per] * (e1[k - 1] + e1[k])
        if k >= 2:
            even(k - 1)
        if k >= 3:
            odd(k - 2)
    o1[n - 1] = o[n - 1] - cc[2] * (e1[n - 1] + wrap.after(e1[0], e1[n - 1]))
    o1[-1] = wrap.before(o1[n - 1], o1[0])
    even(n - 1)
    if n > 2:
        odd(n - 2)
    even(0)
    odd(0)
    e2[n] = wrap.after(e2[0], e2[n - 1])
    odd(n - 1)


class _Squares:
    def __init__(self):
        self.acc = {}

    def add(self, key, v):
        self.acc[key] = v * v if key not in self.acc else self.acc[key] + v * v

    def total(self, rows_ref, tiles):
        out = None
        for q in range(3):
            part = None
            for (band, tile), lanes in tiles.items():
                v = self.acc[(band, tile, q)] * (KS * KS if band == "low" else 1.0 / (KS * KS))
                v = v if lanes is None else v * lanes
                part = v if part is None else part + v
            part = part * rows_ref[q]
            out = part if out is None else out + part
        return out


def _tile(v, i):
    return v[:, 128 * i : 128 * (i + 1)]


def _pack_kernel(sc, x, recv, xs, right, left, xa, xb, sems):
    core = sc[0]
    at_own = pl.multiple_of(core * HALO, 8)
    at_recv = pl.multiple_of((1 - core) * OWN, 8)
    copies = []
    for i, buf in enumerate((xa, xb)):
        lanes = pl.ds(128 * i, 128)
        copies.append(pltpu.make_async_copy(x.at[:, lanes], buf.at[pl.ds(at_own, OWN)], sems.at[2 * i]))
        copies.append(pltpu.make_async_copy(recv.at[:, lanes], buf.at[pl.ds(at_recv, HALO)], sems.at[2 * i + 1]))
    for c in copies:
        c.start()
    for c in copies:
        c.wait()
    group = _lane() // 32
    for i in range(48):
        to_right, to_left = None, None
        for g in range(4):
            j = 48 * g + i
            a = xa[pl.ds(j, 8, stride=SEG), :]
            b = xb[pl.ds(j, 8, stride=SEG), :]
            xs[j, :, 0:128] = a
            xs[j, :, 128:256] = b
            a = pltpu.roll(a, 32 * g, 1) if g else a
            b = pltpu.roll(b, (32 * g + 32) % 128, 1) if g != 3 else b
            to_left = a if to_left is None else jnp.where(group == g, a, to_left)
            to_right = b if to_right is None else jnp.where(group == g, b, to_right)
        right[i] = to_right
        left[i] = to_left


def _own_kernel(xs, t, w, rows, low, dlow, dhigh, sums, y):
    def store(j, step, v):
        y[pl.ds(j, step)] = v

    _time(lambda j, step: xs[pl.ds(j, step)], SEG, t, store, 24)
    sq = _Squares()

    def put_low(k, q, v):
        low[k] = _tile(v, 0)
        dlow[k] = _tile(v, 1)
        sq.add(("low", 1, q), _tile(v, 1))

    def put_high(k, q, v):
        dhigh[k] = v
        sq.add(("high", 0, q), v[:, :128])
        sq.add(("high", 1, q), v[:, 128:])

    _chan_forward(lambda j: y[j], 96, w, 0, 256, put_low, put_high)
    sums[...] = sq.total(rows, {("low", 1): None, ("high", 0): None, ("high", 1): None})


def _rim_kernel(
    sc, xs, from_left, from_right, low0, t0r_all, t1_all, w, rows, lanes,
    dlow_r, dhigh_r, low1, high1, message, sums, t0r, t1, rim, y, y1, sems,
):
    variant = sc[1]
    c0 = pltpu.make_async_copy(t0r_all.at[variant], t0r, sems.at[0])
    c1 = pltpu.make_async_copy(t1_all.at[variant], t1, sems.at[1])
    c0.start()
    c1.start()
    lane = _lane()
    for j in range(SEG):
        g, i = j // 48, j % 48
        a = from_left[i]
        b = from_right[i]
        a = pltpu.roll(a, (32 - 32 * g) % 128, 1) if g != 1 else a
        b = pltpu.roll(b, (64 - 32 * g) % 128, 1) if g != 2 else b
        halo = jnp.where(lane < 64, a, b)
        own = jnp.where(lane < 32, xs[j, :, 0:128], xs[j, :, 128:256])
        rim[j] = jnp.where((lane < 32) | (lane >= 96), own, halo)
    c0.wait()

    def store(j, step, v):
        y[pl.ds(j, step)] = v

    _time(lambda j, step: rim[pl.ds(j, step)], SEG, t0r, store, 24)
    sq = _Squares()

    def put_low(k, q, v):
        dlow_r[k] = v
        sq.add(("low", 0, q), v)

    def put_high(k, q, v):
        dhigh_r[k] = v
        sq.add(("high", 0, q), v)

    _chan_forward(lambda j: y[j], 96, w, 0, 128, put_low, put_high)
    sums[0] = sq.total(rows, {("low", 0): lanes[0:1], ("high", 0): lanes[1:2]})
    c1.wait()

    def load1(j, step):
        return jnp.concatenate([low0[pl.ds(j, step)], dlow_r[pl.ds(j, step)]], axis=2)

    def store1(j, step, v):
        y1[pl.ds(j, step)] = v

    _time(load1, 96, t1, store1, 24)
    sq1 = _Squares()

    def put_low1(k, q, v):
        low1[k] = v
        sq1.add(("low", 0, q), _tile(v, 0))

    def put_high1(k, q, v):
        high1[k] = v
        sq1.add(("high", 0, q), _tile(v, 0))

    _chan_forward(lambda j: y1[j], 48, w, 1, 256, put_low1, put_high1)
    sums[1] = sq1.total(rows, {("low", 0): lanes[2:3], ("high", 0): lanes[3:4]})
    for i in range(24):
        message[i] = jnp.where(lane < 64, low1[i, :, 0:128], pltpu.roll(low1[i + 24, :, 0:128], 64, 1))


def _middle_kernel(
    sc, own, m2, m1, p1, p2, s0, s01, t2_all, t3_all, t4_all, t5_all, w, rows, lanes, place,
    a2l, a2h, a3l, a3h, a4l, a4h, a5l, a5h, payload,
    t2, t3, t4, t5, x2, y2, y3, y4, y5, l5, sems,
):
    variant = sc[2]
    copies = []
    for i, (src, dst) in enumerate(((t2_all, t2), (t3_all, t3), (t4_all, t4), (t5_all, t5))):
        c = pltpu.make_async_copy(src.at[variant], dst, sems.at[i])
        c.start()
        copies.append(c)
    lane = _lane()
    for j in range(48):
        h, i = j // 24, j % 24

        def low_half(ref):
            return ref[i] if h == 0 else pltpu.roll(ref[i], 64, 1)

        def high_half(ref):
            return ref[i] if h == 1 else pltpu.roll(ref[i], 64, 1)

        x2[j, :, 0:128] = jnp.where(lane < 64, low_half(own), high_half(p1))
        x2[j, :, 128:256] = jnp.where(lane < 64, low_half(m1), high_half(p2))
        x2[j, :, 256:384] = low_half(m2)

    totals = [s0[...] + s01[0], s01[1]]

    def level(l, load, count, t, y, step, lanes_n, low, high, tiles):
        def store(j, n, v):
            y[pl.ds(j, n)] = v

        _time(load, count, t, store, step)
        sq = _Squares()

        def put_low(k, q, v):
            low[k] = v
            for i in range(tiles):
                sq.add(("low", i, q), _tile(v, i))

        def put_high(k, q, v):
            if high.shape[2] == v.shape[1]:
                high[k] = v
            else:
                high[k] = _tile(v, 0)
            for i in range(tiles):
                sq.add(("high", i, q), _tile(v, i))

        _chan_forward(lambda j: y[j], count // 2, w, l, lanes_n, put_low, put_high)
        masks = {("low", 0): lanes[2 * l : 2 * l + 1], ("high", 0): lanes[2 * l + 1 : 2 * l + 2]}
        if tiles == 2:
            masks[("low", 1)] = lanes[12:13]
            masks[("high", 1)] = lanes[13:14]
        totals.append(sq.total(rows, masks))

    copies[0].wait()
    level(2, lambda j, n: x2[pl.ds(j, n)], 48, t2, y2, 24, 256, a2l, a2h, 2)
    copies[1].wait()
    level(3, lambda j, n: a2l[pl.ds(j, n)], 24, t3, y3, 24, 128, a3l, a3h, 1)
    copies[2].wait()
    level(4, lambda j, n: a3l[pl.ds(j, n)], 12, t4, y4, 12, 128, a4l, a4h, 1)
    copies[3].wait()
    level(5, lambda j, n: a4l[pl.ds(j, n)], 6, t5, y5, 6, 256, l5, a5h, 1)
    sub = _sublane(128)
    line = jnp.zeros((8, 128), F32)
    for j in range(3):
        a5l[j] = l5[j, :, 0:128]
        line = line + place[j] * l5[j, :, 128:256]
    sums = jnp.zeros((8, 128), F32)
    for l in range(LEVELS):
        sums = jnp.where(sub == l, jnp.sum(totals[l], axis=0, keepdims=True), sums)
    sums = jnp.sum(sums, axis=1, keepdims=True)
    line = line + jnp.where(lane == 96 + sub, sums, 0.0) * jnp.where(sub < LEVELS, 1.0, 0.0)
    line = jnp.sum(line, axis=0, keepdims=True)
    payload[...] = jnp.broadcast_to(line, payload.shape)


def _shrink(v, limit):
    return v - jnp.minimum(jnp.maximum(v, -limit), limit)


def _back_kernel(
    sc, g, w_all, v_all, s0_all, s1_all, s2_all, s3_all, s4_all, s5_all, w, cmask,
    dlow0, dhigh0, rlow0, rhigh0, a1l, a1h, a2l, a2h, a3l, a3h, a4l, a4h, a5l, a5h,
    out,
    v, s0, s1, s2, s3, s4, s5, gt, y5, y4, y3, y2, y1, y0, c4, c3, c2, c1, c0, fa, fb, sems,
):
    variant = sc[1]
    core = sc[0]
    v[...] = jnp.zeros(v.shape, BF16)
    copies = [pltpu.make_async_copy(v_all.at[sc[3]], v.at[:, pl.ds(0, 16), :], sems.at[0])]
    for i, (src, dst) in enumerate(
        ((s5_all, s5), (s4_all, s4), (s3_all, s3), (s2_all, s2), (s1_all, s1), (s0_all, s0))
    ):
        copies.append(pltpu.make_async_copy(src.at[variant], dst, sems.at[i + 1]))
    for c in copies:
        c.start()
    lane1 = _lane(1)
    total = jnp.sum(g[...], axis=0, keepdims=True)
    limits = []
    for l in range(LEVELS):
        entries = 3 * (C >> (l + 1)) * (S >> (l + 1))
        s = jnp.sum(jnp.where(lane1 == 96 + l, total, 0.0), axis=1, keepdims=True)
        limits.append(jnp.sqrt(s * (1.0 / entries) + FLOOR))
    gt[0] = jnp.transpose(g[0:128])
    gt[1] = jnp.transpose(g[128:256])
    rows = [
        jnp.concatenate([gt[c, pl.ds(m, 24, stride=4), :] for m in range(4)], axis=1) for c in range(2)
    ]
    coarse = _dot3(jnp.concatenate(rows, axis=0), w_all)
    position = lax.broadcasted_iota(jnp.int32, (48, 512), 1)
    highs = position >= (S >> (LEVELS + COARSE))
    square = jnp.where(highs, coarse * coarse, 0.0)
    square = square[:, 0:128] + square[:, 128:256] + square[:, 256:384] + square[:, 384:512]
    square = jnp.sum(square * cmask[...], axis=0, keepdims=True)
    square = jnp.sum(square, axis=1, keepdims=True)
    entries = (C >> LEVELS) * ((S >> LEVELS) - (S >> (LEVELS + COARSE)))
    limit = jnp.sqrt(square * (1.0 / entries) + FLOOR)
    coarse = jnp.where(highs, _shrink(coarse, limit), coarse)
    mine = jnp.where(core == 0, coarse[0:24], coarse[24:48])
    mine = jnp.concatenate([mine, jnp.zeros((8, 512), F32)], axis=0)
    hi = mine.astype(BF16)
    lo = (mine - hi.astype(F32)).astype(BF16)
    copies[0].wait()

    def nt(a, b):
        return lax.dot_general(a, b, (((1,), (1,)), ((), ())), preferred_element_type=F32)

    current = nt(hi, v[0]) + nt(lo, v[0]) + nt(hi, v[1])

    lane = _lane()

    def level(l, get_current, low, high, n, y, s, nxt, step, lanes, needed):
        width = y.shape[2]
        tl = jnp.broadcast_to(limits[l] * (1.0 / KS), (8, width))
        th = jnp.broadcast_to(limits[l] * KS, (8, width))
        is_low = lax.broadcasted_iota(jnp.int32, (8, width), 1)
        is_low = needed(is_low)

        def get_low(k):
            return jnp.where(is_low, get_current(k), _shrink(low[k], tl))

        def put(j, value):
            y[j] = value

        _chan_inverse(get_low, lambda k: _shrink(high[k], th), n, w, l, width, put)

        def store(j, m, value):
            nxt[pl.ds(j, m)] = value

        _time(lambda j, m: y[pl.ds(j, m)], 2 * n, s, store, step)

    copies[1].wait()
    level(5, lambda k: current[8 * k : 8 * k + 8], a5l, a5h, 3, y5, s5, c4, 6, 128, lambda i: i < 10)
    copies[2].wait()
    level(4, lambda k: c4[k], a4l, a4h, 6, y4, s4, c3, 12, 128, lambda i: i < 29)
    copies[3].wait()
    level(3, lambda k: c3[k], a3l, a3h, 12, y3, s3, c2, 24, 128, lambda i: i < 65)
    copies[4].wait()
    pad = jnp.zeros((8, 128), F32)
    level(
        2, lambda k: jnp.concatenate([c2[k], pad], axis=1), a2l, a2h, 24, y2, s2, c1, 24, 256, lambda i: i < 128
    )
    copies[5].wait()
    level(
        1, lambda k: c1[k], a1l, a1h, 48, y1, s1, c0, 24, 256, lambda i: (i < 64) | (i >= 134),
    )
    copies[6].wait()
    tl = jnp.broadcast_to(limits[0] * (1.0 / KS), (8, 128))
    th = jnp.broadcast_to(limits[0] * KS, (8, 128))
    th2 = jnp.broadcast_to(limits[0] * KS, (8, 256))
    rim_low = lane < 32

    def get_low0(k):
        now = c0[k]
        rim = jnp.where(rim_low, _tile(now, 1), _shrink(rlow0[k], tl))
        return jnp.concatenate([_tile(now, 0), _shrink(dlow0[k], tl), rim], axis=1)

    def get_high0(k):
        return jnp.concatenate([_shrink(dhigh0[k], th2), _shrink(rhigh0[k], th)], axis=1)

    def put0(j, value):
        y0[j] = value

    _chan_inverse(get_low0, get_high0, 96, w, 0, 384, put0)

    def store0(j, m, value):
        for i in range(m):
            fa[pl.ds(j + i, 8, stride=SEG), :] = value[i, :, 0:128]
            fb[pl.ds(j + i, 8, stride=SEG), :] = value[i, :, 128:256]

    _time(lambda j, m: y0[pl.ds(j, m)], SEG, s0, store0, 24)
    at_own = pl.multiple_of(core * HALO, 8)
    last = [
        pltpu.make_async_copy(buf.at[pl.ds(at_own, OWN)], out.at[:, pl.ds(128 * i, 128)], sems.at[7 + i])
        for i, buf in enumerate((fa, fb))
    ]
    for c in last:
        c.start()
    for c in last:
        c.wait()


VM = pl.BlockSpec(memory_space=pltpu.VMEM)
SM = pl.BlockSpec(memory_space=pltpu.SMEM)
ANY = pl.BlockSpec(memory_space=pl.ANY)


def _call(kernel, name, args, specs, outs, out_specs, scratch):
    return pl.pallas_call(
        kernel,
        out_shape=[jax.ShapeDtypeStruct(s, F32) for s in outs],
        in_specs=specs,
        out_specs=out_specs,
        scratch_shapes=scratch,
        compiler_params=pltpu.CompilerParams(vmem_limit_bytes=40 * 1024 * 1024),
        name=name,
    )(*args)


def _shift(v, by):
    return lax.ppermute(v, "tm", [(i, i + by) for i in range(NT) if 0 <= i + by < NT])


def shards(record, gauge_table, gauge_index):
    tables = _tables()
    core = lax.axis_index("chan")
    place = lax.axis_index("tm")
    v3 = jnp.where(place == 0, 0, jnp.where(place == NT - 1, 2, 1))
    v5 = jnp.minimum(place, 2) + jnp.maximum(place - (NT - 3), 0)
    sc = jnp.stack([core, v3, v5, place]).astype(jnp.int32)

    matches = (gauge_index[:, :, None] == jnp.arange(GTAB, dtype=jnp.int32)[None, None, :]).astype(F32)
    block_weights = jnp.sum(matches * gauge_table[:, None, :], axis=2)
    kept = jnp.where(core == 0, block_weights[:, 0:24], block_weights[:, 8:32])
    weights = jnp.broadcast_to(kept.reshape(LEVELS, 8, 3).transpose(0, 2, 1)[..., None], (LEVELS, 3, 8, 128))

    block = 3 * np.arange(8)[None, :] + np.arange(3)[:, None]
    row_masks = np.stack([block < 16, block >= 8]).astype(np.float32)
    row_mask = jnp.where(core == 0, row_masks[0], row_masks[1])
    row_mask = jnp.broadcast_to(row_mask[..., None], (3, 8, 128))
    lane_masks = jnp.asarray(_lane_masks())
    spots = np.zeros((3, 8, 128), np.float32)
    cmask = np.zeros((48, 128), np.float32)
    for j in range(3):
        for s in range(8):
            spots[j, s, 4 * (8 * j + s) : 4 * (8 * j + s) + 4] = 1.0
            cmask[8 * j + s] = 1.0 if 3 * s + j < 16 else 0.0
            cmask[24 + 8 * j + s] = 1.0 if 3 * s + j >= 8 else 0.0

    sent = jnp.where(core == 0, record[OWN - HALO :], record[:HALO])
    recv = lax.ppermute(sent, "chan", [(0, 1), (1, 0)])
    dma = pltpu.SemaphoreType.DMA
    xs, right, left = _call(
        _pack_kernel, "pack", (sc, record, recv), [SM, ANY, ANY],
        [(SEG, 8, 256), (48, 8, 128), (48, 8, 128)], [VM] * 3,
        [pltpu.VMEM((8 * SEG, 128), F32)] * 2 + [dma((4,))],
    )
    from_left, from_right = _shift(right, 1), _shift(left, -1)
    low0, dlow0, dhigh0, sum0 = _call(
        _own_kernel, "own", (xs, tables["t0"], weights, row_mask), [VM] * 4,
        [(96, 8, 128), (96, 8, 128), (96, 8, 256), (8, 128)], [VM] * 4,
        [pltpu.VMEM((SEG, 8, 256), F32)],
    )
    rlow0, rhigh0, a1l, a1h, message, sum01 = _call(
        _rim_kernel, "rim",
        (sc, xs, from_left, from_right, low0, tables["t0r"], tables["t1"], weights, row_mask, lane_masks),
        [SM, VM, VM, VM, VM, ANY, ANY, VM, VM, VM],
        [(96, 8, 128), (96, 8, 128), (48, 8, 256), (48, 8, 256), (24, 8, 128), (2, 8, 128)], [VM] * 6,
        [
            pltpu.VMEM((2, 128, 128), BF16), pltpu.VMEM((2, 256, 256), BF16),
            pltpu.VMEM((SEG, 8, 128), F32), pltpu.VMEM((SEG, 8, 128), F32), pltpu.VMEM((96, 8, 256), F32),
            dma((2,)),
        ],
    )
    near = [_shift(message, by) for by in (2, 1, -1, -2)]
    a2l, a2h, a3l, a3h, a4l, a4h, a5l, a5h, payload = _call(
        _middle_kernel, "middle",
        (sc, message, *near, sum0, sum01, tables["t2"], tables["t3"], tables["t4"], tables["t5"],
         weights, row_mask, lane_masks, jnp.asarray(spots)),
        [SM] + [VM] * 7 + [ANY] * 4 + [VM] * 4,
        [(24, 8, 256)] * 2 + [(12, 8, 128)] * 2 + [(6, 8, 128)] * 2 + [(3, 8, 128)] * 2 + [(256, 128)], [VM] * 9,
        [
            pltpu.VMEM((2, 384, 256), BF16), pltpu.VMEM((2, 256, 128), BF16),
            pltpu.VMEM((2, 128, 128), BF16), pltpu.VMEM((2, 128, 256), BF16),
            pltpu.VMEM((48, 8, 384), F32), pltpu.VMEM((48, 8, 256), F32), pltpu.VMEM((24, 8, 128), F32),
            pltpu.VMEM((12, 8, 128), F32), pltpu.VMEM((6, 8, 256), F32), pltpu.VMEM((3, 8, 256), F32),
            dma((4,)),
        ],
    )
    everyone = lax.all_to_all(payload, ("chan", "tm"), split_axis=0, concat_axis=0, tiled=True)
    (out,) = _call(
        _back_kernel, "back",
        (sc, everyone, tables["w"], tables["v"], *(tables["s%d" % l] for l in range(6)), weights, jnp.asarray(cmask),
         dlow0, dhigh0, rlow0, rhigh0, a1l, a1h, a2l, a2h, a3l, a3h, a4l, a4h, a5l, a5h),
        [SM, VM, VM] + [ANY] * 7 + [VM] * 16,
        [(OWN, 256)], [ANY],
        [
            pltpu.VMEM((2, 128, 512), BF16),
            pltpu.VMEM((2, 384, 256), BF16), pltpu.VMEM((2, 256, 256), BF16), pltpu.VMEM((2, 256, 256), BF16),
            pltpu.VMEM((2, 128, 128), BF16), pltpu.VMEM((2, 128, 128), BF16), pltpu.VMEM((2, 128, 128), BF16),
            pltpu.VMEM((2, 128, 128), F32),
            pltpu.VMEM((6, 8, 128), F32), pltpu.VMEM((12, 8, 128), F32), pltpu.VMEM((24, 8, 128), F32),
            pltpu.VMEM((48, 8, 256), F32), pltpu.VMEM((96, 8, 256), F32), pltpu.VMEM((SEG, 8, 384), F32),
            pltpu.VMEM((6, 8, 128), F32), pltpu.VMEM((12, 8, 128), F32), pltpu.VMEM((24, 8, 128), F32),
            pltpu.VMEM((48, 8, 256), F32), pltpu.VMEM((96, 8, 256), F32),
            pltpu.VMEM((8 * SEG, 128), F32), pltpu.VMEM((8 * SEG, 128), F32),
            dma((9,)),
        ],
    )
    return out


def solution(mesh):
    return jax.shard_map(
        shards,
        mesh=mesh,
        in_specs=(P("chan", "tm"), P(), P()),
        out_specs=P("chan", "tm"),
        check_vma=False,
    )
```

```python
import functools

import jax
import jax.numpy as jnp
import ml_dtypes
import numpy as np
from jax import lax
from jax.experimental import pallas as pl
from jax.experimental.pallas import tpu as pltpu
from jax.sharding import PartitionSpec as P

LEVELS = 6
COARSE = 6
GTAB = 8
NBLK = 32
C = 2048
S = 32768
NT = 128
OWN = 1024
HALO = 512
SEG = 192
A1 = -1.586134342059924
B1 = -0.052980118572961
A2 = 0.882911075530934
B2 = 0.443506852043971
KS = 1.149604398860241
FLOOR = 1e-06
F32 = jnp.float32
BF16 = jnp.bfloat16


def _next(e):
    return np.concatenate((e[1:], e[-1:]))


def _prev(o):
    return np.concatenate((o[:1], o[:-1]))


def _lift(x):
    e, o = x[0::2], x[1::2]
    o = o + A1 * (e + _next(e))
    e = e + B1 * (_prev(o) + o)
    o = o + A2 * (e + _next(e))
    e = e + B2 * (_prev(o) + o)
    return KS * e, o / KS


def _unlift(low, high):
    e, o = low / KS, high * KS
    e = e - B2 * (_prev(o) + o)
    o = o - A2 * (e + _next(e))
    e = e - B1 * (_prev(o) + o)
    o = o - A1 * (e + _next(e))
    return np.stack((e, o), axis=1).reshape((2 * e.shape[0],) + e.shape[1:])


def _forward(inputs, lows, highs, rows, cols, start, stop, scale):
    pairs = list(lows) + list(highs)
    a = max(2 * min(pairs) - 16, start)
    b = min(2 * max(pairs) + 16, stop)
    low, high = _lift(np.eye(b - a))
    out = np.zeros((rows, cols))
    for band, places in ((low, lows), (high, highs)):
        for pair, col in places.items():
            if a <= 2 * pair < b:
                line = band[pair - a // 2]
                for i in np.nonzero(line)[0]:
                    out[inputs[a + int(i)], col] += scale * line[i]
    return out


def _inverse(lows, highs, outputs, rows, cols, start, stop, scale):
    a = max(2 * (min(outputs) // 2) - 16, start) // 2
    b = min(2 * (max(outputs) // 2) + 18, stop) // 2
    n = b - a
    eye, zero = np.eye(n), np.zeros((n, n))
    from_low, from_high = _unlift(eye, zero), _unlift(zero, eye)
    out = np.zeros((rows, cols))
    for sample, col in outputs.items():
        if 2 * a <= sample < 2 * b:
            for lines, places in ((from_low, lows), (from_high, highs)):
                line = lines[sample - 2 * a]
                for i in np.nonzero(line)[0]:
                    out[places[a + int(i)], col] += scale * line[i]
    return out


def _pair(m):
    hi = m.astype(ml_dtypes.bfloat16)
    lo = (m - hi.astype(np.float64)).astype(ml_dtypes.bfloat16)
    return np.stack((hi, lo))


def _run(first, last, at):
    return {k: at + k - first for k in range(first, last)}


OWN_LOW0 = _run(2, 126, 2)
OWN_HIGH0 = _run(2, 126, 130)
RIM_LOW0 = {**_run(-10, 2, 0), **_run(126, 137, 12)}
RIM_HIGH0 = {**_run(-2, 2, 32), **_run(126, 130, 36)}
RIM_IN0 = {**_run(0, 32, 0), **_run(-32, 0, 32), **_run(256, 288, 64), **_run(224, 256, 96)}
OWN_LOW1 = _run(3, 61, 3)
OWN_HIGH1 = _run(2, 61, 66)
RIM_LOW1 = {**_run(-3, 3, 64), **_run(61, 67, 70)}
RIM_HIGH1 = {**_run(-3, 2, 80), **_run(61, 67, 85)}
IN1 = {**OWN_LOW0, **{k: 128 + v for k, v in RIM_LOW0.items()}}
IN2 = {
    **OWN_LOW1, **_run(67, 125, 67), **_run(-61, -3, 131), **{k: 128 + v for k, v in RIM_LOW1.items()}
}
LOW2 = _run(-28, 57, 0)
HIGH2 = _run(-3, 36, 85)
LOW3 = _run(-12, 27, 0)
HIGH3 = _run(-3, 20, 64)
LOW4 = _run(-4, 12, 0)
HIGH4 = _run(-3, 12, 32)
LOW5 = {4 * (d - 1) + i: 4 * i + d for i in range(4) for d in range(3)}
HIGH5 = {k: 32 + v for k, v in LOW5.items()}


def _part(places, first, last):
    return {k: places[k] for k in range(first, last)}


def _edges(width):
    far = 1 << 20
    return ((0, far), (-far, far), (-far, width))


def _bundle(parts, rows):
    out = np.zeros((rows, 256))
    for r, c, m in parts:
        out[r : r + m.shape[0], c : c + m.shape[1]] = m
    return _pair(out)


@functools.cache
def _tables():
    fw, inv = _forward, _inverse
    far = 1 << 20
    out = {}
    out["own"] = _bundle(
        (
            (0, 0, fw(_run(0, 256, 0), OWN_LOW0, OWN_HIGH0, 256, 256, -far, far, 1.0)),
            (256, 0, fw(OWN_LOW0, OWN_LOW1, OWN_HIGH1, 128, 128, -far, far, KS)),
        ),
        384,
    )
    rim, back = [], []
    for v in range(3):
        a, b = zip(*(_edges(256 >> l)[v] for l in range(LEVELS)))
        t5 = fw(LOW4, _part(LOW5, 0, 4), _part(HIGH5, 0, 4), 128, 256, a[5], b[5], KS)
        for i in range(128):
            t5[:, 128 + i] = t5[:, LOW5[i % 4]]
        rim.append(
            _bundle(
                (
                    (0, 0, fw(IN1, RIM_LOW1, RIM_HIGH1, 256, 128, a[1], b[1], KS)),
                    (0, 128, fw(IN2, LOW2, HIGH2, 256, 128, a[2], b[2], KS)),
                    (256, 0, fw(RIM_IN0, RIM_LOW0, RIM_HIGH0, 128, 128, a[0], b[0], 1.0)),
                    (256, 128, fw(LOW2, LOW3, HIGH3, 128, 128, a[3], b[3], KS)),
                    (384, 0, t5),
                    (512, 0, fw(LOW3, LOW4, HIGH4, 128, 128, a[4], b[4], KS)),
                ),
                640,
            )
        )
        low0 = {**OWN_LOW0, **{k: 256 + v for k, v in RIM_LOW0.items() if -2 <= k < 130}}
        high0 = {**OWN_HIGH0, **{k: 256 + v for k, v in RIM_HIGH0.items()}}
        low1 = {**OWN_LOW1, **{k: 128 + v for k, v in RIM_LOW1.items()}}
        high1 = {**OWN_HIGH1, **{k: 128 + v for k, v in RIM_HIGH1.items()}}
        back.append(
            _bundle(
                (
                    (0, 0, inv(low0, high0, _run(0, 256, 0), 384, 256, a[0], b[0], 1.0)),
                    (384, 0, inv(low1, high1, _part(IN1, -1, 130), 256, 256, a[1], b[1], 1.0 / KS)),
                    (640, 0, inv(LOW2, HIGH2, _part(low1, -2, 67), 128, 256, a[2], b[2], 1.0 / KS)),
                    (768, 0, inv(LOW3, HIGH3, _part(LOW2, -2, 36), 128, 128, a[3], b[3], 1.0 / KS)),
                    (768, 128, inv(LOW4, HIGH4, _part(LOW3, -2, 20), 128, 128, a[4], b[4], 1.0 / KS)),
                    (896, 0, inv(LOW5, HIGH5, _part(LOW4, -2, 12), 128, 128, a[5], b[5], 1.0 / KS)),
                ),
                1024,
            )
        )
    out["rim"], out["back"] = np.stack(rim), np.stack(back)
    n = S >> LEVELS
    bands = []
    current = np.eye(n)
    for _ in range(COARSE):
        current, high = _lift(current)
        bands.append(high)
    coarse = np.concatenate([current] + bands[::-1])
    order = (np.arange(n) % NT) * 4 + np.arange(n) // NT
    out["w"] = _pair((KS * coarse.T)[order])
    last = n >> COARSE
    current = np.eye(n)[:last]
    for step in range(COARSE):
        size = last << step
        current = _unlift(current, np.eye(n)[size : 2 * size])
    rebuilt = np.zeros((n + 8, n))
    rebuilt[4 : n + 4] = current / KS
    rebuilt = _pair(rebuilt)
    pieces = np.zeros((NT, 2, 16, n), ml_dtypes.bfloat16)
    for k, lane in LOW5.items():
        pieces[:, :, lane] = np.moveaxis(rebuilt[:, 4 + k : 4 + k + n : 4], 0, 1)
    out["v"] = pieces
    return out


def _mask(lane, places, first, last, base=0):
    lanes = sorted(v - base for k, v in places.items() if first <= k < last)
    out, i = None, 0
    while i < len(lanes):
        j = i
        while j + 1 < len(lanes) and lanes[j + 1] == lanes[j] + 1:
            j += 1
        hit = (lane >= lanes[i]) & (lane <= lanes[j])
        out = hit if out is None else out | hit
        i = j + 1
    return out


def _ones(hit):
    return jnp.where(hit, 1.0, 0.0)


def _dot3(x, t):
    hi = x.astype(BF16)
    lo = (x - hi.astype(F32)).astype(BF16)
    d = functools.partial(jnp.dot, preferred_element_type=F32)
    return d(hi, t(0)) + d(lo, t(0)) + d(hi, t(1))


def _time(load, t, y, step, j):
    x = load(j, step)
    y[pl.ds(j, step)] = _dot3(x.reshape(step * 8, x.shape[2]), t).reshape(step, 8, y.shape[2])


class _Forward:
    def __init__(self, load, t, y, step):
        self.load, self.t, self.y, self.step, self.done = load, t, y, step, 0

    def __call__(self, j):
        ahead = min(j + self.step, self.y.shape[0] - 1)
        while self.done <= ahead:
            _time(self.load, self.t, self.y, self.step, self.done)
            self.done += self.step
        return self.y[j]


class _Backward:
    def __init__(self, y, t, store, step):
        self.y, self.t, self.store, self.step, self.left = y, t, store, step, {}

    def __call__(self, j, value):
        self.y[j] = value
        chunk = j // self.step
        self.left[chunk] = self.left.get(chunk, self.step) - 1
        if not self.left[chunk]:
            x = self.y[pl.ds(chunk * self.step, self.step)]
            out = _dot3(x.reshape(self.step * 8, x.shape[2]), self.t)
            self.store(chunk * self.step, self.step, out.reshape(self.step, 8, out.shape[1]))


def _table(ref, rows, cols, *lead):
    r, c = pl.ds(*rows), pl.ds(*cols)
    return lambda i: ref[(*lead, i, r, c)]


def _sublane(lanes):
    return lax.broadcasted_iota(jnp.int32, (8, lanes), 0)


def _lane(rows=8):
    return lax.broadcasted_iota(jnp.int32, (rows, 128), 1)


def _wide(v, lanes):
    return v if lanes == 128 else jnp.concatenate([v] * (lanes // 128), axis=1)


class _Wrap:
    def __init__(self, lanes):
        sub = _sublane(lanes)
        self.last, self.first = sub == 7, sub == 0

    def after(self, first, last):
        return jnp.where(self.last, last, pltpu.roll(first, 7, 0))

    def before(self, last, first):
        return jnp.where(self.first, first, pltpu.roll(last, 1, 0))


def _coefs(w_ref, level, lanes):
    return [[_wide(c * w_ref[level, q], lanes) for q in range(3)] for c in (A1, B1, A2, B2)]


def _chan_forward(get, n, w_ref, level, lanes, put_low, put_high):
    wrap = _Wrap(lanes)
    ca, cb, cc, cd = _coefs(w_ref, level, lanes)
    per = n // 3
    first = get(0)
    e, o1, e1, o2 = {0: first}, {}, {}, {}

    def high(k, v):
        o2[k] = v
        put_high(k, k // per, v)

    def low(k):
        put_low(k, k // per, e1[k] + cd[k // per] * (o2[k - 1] + o2[k]))

    for k in range(n):
        q = k // per
        e[k + 1] = get(2 * k + 2) if k + 1 < n else wrap.after(first, e[k])
        o1[k] = get(2 * k + 1) + ca[q] * (e[k] + e[k + 1])
        if k >= 1:
            e1[k] = e[k] + cb[q] * (o1[k - 1] + o1[k])
        if k >= 2:
            high(k - 1, o1[k - 1] + cc[(k - 1) // per] * (e1[k - 1] + e1[k]))
        if k >= 3:
            low(k - 1)
    e1[0] = first + cb[0] * (wrap.before(o1[n - 1], o1[0]) + o1[0])
    high(0, o1[0] + cc[0] * (e1[0] + e1[1]))
    high(n - 1, o1[n - 1] + cc[2] * (e1[n - 1] + wrap.after(e1[0], e1[n - 1])))
    o2[-1] = wrap.before(o2[n - 1], o2[0])
    for k in (0, 1, n - 1):
        low(k)


def _chan_inverse(get_low, get_high, n, w_ref, level, lanes, put):
    wrap = _Wrap(lanes)
    ca, cb, cc, cd = _coefs(w_ref, level, lanes)
    per = n // 3
    o = {0: get_high(0)}
    o[-1] = wrap.before(get_high(n - 1), o[0])
    e1, o1, e2 = {}, {}, {}

    def even(k):
        e2[k] = e1[k] - cb[k // per] * (o1[k - 1] + o1[k])
        put(2 * k, e2[k])

    def odd(k):
        put(2 * k + 1, o1[k] - ca[k // per] * (e2[k] + e2[k + 1]))

    for k in range(n):
        q = k // per
        if k:
            o[k] = get_high(k)
        e1[k] = get_low(k) - cd[q] * (o[k - 1] + o[k])
        if k >= 1:
            o1[k - 1] = o[k - 1] - cc[(k - 1) // per] * (e1[k - 1] + e1[k])
        if k >= 2:
            even(k - 1)
        if k >= 3:
            odd(k - 2)
    o1[n - 1] = o[n - 1] - cc[2] * (e1[n - 1] + wrap.after(e1[0], e1[n - 1]))
    o1[-1] = wrap.before(o1[n - 1], o1[0])
    even(n - 1)
    if n > 2:
        odd(n - 2)
    even(0)
    odd(0)
    e2[n] = wrap.after(e2[0], e2[n - 1])
    odd(n - 1)


class _Squares:
    def __init__(self):
        self.acc = {}

    def add(self, key, v):
        self.acc[key] = v * v if key not in self.acc else self.acc[key] + v * v

    def total(self, rows, tiles):
        out = None
        for q in range(3):
            part = None
            for (band, tile), lanes in tiles.items():
                v = self.acc[(band, tile, q)] * (KS * KS if band == "low" else 1.0 / (KS * KS))
                v = v if lanes is None else v * lanes
                part = v if part is None else part + v
            part = part * rows[q]
            out = part if out is None else out + part
        return out


def _tile(v, i):
    return v[:, 128 * i : 128 * (i + 1)]


def _own_rows(core):
    block = 3 * _sublane(128)
    return [
        jnp.where(core == 0, _ones(block + q < 16), _ones(block + q >= 8)) for q in range(3)
    ]


def _half_kernel(sc, x, out, sems):
    at = pl.multiple_of((1 - sc[0]) * HALO, 8)
    copies = [
        pltpu.make_async_copy(x.at[pl.ds(at + 128 * i, 128)], out.at[pl.ds(128 * i, 128)], sems.at[i])
        for i in range(4)
    ]
    for c in copies:
        c.start()
    for c in copies:
        c.wait()


def _own_kernel(
    sc, x, recv, gauge_table_all, gauge_index_all, table_all, rim_all,
    right, left, rim_in, low0, a1l, sums, w, rim_table, kept,
    gauge_table, gauge_index, table, details, xa, xb, xs, y0, y1, sems,
):
    core = sc[0]
    gauges = [
        pltpu.make_async_copy(gauge_index_all, gauge_index, sems.at[4]),
        pltpu.make_async_copy(gauge_table_all, gauge_table, sems.at[5]),
    ]
    for c in gauges:
        c.start()
    at_own = pl.multiple_of(core * HALO, 8)
    at_recv = pl.multiple_of((1 - core) * OWN, 8)
    copies = []
    for i, buf in enumerate((xa, xb)):
        lanes = pl.ds(128 * i, 128)
        copies.append(pltpu.make_async_copy(x.at[:, lanes], buf.at[pl.ds(at_own, OWN)], sems.at[2 * i]))
        copies.append(pltpu.make_async_copy(recv.at[:, lanes], buf.at[pl.ds(at_recv, HALO)], sems.at[2 * i + 1]))
    for c in copies:
        c.start()
    own_table = pltpu.make_async_copy(table_all, table, sems.at[6])
    own_table.start()
    next_table = pltpu.make_async_copy(rim_all.at[sc[1]], rim_table, sems.at[7])
    next_table.start()
    for c in gauges:
        c.wait()
    index = gauge_index[...]
    table_rows = gauge_table[...]
    weights = jnp.zeros(index.shape, F32)
    for g in range(GTAB):
        weights = weights + jnp.where(index == g, table_rows[:, g : g + 1], 0.0)
    block = lax.broadcasted_iota(jnp.int32, (8, NBLK), 1) - 3 * lax.broadcasted_iota(jnp.int32, (8, NBLK), 0)
    block = block - 8 * core
    for l in range(LEVELS):
        for q in range(3):
            hit = jnp.where(block == q, weights[l : l + 1], 0.0)
            w[l, q] = jnp.broadcast_to(jnp.sum(hit, axis=1, keepdims=True), (8, 128))
    for c in copies:
        c.wait()
    lane = _lane()
    group = lane // 32
    for i in range(48):
        to_right, to_left = None, None
        for g in range(4):
            j = 48 * g + i
            a = xa[pl.ds(j, 8, stride=SEG), :]
            b = xb[pl.ds(j, 8, stride=SEG), :]
            xs[j, :, 0:128] = a
            xs[j, :, 128:256] = b
            rim_in[j] = jnp.where(lane < 32, a, b)
            a = pltpu.roll(a, 32 * g, 1) if g else a
            b = pltpu.roll(b, (32 * g + 32) % 128, 1) if g != 3 else b
            to_left = a if to_left is None else jnp.where(group == g, a, to_left)
            to_right = b if to_right is None else jnp.where(group == g, b, to_right)
        right[i] = to_right
        left[i] = to_left
    own_table.wait()
    rows = _own_rows(core)
    sq = _Squares()

    def put_low(k, q, v):
        low0[k] = _tile(v, 0)
        details[k] = _tile(v, 1)
        sq.add(("low", 1, q), _tile(v, 1))

    def put_high(k, q, v):
        details[96 + k] = _tile(v, 0)
        details[192 + k] = _tile(v, 1)
        sq.add(("high", 0, q), _tile(v, 0))
        sq.add(("high", 1, q), _tile(v, 1))

    get = _Forward(lambda j, n: xs[pl.ds(j, n)], _table(table, (0, 256), (0, 256)), y0, 24)
    _chan_forward(get, 96, w, 0, 256, put_low, put_high)
    sums[0] = sq.total(rows, {("low", 1): None, ("high", 0): None, ("high", 1): None})
    keep0 = pltpu.make_async_copy(details.at[pl.ds(0, 288)], kept.at[pl.ds(0, 288)], sems.at[8])
    keep0.start()
    sq1 = _Squares()

    def put_low1(k, q, v):
        a1l[k] = v
        details[288 + k] = v
        sq1.add(("low", 0, q), v)
        if k >= 26:
            packed = jnp.where(lane < 64, a1l[k - 24], pltpu.roll(v, 64, 1))
            right[24 + k] = packed
            left[24 + k] = packed

    def put_high1(k, q, v):
        details[336 + k] = v
        sq1.add(("high", 0, q), v)

    get = _Forward(lambda j, n: low0[pl.ds(j, n)], _table(table, (256, 128), (0, 128)), y1, 24)
    _chan_forward(get, 48, w, 1, 128, put_low1, put_high1)
    keep1 = pltpu.make_async_copy(details.at[pl.ds(288, 96)], kept.at[pl.ds(288, 96)], sems.at[9])
    keep1.start()
    for k in (24, 25):
        packed = jnp.where(lane < 64, a1l[k - 24], pltpu.roll(a1l[k], 64, 1))
        right[24 + k] = packed
        left[24 + k] = packed
    sums[1] = sq1.total(rows, {("low", 0): _ones(_mask(lane, OWN_HIGH1, 0, 64)), ("high", 0): None})
    next_table.wait()
    keep0.wait()
    keep1.wait()


def _bands(details):
    out, at = [], 0
    for n in (96, 48, 24, 12, 6, 3):
        out += [details.at[pl.ds(at, n)], details.at[pl.ds(at + n, n)]]
        at += 2 * n
    return out


def _rim_kernel(
    sc, rim_in, from_left, from_right, low0, a1l, own_sums, table, w,
    kept, message_out, payload_out,
    details, message, payload, rim, y0, y1, x2, y2, y3, y4, y5, l5, sems,
):
    core = sc[0]
    rlow0, rhigh0, r1l, r1h, a2l, a2h, a3l, a3h, a4l, a4h, a5l, a5h = _bands(details)
    copies = []

    def keep(first, last):
        rows = pl.ds(first, last - first)
        c = pltpu.make_async_copy(details.at[rows], kept.at[rows], sems.at[len(copies)])
        c.start()
        copies.append(c)

    lane = _lane()
    for j in range(SEG):
        g, i = j // 48, j % 48
        a = from_left[i]
        b = from_right[i]
        a = pltpu.roll(a, (32 - 32 * g) % 128, 1) if g != 1 else a
        b = pltpu.roll(b, (64 - 32 * g) % 128, 1) if g != 2 else b
        halo = jnp.where(lane < 64, a, b)
        rim[j] = jnp.where((lane < 32) | (lane >= 96), rim_in[j], halo)
    rows = _own_rows(core)
    totals = []

    def level(l, load, n, t, y, step, lanes, low, high, own_low, own_high, pairs):
        sq = _Squares()

        def put_low(k, q, value):
            low[k] = value
            sq.add(("low", 0, q), _tile(value, 0))

        def put_high(k, q, value):
            high[k] = _tile(value, 0)
            sq.add(("high", 0, q), _tile(value, 0))

        _chan_forward(_Forward(load, t, y, step), n, w, l, lanes, put_low, put_high)
        is_high = _mask(lane, own_high, 0, pairs)
        is_low = _mask(lane, own_low, 0, pairs)
        total = sq.total(rows, {("low", 0): _ones(is_high), ("high", 0): _ones(is_high | is_low)})
        totals.append(total + own_sums[l] if l < 2 else total)

    def pick(r, k, c, n):
        return _table(table, (r, k), (c, n))

    level(0, lambda j, n: rim[pl.ds(j, n)], 96, pick(256, 128, 0, 128), y0, 24, 128, rlow0, rhigh0, RIM_LOW0, RIM_HIGH0, 128)
    keep(0, 192)

    def load1(j, n):
        return jnp.concatenate([low0[pl.ds(j, n)], rlow0[pl.ds(j, n)]], axis=2)

    level(1, load1, 48, pick(0, 256, 0, 128), y1, 24, 128, r1l, r1h, RIM_LOW1, RIM_HIGH1, 64)
    keep(192, 288)
    for j in range(48):
        h, i = j // 24, 48 + j % 24
        b, a = from_left[i], from_right[i]
        if h == 0:
            a = pltpu.roll(a, 64, 1)
        else:
            b = pltpu.roll(b, 64, 1)
        x2[j, :, 0:128] = jnp.where(lane < 64, a1l[j], a)
        x2[j, :, 128:256] = jnp.where(lane < 64, b, r1l[j])
    level(2, lambda j, n: x2[pl.ds(j, n)], 24, pick(0, 256, 128, 128), y2, 24, 128, a2l, a2h, LOW2, HIGH2, 32)
    level(3, lambda j, n: a2l[pl.ds(j, n)], 12, pick(256, 128, 128, 128), y3, 24, 128, a3l, a3h, LOW3, HIGH3, 16)
    keep(288, 360)
    level(4, lambda j, n: a3l[pl.ds(j, n)], 6, pick(512, 128, 0, 128), y4, 12, 128, a4l, a4h, LOW4, HIGH4, 8)
    level(5, lambda j, n: a4l[pl.ds(j, n)], 3, pick(384, 128, 0, 256), y5, 6, 256, l5, a5h, LOW5, HIGH5, 4)
    sub = _sublane(128)
    line = jnp.zeros((8, 128), F32)
    for j in range(3):
        a = l5[j, :, 0:128]
        a5l[j] = a
        message[j] = jnp.where(lane < 64, a5h[j], pltpu.roll(a, 64, 1))
        line = line + jnp.where(lane // 4 == 8 * j + sub, l5[j, :, 128:256], 0.0)
    keep(360, 378)
    copies.append(pltpu.make_async_copy(message, message_out, sems.at[4]))
    copies[-1].start()
    sums = jnp.zeros((8, 128), F32)
    for l in range(LEVELS):
        sums = jnp.where(sub == l, jnp.sum(totals[l], axis=0, keepdims=True), sums)
    sums = jnp.sum(sums, axis=1, keepdims=True)
    line = line + jnp.where((lane == 96 + sub) & (sub < LEVELS), sums, 0.0)
    line = jnp.sum(line, axis=0, keepdims=True)
    payload[...] = jnp.broadcast_to(line, payload.shape)
    copies.append(pltpu.make_async_copy(payload, payload_out, sems.at[5]))
    copies[-1].start()
    for c in copies:
        c.wait()


def _shrink(v, limit):
    return v - jnp.minimum(jnp.maximum(v, -limit), limit)


def _back_kernel(
    sc, g, near_left_all, near_right_all, coarse_all, v_all, back_all, own_kept, rim_kept, w,
    out,
    near_left, near_right, w_all, table, own_details, rim_details, v, gt, x5l, x5h, y5, y4, y3, y2, y1, y0, c4, c3, c2, c1, c0, fa, fb, sems,
):
    core, variant = sc[0], sc[1]
    rlow0, rhigh0, r1l, r1h, a2l, a2h, a3l, a3h, a4l, a4h, a5l, a5h = _bands(rim_details)
    dlow0, dhigh0, dhigh1 = (own_details.at[pl.ds(96 * i, 96)] for i in range(3))
    a1l, a1h = (own_details.at[pl.ds(288 + 48 * i, 48)] for i in range(2))
    v[...] = jnp.zeros(v.shape, BF16)
    small = pl.ds(288, 90)
    large = pl.ds(0, 288)
    copies = [
        pltpu.make_async_copy(src, dst, sems.at[3 + i])
        for i, (src, dst) in enumerate(
            (
                (coarse_all, w_all),
                (v_all.at[sc[2]], v.at[:, pl.ds(0, 16), :]),
                (near_left_all, near_left),
                (near_right_all, near_right),
                (rim_kept.at[small], rim_details.at[small]),
                (back_all.at[variant], table),
                (own_kept, own_details),
                (rim_kept.at[large], rim_details.at[large]),
            )
        )
    ]
    for c in copies:
        c.start()
    lane = _lane()
    lane1 = _lane(1)
    total = jnp.sum(g[...], axis=0, keepdims=True)
    limits = []
    for l in range(LEVELS):
        entries = 3 * (C >> (l + 1)) * (S >> (l + 1))
        s = jnp.sum(jnp.where(lane1 == 96 + l, total, 0.0), axis=1, keepdims=True)
        limits.append(jnp.sqrt(s * (1.0 / entries) + FLOOR))
    gt[0] = jnp.transpose(g[0:128])
    gt[1] = jnp.transpose(g[128:256])
    rows = [
        jnp.concatenate([gt[c, pl.ds(m, 24, stride=4), :] for m in range(4)], axis=1) for c in range(2)
    ]
    copies[0].wait()
    coarse = _dot3(jnp.concatenate(rows, axis=0), lambda i: w_all[i])
    position = lax.broadcasted_iota(jnp.int32, (48, 512), 1)
    highs = position >= (S >> (LEVELS + COARSE))
    square = jnp.where(highs, coarse * coarse, 0.0)
    square = square[:, 0:128] + square[:, 128:256] + square[:, 256:384] + square[:, 384:512]
    kept = jnp.zeros((8, 128), F32)
    row = 3 * _sublane(128)
    for j in range(3):
        kept = kept + jnp.where(row + j < 16, square[8 * j : 8 * j + 8], 0.0)
        kept = kept + jnp.where(row + j >= 8, square[24 + 8 * j : 32 + 8 * j], 0.0)
    square = jnp.sum(jnp.sum(kept, axis=0, keepdims=True), axis=1, keepdims=True)
    entries = (C >> LEVELS) * ((S >> LEVELS) - (S >> (LEVELS + COARSE)))
    limit = jnp.sqrt(square * (1.0 / entries) + FLOOR)
    coarse = jnp.where(highs, _shrink(coarse, limit), coarse)
    mine = jnp.where(core == 0, coarse[0:24], coarse[24:48])
    mine = jnp.concatenate([mine, jnp.zeros((8, 512), F32)], axis=0)
    hi = mine.astype(BF16)
    lo = (mine - hi.astype(F32)).astype(BF16)
    for c in copies[1:6]:
        c.wait()
    for k in range(3):
        before, after = near_left[k], near_right[k]
        at = lane % 4
        for ref, own, roll in ((x5h, a5h, 0), (x5l, a5l, 64)):
            a = pltpu.roll(before, (roll + 127) % 128, 1)
            b = pltpu.roll(after, (roll + 1) % 128, 1)
            ref[k] = jnp.where(at == 1, own[k], jnp.where(at == 0, a, b))
    def nt(a, b):
        return lax.dot_general(a, b, (((1,), (1,)), ((), ())), preferred_element_type=F32)

    current = nt(hi, v[0]) + nt(lo, v[0]) + nt(hi, v[1])

    def level(l, get_current, low, high, n, y, t, nxt, step, needed):
        tl = jnp.broadcast_to(limits[l] * (1.0 / KS), (8, 128))
        th = jnp.broadcast_to(limits[l] * KS, (8, 128))
        is_low = needed(lane)

        def get_low(k):
            return jnp.where(is_low, get_current(k), _shrink(low[k], tl))

        def store(j, m, value):
            nxt[pl.ds(j, m)] = value

        put = _Backward(y, t, store, step)
        _chan_inverse(get_low, lambda k: _shrink(high[k], th), n, w, l, 128, put)

    def pick(r, k, c, n):
        return _table(table, (r, k), (c, n))

    level(
        5, lambda k: current[8 * k : 8 * k + 8], x5l, x5h, 3, y5, pick(896, 128, 0, 128), c4, 6, lambda i: i < 32
    )
    level(4, lambda k: c4[k], a4l, a4h, 6, y4, pick(768, 128, 128, 128), c3, 12, lambda i: i < 32)
    level(3, lambda k: c3[k], a3l, a3h, 12, y3, pick(768, 128, 0, 128), c2, 24, lambda i: i < 64)
    level(2, lambda k: c2[k], a2l, a2h, 24, y2, pick(640, 128, 0, 256), c1, 24, lambda i: i < 85)
    for c in copies[6:]:
        c.wait()
    tl = jnp.broadcast_to(limits[1] * (1.0 / KS), (8, 256))
    th = jnp.broadcast_to(limits[1] * KS, (8, 256))
    lane2 = lax.broadcasted_iota(jnp.int32, (8, 256), 1)
    is_low1 = (lane2 < 64) | ((lane2 >= 192) & (lane2 < 208))

    def get_low1(k):
        v1 = jnp.concatenate([a1l[k], r1l[k]], axis=1)
        return jnp.where(is_low1, c1[k], _shrink(v1, tl))

    def get_high1(k):
        return _shrink(jnp.concatenate([a1h[k], r1h[k]], axis=1), th)

    def store1(j, m, value):
        c0[pl.ds(j, m)] = value

    put1 = _Backward(y1, pick(384, 256, 0, 256), store1, 24)
    _chan_inverse(get_low1, get_high1, 48, w, 1, 256, put1)
    tl0 = jnp.broadcast_to(limits[0] * (1.0 / KS), (8, 128))
    th0 = jnp.broadcast_to(limits[0] * KS, (8, 384))
    rim_low = lane < 32

    def get_low0(k):
        now = c0[k]
        rim = jnp.where(rim_low, _tile(now, 1), _shrink(rlow0[k], tl0))
        return jnp.concatenate([_tile(now, 0), _shrink(dlow0[k], tl0), rim], axis=1)

    def get_high0(k):
        return _shrink(jnp.concatenate([dhigh0[k], dhigh1[k], rhigh0[k]], axis=1), th0)

    def store0(j, m, value):
        for i in range(m):
            fa[pl.ds(j + i, 8, stride=SEG), :] = value[i, :, 0:128]
            fb[pl.ds(j + i, 8, stride=SEG), :] = value[i, :, 128:256]

    put0 = _Backward(y0, pick(0, 384, 0, 256), store0, 24)
    _chan_inverse(get_low0, get_high0, 96, w, 0, 384, put0)
    at_own = pl.multiple_of(core * HALO, 8)
    last = [
        pltpu.make_async_copy(buf.at[pl.ds(at_own, OWN)], out.at[:, pl.ds(128 * i, 128)], sems.at[1 + i])
        for i, buf in enumerate((fa, fb))
    ]
    for c in last:
        c.start()
    for c in last:
        c.wait()


VM = pl.BlockSpec(memory_space=pltpu.VMEM)
SM = pl.BlockSpec(memory_space=pltpu.SMEM)
ANY = pl.BlockSpec(memory_space=pl.ANY)
HBM = pl.BlockSpec(memory_space=pltpu.HBM)


def _call(kernel, name, limit, args, specs, outs, out_specs, scratch):
    args = [
        pltpu.with_memory_space_constraint(x, pltpu.HBM) if spec is HBM else x for x, spec in zip(args, specs)
    ]
    outs = [jax.ShapeDtypeStruct(s, F32) if isinstance(s, tuple) else s for s in outs]
    return pl.pallas_call(
        kernel,
        out_shape=[pltpu.HBM(s.shape, s.dtype) if spec is HBM else s for s, spec in zip(outs, out_specs)],
        in_specs=specs,
        out_specs=out_specs,
        scratch_shapes=[pltpu.VMEM(s, F32) if isinstance(s, tuple) else s for s in scratch],
        compiler_params=pltpu.CompilerParams(vmem_limit_bytes=limit << 20),
        name=name,
    )(*args)


def _shift(v, by):
    return lax.ppermute(v, "tm", [(i, i + by) for i in range(NT) if 0 <= i + by < NT])


def shards(record, gauge_table, gauge_index):
    tables = _tables()
    core = lax.axis_index("chan")
    place = lax.axis_index("tm")
    variant = jnp.where(place == 0, 0, jnp.where(place == NT - 1, 2, 1))
    sc = jnp.stack([core, variant, place]).astype(jnp.int32)
    dma = pltpu.SemaphoreType.DMA
    (sent,) = _call(_half_kernel, "half", 2, (sc, record), [SM, HBM], [(HALO, 256)], [ANY], [dma((4,))])
    recv = lax.ppermute(sent, "chan", [(0, 1), (1, 0)])
    right, left, rim_in, low0, a1l, sums, w, rim_table, own_kept = _call(
        _own_kernel, "own", 20,
        (sc, record, recv, gauge_table, gauge_index, tables["own"], tables["rim"]),
        [SM, HBM, ANY, HBM, HBM, HBM, HBM],
        [(72, 8, 128), (72, 8, 128), (SEG, 8, 128), (96, 8, 128), (48, 8, 128), (2, 8, 128),
         (LEVELS, 3, 8, 128), jax.ShapeDtypeStruct((2, 640, 256), BF16), (384, 8, 128)],
        [VM] * 8 + [HBM],
        [(LEVELS, GTAB), pltpu.VMEM((LEVELS, NBLK), jnp.int32), pltpu.VMEM((2, 384, 256), BF16), (384, 8, 128),
         (8 * SEG, 128), (8 * SEG, 128), (SEG, 8, 256), (SEG, 8, 256), (96, 8, 128), dma((10,))],
    )
    from_left, from_right = _shift(right, 1), _shift(left, -1)
    rim_kept, message, payload = _call(
        _rim_kernel, "rim", 16, (sc, rim_in, from_left, from_right, low0, a1l, sums, rim_table, w),
        [SM] + [VM] * 8, [(378, 8, 128), (3, 8, 128), (256, 128)], [HBM] * 3,
        [(378, 8, 128), (3, 8, 128), (256, 128),
         (SEG, 8, 128), (SEG, 8, 128), (96, 8, 128), (48, 8, 256), (48, 8, 128), (24, 8, 128), (12, 8, 128),
         (6, 8, 256), (3, 8, 256), dma((6,))],
    )
    everyone = lax.all_to_all(payload, ("chan", "tm"), split_axis=0, concat_axis=0, tiled=True)
    near_left, near_right = _shift(message, 1), _shift(message, -1)
    (out,) = _call(
        _back_kernel, "back", 24,
        (sc, everyone, near_left, near_right, tables["w"], tables["v"], tables["back"], own_kept, rim_kept, w),
        [SM, VM] + [HBM] * 7 + [VM], [(OWN, 256)], [HBM],
        [
            (3, 8, 128), (3, 8, 128), pltpu.VMEM((2, 512, 512), BF16), pltpu.VMEM((2, 1024, 256), BF16),
            (384, 8, 128), (378, 8, 128),
            pltpu.VMEM((2, 128, 512), BF16), (2, 128, 128), (3, 8, 128), (3, 8, 128),
            (6, 8, 128), (12, 8, 128), (24, 8, 128), (48, 8, 128), (96, 8, 256), (SEG, 8, 384),
            (6, 8, 128), (12, 8, 128), (24, 8, 128), (48, 8, 256), (96, 8, 256),
            (8 * SEG, 128), (8 * SEG, 128), dma((11,)),
        ],
    )
    return out


def solution(mesh):
    return jax.shard_map(
        shards,
        mesh=mesh,
        in_specs=(P("chan", "tm"), P(), P()),
        out_specs=P("chan", "tm"),
        check_vma=False,
    )
```

```python
import functools

import jax
import jax.numpy as jnp
import ml_dtypes
import numpy as np
from jax import lax
from jax.experimental import pallas as pl
from jax.experimental.pallas import tpu as pltpu
from jax.sharding import PartitionSpec as P

LEVELS = 6
COARSE = 6
GTAB = 8
NBLK = 32
C = 2048
S = 32768
NT = 128
OWN = 1024
HALO = 512
SEG = 192
A1 = -1.586134342059924
B1 = -0.052980118572961
A2 = 0.882911075530934
B2 = 0.443506852043971
KS = 1.149604398860241
FLOOR = 1e-06
F32 = jnp.float32
BF16 = jnp.bfloat16


def _next(e):
    return np.concatenate((e[1:], e[-1:]))


def _prev(o):
    return np.concatenate((o[:1], o[:-1]))


def _lift(x):
    e, o = x[0::2], x[1::2]
    o = o + A1 * (e + _next(e))
    e = e + B1 * (_prev(o) + o)
    o = o + A2 * (e + _next(e))
    e = e + B2 * (_prev(o) + o)
    return KS * e, o / KS


def _unlift(low, high):
    e, o = low / KS, high * KS
    e = e - B2 * (_prev(o) + o)
    o = o - A2 * (e + _next(e))
    e = e - B1 * (_prev(o) + o)
    o = o - A1 * (e + _next(e))
    return np.stack((e, o), axis=1).reshape((2 * e.shape[0],) + e.shape[1:])


def _forward(inputs, lows, highs, rows, cols, start, stop, scale):
    pairs = list(lows) + list(highs)
    a = max(2 * min(pairs) - 16, start)
    b = min(2 * max(pairs) + 16, stop)
    low, high = _lift(np.eye(b - a))
    out = np.zeros((rows, cols))
    for band, places in ((low, lows), (high, highs)):
        for pair, col in places.items():
            if a <= 2 * pair < b:
                line = band[pair - a // 2]
                for i in np.nonzero(line)[0]:
                    out[inputs[a + int(i)], col] += scale * line[i]
    return out


def _inverse(lows, highs, outputs, rows, cols, start, stop, scale):
    a = max(2 * (min(outputs) // 2) - 16, start) // 2
    b = min(2 * (max(outputs) // 2) + 18, stop) // 2
    n = b - a
    eye, zero = np.eye(n), np.zeros((n, n))
    from_low, from_high = _unlift(eye, zero), _unlift(zero, eye)
    out = np.zeros((rows, cols))
    for sample, col in outputs.items():
        if 2 * a <= sample < 2 * b:
            for lines, places in ((from_low, lows), (from_high, highs)):
                line = lines[sample - 2 * a]
                for i in np.nonzero(line)[0]:
                    out[places[a + int(i)], col] += scale * line[i]
    return out


def _pair(m):
    hi = m.astype(ml_dtypes.bfloat16)
    lo = (m - hi.astype(np.float64)).astype(ml_dtypes.bfloat16)
    return np.stack((hi, lo))


def _run(first, last, at):
    return {k: at + k - first for k in range(first, last)}


OWN_LOW0 = _run(2, 126, 2)
OWN_HIGH0 = _run(2, 126, 130)
RIM_LOW0 = {**_run(-10, 2, 0), **_run(126, 137, 12)}
RIM_HIGH0 = {**_run(-2, 2, 32), **_run(126, 130, 36)}
RIM_IN0 = {**_run(0, 32, 0), **_run(-32, 0, 32), **_run(256, 288, 64), **_run(224, 256, 96)}
OWN_LOW1 = _run(3, 61, 3)
OWN_HIGH1 = _run(2, 61, 66)
RIM_LOW1 = {**_run(-3, 3, 64), **_run(61, 67, 70)}
RIM_HIGH1 = {**_run(-3, 2, 80), **_run(61, 67, 85)}
IN1 = {**OWN_LOW0, **{k: 128 + v for k, v in RIM_LOW0.items()}}
IN2 = {
    **OWN_LOW1, **_run(67, 125, 67), **_run(-61, -3, 131), **{k: 128 + v for k, v in RIM_LOW1.items()}
}
LOW2 = _run(-28, 61, 0)
HIGH2 = _run(-3, 36, 89)
LOW3 = _run(-12, 29, 0)
HIGH3 = _run(-3, 20, 64)
LOW4 = _run(-4, 13, 0)
HIGH4 = _run(-3, 12, 32)
LOW5 = _run(-4, 8, 0)
HIGH5 = _run(-4, 8, 16)


def _part(places, first, last):
    return {k: places[k] for k in range(first, last)}


def _edges(width):
    far = 1 << 20
    return ((0, far), (-far, far), (-far, width))


def _bundle(parts, rows, cols):
    out = np.zeros((rows, cols))
    for r, c, m in parts:
        out[r : r + m.shape[0], c : c + m.shape[1]] = m
    return _pair(out)


@functools.cache
def _tables():
    fw, inv = _forward, _inverse
    far = 1 << 20
    out = {}
    out["own"] = _bundle(
        (
            (0, 0, fw(_run(0, 256, 0), OWN_LOW0, OWN_HIGH0, 256, 256, -far, far, 1.0)),
            (256, 0, fw(OWN_LOW0, OWN_LOW1, OWN_HIGH1, 128, 128, -far, far, KS)),
        ),
        384,
        256,
    )
    rim, back = [], []
    for v in range(3):
        a, b = zip(*(_edges(256 >> l)[v] for l in range(LEVELS)))
        t5 = fw(LOW4, _part(LOW5, 0, 5), _part(HIGH5, 0, 5), 128, 256, a[5], b[5], KS)
        lows, highs = t5[:, 4:8].copy(), t5[:, 20:24].copy()
        sixteen = np.concatenate([lows, highs[:, 1:], lows[:, 1:], highs[:, 1:], np.zeros((128, 3))], axis=1)
        t5[:, 128:] = np.tile(sixteen, (1, 8))
        rim.append(
            _bundle(
                (
                    (0, 0, fw(IN1, RIM_LOW1, RIM_HIGH1, 256, 128, a[1], b[1], KS)),
                    (0, 128, fw(IN2, LOW2, HIGH2, 256, 128, a[2], b[2], KS)),
                    (0, 256, fw(LOW2, LOW3, HIGH3, 128, 128, a[3], b[3], KS)),
                    (128, 256, fw(LOW3, LOW4, HIGH4, 128, 128, a[4], b[4], KS)),
                    (256, 0, t5),
                    (384, 0, fw(RIM_IN0, RIM_LOW0, RIM_HIGH0, 128, 128, a[0], b[0], 1.0)),
                ),
                512,
                384,
            )
        )
        low0 = {**OWN_LOW0, **{k: 256 + v for k, v in RIM_LOW0.items() if -2 <= k < 130}}
        high0 = {**OWN_HIGH0, **{k: 256 + v for k, v in RIM_HIGH0.items()}}
        low1 = {**OWN_LOW1, **{k: 128 + v for k, v in RIM_LOW1.items()}}
        high1 = {**OWN_HIGH1, **{k: 128 + v for k, v in RIM_HIGH1.items()}}
        back.append(
            _bundle(
                (
                    (0, 0, inv(low0, high0, _run(0, 256, 0), 384, 256, a[0], b[0], 1.0)),
                    (384, 0, inv(low1, high1, _part(IN1, -1, 130), 256, 256, a[1], b[1], 1.0 / KS)),
                    (640, 0, inv(LOW2, HIGH2, _part(low1, -2, 67), 128, 256, a[2], b[2], 1.0 / KS)),
                    (768, 0, inv(LOW3, HIGH3, _part(LOW2, -2, 36), 128, 128, a[3], b[3], 1.0 / KS)),
                    (768, 128, inv(LOW4, HIGH4, _part(LOW3, -2, 20), 128, 128, a[4], b[4], 1.0 / KS)),
                    (896, 0, inv(LOW5, HIGH5, _part(LOW4, -2, 12), 128, 128, a[5], b[5], 1.0 / KS)),
                ),
                1024,
                256,
            )
        )
    out["rim"], out["back"] = np.stack(rim), np.stack(back)
    n = S >> LEVELS
    bands = []
    current = np.eye(n)
    for _ in range(COARSE):
        current, high = _lift(current)
        bands.append(high)
    coarse = np.concatenate([current] + bands[::-1])
    order = (np.arange(n) % NT) * 4 + np.arange(n) // NT
    last = n >> COARSE
    current = np.eye(n)[:last]
    for step in range(COARSE):
        size = last << step
        current = _unlift(current, np.eye(n)[size : 2 * size])
    both = np.zeros((n + 640, n))
    both[:n] = (KS * coarse.T)[order]
    both[n + 4 : 2 * n + 4] = current / KS
    out["coarse"] = _pair(both)
    return out


def _mask(lane, places, first, last, base=0):
    lanes = sorted(v - base for k, v in places.items() if first <= k < last)
    out, i = None, 0
    while i < len(lanes):
        j = i
        while j + 1 < len(lanes) and lanes[j + 1] == lanes[j] + 1:
            j += 1
        hit = (lane >= lanes[i]) & (lane <= lanes[j])
        out = hit if out is None else out | hit
        i = j + 1
    return out


def _ones(hit):
    return jnp.where(hit, 1.0, 0.0)


def _dot3(x, t):
    hi = x.astype(BF16)
    lo = (x - hi.astype(F32)).astype(BF16)
    d = functools.partial(jnp.dot, preferred_element_type=F32)
    return d(hi, t(0)) + d(lo, t(0)) + d(hi, t(1))


def _time(load, t, y, step, j):
    x = load(j, step)
    y[pl.ds(j, step)] = _dot3(x.reshape(step * 8, x.shape[2]), t).reshape(step, 8, y.shape[2])


class _Forward:
    def __init__(self, load, t, y, step):
        self.load, self.t, self.y, self.step, self.done = load, t, y, step, 0

    def __call__(self, j):
        ahead = min(j + self.step, self.y.shape[0] - 1)
        while self.done <= ahead:
            _time(self.load, self.t, self.y, self.step, self.done)
            self.done += self.step
        return self.y[j]


class _Backward:
    def __init__(self, y, t, store, step):
        self.y, self.t, self.store, self.step, self.left = y, t, store, step, {}

    def __call__(self, j, value):
        self.y[j] = value
        chunk = j // self.step
        self.left[chunk] = self.left.get(chunk, self.step) - 1
        if not self.left[chunk]:
            x = self.y[pl.ds(chunk * self.step, self.step)]
            out = _dot3(x.reshape(self.step * 8, x.shape[2]), self.t)
            self.store(chunk * self.step, self.step, out.reshape(self.step, 8, out.shape[1]))


def _table(ref, rows, cols, *lead):
    r, c = pl.ds(*rows), pl.ds(*cols)
    return lambda i: ref[(*lead, i, r, c)]


def _sublane(lanes):
    return lax.broadcasted_iota(jnp.int32, (8, lanes), 0)


def _lane(rows=8):
    return lax.broadcasted_iota(jnp.int32, (rows, 128), 1)


def _wide(v, lanes):
    return v if lanes == 128 else jnp.concatenate([v] * (lanes // 128), axis=1)


class _Wrap:
    def __init__(self, lanes):
        sub = _sublane(lanes)
        self.last, self.first = sub == 7, sub == 0

    def after(self, first, last):
        return jnp.where(self.last, last, pltpu.roll(first, 7, 0))

    def before(self, last, first):
        return jnp.where(self.first, first, pltpu.roll(last, 1, 0))


def _coefs(w_ref, level, lanes):
    return [[_wide(c * w_ref[level, q], lanes) for q in range(3)] for c in (A1, B1, A2, B2)]


def _chan_forward(get, n, w_ref, level, lanes, put_low, put_high):
    wrap = _Wrap(lanes)
    ca, cb, cc, cd = _coefs(w_ref, level, lanes)
    per = n // 3
    first = get(0)
    e, o1, e1, o2 = {0: first}, {}, {}, {}

    def high(k, v):
        o2[k] = v
        put_high(k, k // per, v)

    def low(k):
        put_low(k, k // per, e1[k] + cd[k // per] * (o2[k - 1] + o2[k]))

    for k in range(n):
        q = k // per
        e[k + 1] = get(2 * k + 2) if k + 1 < n else wrap.after(first, e[k])
        o1[k] = get(2 * k + 1) + ca[q] * (e[k] + e[k + 1])
        if k >= 1:
            e1[k] = e[k] + cb[q] * (o1[k - 1] + o1[k])
        if k >= 2:
            high(k - 1, o1[k - 1] + cc[(k - 1) // per] * (e1[k - 1] + e1[k]))
        if k >= 3:
            low(k - 1)
    e1[0] = first + cb[0] * (wrap.before(o1[n - 1], o1[0]) + o1[0])
    high(0, o1[0] + cc[0] * (e1[0] + e1[1]))
    high(n - 1, o1[n - 1] + cc[2] * (e1[n - 1] + wrap.after(e1[0], e1[n - 1])))
    o2[-1] = wrap.before(o2[n - 1], o2[0])
    for k in (0, 1, n - 1):
        low(k)


def _chan_inverse(get_low, get_high, n, w_ref, level, lanes, put):
    wrap = _Wrap(lanes)
    ca, cb, cc, cd = _coefs(w_ref, level, lanes)
    per = n // 3
    o = {0: get_high(0)}
    o[-1] = wrap.before(get_high(n - 1), o[0])
    e1, o1, e2 = {}, {}, {}

    def even(k):
        e2[k] = e1[k] - cb[k // per] * (o1[k - 1] + o1[k])
        put(2 * k, e2[k])

    def odd(k):
        put(2 * k + 1, o1[k] - ca[k // per] * (e2[k] + e2[k + 1]))

    for k in range(n):
        q = k // per
        if k:
            o[k] = get_high(k)
        e1[k] = get_low(k) - cd[q] * (o[k - 1] + o[k])
        if k >= 1:
            o1[k - 1] = o[k - 1] - cc[(k - 1) // per] * (e1[k - 1] + e1[k])
        if k >= 2:
            even(k - 1)
        if k >= 3:
            odd(k - 2)
    o1[n - 1] = o[n - 1] - cc[2] * (e1[n - 1] + wrap.after(e1[0], e1[n - 1]))
    o1[-1] = wrap.before(o1[n - 1], o1[0])
    even(n - 1)
    if n > 2:
        odd(n - 2)
    even(0)
    odd(0)
    e2[n] = wrap.after(e2[0], e2[n - 1])
    odd(n - 1)


class _Squares:
    def __init__(self):
        self.acc = {}

    def add(self, key, v):
        self.acc[key] = v * v if key not in self.acc else self.acc[key] + v * v

    def total(self, rows, tiles):
        out = None
        for q in range(3):
            part = None
            for (band, tile), lanes in tiles.items():
                v = self.acc[(band, tile, q)] * (KS * KS if band == "low" else 1.0 / (KS * KS))
                v = v if lanes is None else v * lanes
                part = v if part is None else part + v
            part = part * rows[q]
            out = part if out is None else out + part
        return out


def _tile(v, i):
    return v[:, 128 * i : 128 * (i + 1)]


def _own_rows(core):
    block = 3 * _sublane(128)
    return [
        jnp.where(core == 0, _ones(block + q < 16), _ones(block + q >= 8)) for q in range(3)
    ]


def _load_kernel(
    sc, x_all, gauge_table_all, gauge_index_all, own_all, rim_all,
    low, high, ends, own_table, rim_table, w,
    x, gauge_table, gauge_index, sems,
):
    core = sc[0]
    copies = [
        pltpu.make_async_copy(src, dst, sems.at[i])
        for i, (src, dst) in enumerate(
            (
                (gauge_index_all, gauge_index),
                (gauge_table_all, gauge_table),
                (own_all, own_table),
                *((x_all.at[pl.ds(256 * i, 256)], x.at[pl.ds(256 * i, 256)]) for i in range(4)),
                (rim_all.at[sc[1]], rim_table),
            )
        )
    ]
    for c in copies:
        c.start()
    for c in copies[:2]:
        c.wait()
    index = gauge_index[...]
    table_rows = gauge_table[...]
    weights = jnp.zeros(index.shape, F32)
    for g in range(GTAB):
        weights = weights + jnp.where(index == g, table_rows[:, g : g + 1], 0.0)
    block = lax.broadcasted_iota(jnp.int32, (8, NBLK), 1) - 3 * lax.broadcasted_iota(jnp.int32, (8, NBLK), 0)
    block = block - 8 * core
    for l in range(LEVELS):
        for q in range(3):
            hit = jnp.where(block == q, weights[l : l + 1], 0.0)
            w[l, q] = jnp.broadcast_to(jnp.sum(hit, axis=1, keepdims=True), (8, 128))
    copies[2].wait()
    for i in range(4):
        copies[3 + i].wait()
        _first(x, own_table, low, high, ends, 0, range(256 * i, 256 * i + 256, 128))
    copies[7].wait()


def _first(x, table, low, high, ends, at, blocks):
    lane = _lane(128)
    for r in blocks:
        v = x[pl.ds(r, 128), :]
        y = _dot3(v, _table(table, (0, 256), (0, 256)))
        rows = pl.ds(at + r, 128)
        low[rows, :] = y[:, 0:128]
        high[rows, :] = y[:, 128:256]
        ends[rows, :] = jnp.where(lane < 32, v[:, 0:128], v[:, 128:256])


def _own_kernel(
    sc, recv, own_low, own_high, own_ends, table, w,
    right, left, rim_in, low0, a1l, details, sums,
    fl, fh, fe, y1,
):
    core = sc[0]
    at_own = pl.multiple_of(core * HALO, 8)
    at_recv = pl.multiple_of((1 - core) * OWN, 8)
    for src, dst in ((own_low, fl), (own_high, fh), (own_ends, fe)):
        for r in range(0, OWN, 128):
            dst[pl.ds(at_own + r, 128), :] = src[pl.ds(r, 128), :]
    theirs = recv.at[pl.ds(at_own, HALO)]
    _first(theirs, table, fl, fh, fe, at_recv, range(0, HALO, 128))
    lane = _lane()
    group = lane // 32
    for i in range(48):
        to_right, to_left = None, None
        for g in range(4):
            j = 48 * g + i
            v = fe[pl.ds(j, 8, stride=SEG), :]
            rim_in[j] = v
            a = pltpu.roll(v, 32 * g, 1) if g else v
            b = pltpu.roll(v, (32 * g + 32) % 128, 1) if g != 3 else v
            to_left = a if to_left is None else jnp.where(group == g, a, to_left)
            to_right = b if to_right is None else jnp.where(group == g, b, to_right)
        right[i] = to_right
        left[i] = to_left
    rows = _own_rows(core)
    sq = _Squares()

    def put_low(k, q, v):
        low0[k] = _tile(v, 0)
        details[k] = _tile(v, 1)
        sq.add(("low", 1, q), _tile(v, 1))

    def put_high(k, q, v):
        details[96 + k] = _tile(v, 0)
        details[192 + k] = _tile(v, 1)
        sq.add(("high", 0, q), _tile(v, 0))
        sq.add(("high", 1, q), _tile(v, 1))

    def get(j):
        rows = pl.ds(j, 8, stride=SEG)
        return jnp.concatenate([fl[rows, :], fh[rows, :]], axis=1)

    _chan_forward(get, 96, w, 0, 256, put_low, put_high)
    sums[0] = sq.total(rows, {("low", 1): None, ("high", 0): None, ("high", 1): None})
    sq1 = _Squares()

    def put_low1(k, q, v):
        a1l[k] = v
        details[288 + k] = v
        sq1.add(("low", 0, q), v)
        if k >= 26:
            packed = jnp.where(lane < 64, a1l[k - 24], pltpu.roll(v, 64, 1))
            right[24 + k] = packed
            left[24 + k] = packed

    def put_high1(k, q, v):
        details[336 + k] = v
        sq1.add(("high", 0, q), v)

    get = _Forward(lambda j, n: low0[pl.ds(j, n)], _table(table, (256, 128), (0, 128)), y1, 24)
    _chan_forward(get, 48, w, 1, 128, put_low1, put_high1)
    for k in (24, 25):
        packed = jnp.where(lane < 64, a1l[k - 24], pltpu.roll(a1l[k], 64, 1))
        right[24 + k] = packed
        left[24 + k] = packed
    sums[1] = sq1.total(rows, {("low", 0): _ones(_mask(lane, OWN_HIGH1, 0, 64)), ("high", 0): None})


def _bands(details):
    out, at = [], 0
    for n in (96, 48, 24, 12, 6, 3):
        out += [details.at[pl.ds(at, n)], details.at[pl.ds(at + n, n)]]
        at += 2 * n
    return out


def _fetch_kernel(sc, after, back_all, coarse_all, back_table, coarse_table, sems):
    del after
    copies = []
    for src, dst, parts in ((back_all.at[sc[1]], back_table, 4), (coarse_all, coarse_table, 4)):
        n = dst.shape[1] // parts
        for i in range(2):
            for k in range(parts):
                rows = pl.ds(n * k, n)
                copies.append(pltpu.make_async_copy(src.at[i, rows], dst.at[i, rows], sems.at[len(copies)]))
    for c in copies:
        c.start()
    for c in copies:
        c.wait()


def _rim_kernel(
    sc, rim_in, from_left, from_right, low0, a1l, own_sums, table, w, after,
    details, payload,
    rim, y0, y1, x2, y2, y3, y4, y5, l5, h5, flat,
):
    del after
    core = sc[0]
    rlow0, rhigh0, r1l, r1h, a2l, a2h, a3l, a3h, a4l, a4h, a5l, a5h = _bands(details)
    lane = _lane()
    for j in range(SEG):
        g, i = j // 48, j % 48
        a = from_left[i]
        b = from_right[i]
        a = pltpu.roll(a, (32 - 32 * g) % 128, 1) if g != 1 else a
        b = pltpu.roll(b, (64 - 32 * g) % 128, 1) if g != 2 else b
        halo = jnp.where(lane < 64, a, b)
        rim[j] = jnp.where((lane < 32) | (lane >= 96), rim_in[j], halo)
    rows = _own_rows(core)
    totals = []

    def level(l, load, n, t, y, step, lanes, low, high, own_low, own_high, pairs):
        sq = _Squares()

        def put_low(k, q, value):
            low[k] = value
            sq.add(("low", 0, q), _tile(value, 0))

        def put_high(k, q, value):
            high[k] = value
            sq.add(("high", 0, q), _tile(value, 0))

        _chan_forward(_Forward(load, t, y, step), n, w, l, lanes, put_low, put_high)
        is_high = _mask(lane, own_high, 0, pairs)
        is_low = _mask(lane, own_low, 0, pairs)
        total = sq.total(rows, {("low", 0): _ones(is_high), ("high", 0): _ones(is_high | is_low)})
        totals.append(total + own_sums[l] if l < 2 else total)

    def pick(r, k, c, n):
        return _table(table, (r, k), (c, n))

    level(0, lambda j, n: rim[pl.ds(j, n)], 96, pick(384, 128, 0, 128), y0, 24, 128, rlow0, rhigh0, RIM_LOW0, RIM_HIGH0, 128)

    def load1(j, n):
        return jnp.concatenate([low0[pl.ds(j, n)], rlow0[pl.ds(j, n)]], axis=2)

    level(1, load1, 48, pick(0, 256, 0, 128), y1, 24, 128, r1l, r1h, RIM_LOW1, RIM_HIGH1, 64)
    for j in range(48):
        h, i = j // 24, 48 + j % 24
        b, a = from_left[i], from_right[i]
        if h == 0:
            a = pltpu.roll(a, 64, 1)
        else:
            b = pltpu.roll(b, 64, 1)
        x2[j, :, 0:128] = jnp.where(lane < 64, a1l[j], a)
        x2[j, :, 128:256] = jnp.where(lane < 64, b, r1l[j])
    level(2, lambda j, n: x2[pl.ds(j, n)], 24, pick(0, 256, 128, 128), y2, 24, 128, a2l, a2h, LOW2, HIGH2, 32)
    level(3, lambda j, n: a2l[pl.ds(j, n)], 12, pick(0, 128, 256, 128), y3, 24, 128, a3l, a3h, LOW3, HIGH3, 16)
    level(4, lambda j, n: a3l[pl.ds(j, n)], 6, pick(128, 128, 256, 128), y4, 12, 128, a4l, a4h, LOW4, HIGH4, 8)
    level(5, lambda j, n: a4l[pl.ds(j, n)], 3, pick(256, 128, 0, 256), y5, 6, 256, l5, h5, LOW5, HIGH5, 4)
    sub = _sublane(128)
    for j in range(3):
        a5l[j] = l5[j, :, 0:128]
        a5h[j] = h5[j, :, 0:128]
        flat[pl.ds(j, 8, stride=3), :] = jnp.where(lane % 16 < 7, l5[j, :, 128:256], h5[j, :, 128:256])
    sums = jnp.zeros((8, 128), F32)
    for l in range(LEVELS):
        sums = jnp.where(sub == l, jnp.sum(totals[l], axis=0, keepdims=True), sums)
    sums = jnp.where((lane == 16 * sub + 13) & (sub < LEVELS), jnp.sum(sums, axis=1, keepdims=True), 0.0)
    lines = []
    for h in range(2):
        mine = flat[pl.ds(pl.multiple_of(8 * core + 8 * h, 8), 8), :]
        mine = jnp.where(lane // 16 == sub, mine, 0.0)
        lines.append(jnp.sum(mine + sums if h == 0 else mine, axis=0, keepdims=True))
    block = jnp.where(sub % 2 == 0, lines[0], lines[1])
    for i in range(64):
        payload[pl.ds(8 * i, 8), :] = block


def _shrink(v, limit):
    return v - jnp.minimum(jnp.maximum(v, -limit), limit)


def _back_kernel(
    sc, g, coarse_table, table, own_details, rim_details, w,
    out,
    gt, nears, cur, x5l, x5h, y5, y4, y3, y2, y1, y0, c4, c3, c2, c1, c0, fa, fb, sems,
):
    core, place = sc[0], sc[2]
    rlow0, rhigh0, r1l, r1h, a2l, a2h, a3l, a3h, a4l, a4h, a5l, a5h = _bands(rim_details)
    dlow0, dhigh0, dhigh1 = (own_details.at[pl.ds(96 * i, 96)] for i in range(3))
    a1l, a1h = (own_details.at[pl.ds(288 + 48 * i, 48)] for i in range(2))
    lane = _lane()
    lane1 = _lane(1)
    sub = _sublane(128)
    for h in range(2):
        half = g[pl.ds(h, 256, stride=2), :]
        if h == 0:
            total = jnp.sum(half, axis=0, keepdims=True)
        for c in range(2):
            gt[c, h] = jnp.transpose(half[NT * c : NT * c + NT])
    limits = []
    for l in range(LEVELS):
        entries = 3 * (C >> (l + 1)) * (S >> (l + 1))
        s = jnp.sum(jnp.where(lane1 == 16 * l + 13, total, 0.0), axis=1, keepdims=True)
        limits.append(jnp.sqrt(s * (1.0 / entries) + FLOOR))
    rows = [
        jnp.concatenate([gt[c, h, pl.ds(m, 8, stride=16), :] for m in range(4)], axis=1)
        for c in range(2)
        for h in range(2)
    ]
    coarse = _dot3(jnp.concatenate(rows, axis=0), lambda i: coarse_table[i, 0:512, :])
    highs = lax.broadcasted_iota(jnp.int32, (32, 512), 1) >= (S >> (LEVELS + COARSE))
    square = jnp.sum(jnp.where(highs, coarse * coarse, 0.0), axis=0, keepdims=True)
    square = jnp.sum(square, axis=1, keepdims=True)
    entries = (C >> LEVELS) * ((S >> LEVELS) - (S >> (LEVELS + COARSE)))
    limit = jnp.sqrt(square * (1.0 / entries) + FLOOR)
    coarse = jnp.where(highs, _shrink(coarse, limit), coarse)
    hi = coarse.astype(BF16)
    lo = (coarse - hi.astype(F32)).astype(BF16)
    for side, other in enumerate((jnp.maximum(place - 1, 0), jnp.minimum(place + 1, NT - 1))):
        for c in range(2):
            for h in range(2):
                line = jnp.broadcast_to(g[pl.ds(2 * (NT * c + other) + h, 1), :], (8, 128))
                near = line
                for k in range(1, 8):
                    near = jnp.where(sub == k, pltpu.roll(line, 128 - 16 * k, 1), near)
                nears[side, pl.ds(16 * c + 8 * h, 8), :] = near
    for k in range(3):
        rows = pl.ds(8 * core + k, 8, stride=3)
        before, after = nears[0, rows, :], nears[1, rows, :]
        v = a5h[k]
        for at, near, shift in ((1, before, 122), (9, after, 2), (17, before, 7), (25, after, 15)):
            v = jnp.where((lane >= at) & (lane < at + 3), pltpu.roll(near, shift, 1), v)
        x5h[k] = v
        v = a5l[k]
        for at, near, shift in ((17, before, 13), (25, after, 21)):
            v = jnp.where((lane >= at) & (lane < at + 3), pltpu.roll(near, shift, 1), v)
        x5l[k] = v

    def nt(a, b):
        return lax.dot_general(a, b, (((1,), (1,)), ((), ())), preferred_element_type=F32)

    rows = pl.ds(pl.multiple_of(512 + 16 * (place // 4), 16), 128)
    current = nt(hi, coarse_table[0, rows, :]) + nt(lo, coarse_table[0, rows, :]) + nt(hi, coarse_table[1, rows, :])
    cur[...] = pltpu.roll(current, (128 - 4 * (place % 4)) % 128, 1)

    def level(l, get_current, low, high, n, y, t, nxt, step, needed):
        tl = jnp.broadcast_to(limits[l] * (1.0 / KS), (8, 128))
        th = jnp.broadcast_to(limits[l] * KS, (8, 128))
        is_low = needed(lane)

        def get_low(k):
            return jnp.where(is_low, get_current(k), _shrink(low[k], tl))

        def store(j, m, value):
            nxt[pl.ds(j, m)] = value

        put = _Backward(y, t, store, step)
        _chan_inverse(get_low, lambda k: _shrink(high[k], th), n, w, l, 128, put)

    def pick(r, k, c, n):
        return _table(table, (r, k), (c, n))

    level(
        5, lambda k: cur[pl.ds(8 * core + k, 8, stride=3), :], x5l, x5h, 3, y5, pick(896, 128, 0, 128), c4, 6, lambda i: i < 12
    )
    level(4, lambda k: c4[k], a4l, a4h, 6, y4, pick(768, 128, 128, 128), c3, 12, lambda i: i < 32)
    level(3, lambda k: c3[k], a3l, a3h, 12, y3, pick(768, 128, 0, 128), c2, 24, lambda i: i < 64)
    level(2, lambda k: c2[k], a2l, a2h, 24, y2, pick(640, 128, 0, 256), c1, 24, lambda i: i < 89)
    tl = jnp.broadcast_to(limits[1] * (1.0 / KS), (8, 256))
    th = jnp.broadcast_to(limits[1] * KS, (8, 256))
    lane2 = lax.broadcasted_iota(jnp.int32, (8, 256), 1)
    is_low1 = (lane2 < 64) | ((lane2 >= 192) & (lane2 < 208))

    def get_low1(k):
        v1 = jnp.concatenate([a1l[k], r1l[k]], axis=1)
        return jnp.where(is_low1, c1[k], _shrink(v1, tl))

    def get_high1(k):
        return _shrink(jnp.concatenate([a1h[k], r1h[k]], axis=1), th)

    def store1(j, m, value):
        c0[pl.ds(j, m)] = value

    put1 = _Backward(y1, pick(384, 256, 0, 256), store1, 24)
    _chan_inverse(get_low1, get_high1, 48, w, 1, 256, put1)
    tl0 = jnp.broadcast_to(limits[0] * (1.0 / KS), (8, 128))
    th0 = jnp.broadcast_to(limits[0] * KS, (8, 384))
    rim_low = lane < 32

    def get_low0(k):
        now = c0[k]
        rim = jnp.where(rim_low, _tile(now, 1), _shrink(rlow0[k], tl0))
        return jnp.concatenate([_tile(now, 0), _shrink(dlow0[k], tl0), rim], axis=1)

    def get_high0(k):
        return _shrink(jnp.concatenate([dhigh0[k], dhigh1[k], rhigh0[k]], axis=1), th0)

    def store0(j, m, value):
        for i in range(m):
            fa[pl.ds(j + i, 8, stride=SEG), :] = value[i, :, 0:128]
            fb[pl.ds(j + i, 8, stride=SEG), :] = value[i, :, 128:256]

    put0 = _Backward(y0, pick(0, 384, 0, 256), store0, 24)
    _chan_inverse(get_low0, get_high0, 96, w, 0, 384, put0)
    at_own = pl.multiple_of(core * HALO, 8)
    last = [
        pltpu.make_async_copy(buf.at[pl.ds(at_own, OWN)], out.at[:, pl.ds(128 * i, 128)], sems.at[i])
        for i, buf in enumerate((fa, fb))
    ]
    for c in last:
        c.start()
    for c in last:
        c.wait()


VM = pl.BlockSpec(memory_space=pltpu.VMEM)
SM = pl.BlockSpec(memory_space=pltpu.SMEM)
ANY = pl.BlockSpec(memory_space=pl.ANY)
HBM = pl.BlockSpec(memory_space=pltpu.HBM)


def _call(kernel, name, limit, args, specs, outs, out_specs, scratch):
    args = [
        pltpu.with_memory_space_constraint(x, pltpu.HBM) if spec is HBM else x for x, spec in zip(args, specs)
    ]
    outs = [jax.ShapeDtypeStruct(s, F32) if isinstance(s, tuple) else s for s in outs]
    return pl.pallas_call(
        kernel,
        out_shape=[pltpu.HBM(s.shape, s.dtype) if spec is HBM else s for s, spec in zip(outs, out_specs)],
        in_specs=specs,
        out_specs=out_specs,
        scratch_shapes=[pltpu.VMEM(s, F32) if isinstance(s, tuple) else s for s in scratch],
        compiler_params=pltpu.CompilerParams(vmem_limit_bytes=limit << 20),
        name=name,
    )(*args)


def _shift(v, by):
    return lax.ppermute(v, "tm", [(i, i + by) for i in range(NT) if 0 <= i + by < NT])


def shards(record, gauge_table, gauge_index):
    tables = _tables()
    core = lax.axis_index("chan")
    place = lax.axis_index("tm")
    variant = jnp.where(place == 0, 0, jnp.where(place == NT - 1, 2, 1))
    sc = jnp.stack([core, variant, place]).astype(jnp.int32)
    dma = pltpu.SemaphoreType.DMA
    recv = lax.ppermute(record, "chan", [(0, 1), (1, 0)])
    low, high, ends, own_table, rim_table, w = _call(
        _load_kernel, "load", 12, (sc, record, gauge_table, gauge_index, tables["own"], tables["rim"]),
        [SM] + [HBM] * 5,
        [(OWN, 128), (OWN, 128), (OWN, 128), jax.ShapeDtypeStruct((2, 384, 256), BF16),
         jax.ShapeDtypeStruct((2, 512, 384), BF16), (LEVELS, 3, 8, 128)],
        [VM] * 6,
        [(OWN, 256), (LEVELS, GTAB), pltpu.VMEM((LEVELS, NBLK), jnp.int32), dma((8,))],
    )
    right, left, rim_in, low0, a1l, own_details, sums = _call(
        _own_kernel, "own", 12, (sc, recv, low, high, ends, own_table, w), [SM] + [VM] * 6,
        [(72, 8, 128), (72, 8, 128), (SEG, 8, 128), (96, 8, 128), (48, 8, 128), (384, 8, 128), (2, 8, 128)],
        [VM] * 7,
        [(8 * SEG, 128), (8 * SEG, 128), (8 * SEG, 128), (48 * 2, 8, 128)],
    )
    from_left, from_right = _shift(right, 1), _shift(left, -1)
    back_table, coarse_table = _call(
        _fetch_kernel, "fetch", 2, (sc, sums, tables["back"], tables["coarse"]), [SM, VM, HBM, HBM],
        [jax.ShapeDtypeStruct((2, 1024, 256), BF16), jax.ShapeDtypeStruct((2, 1152, 512), BF16)], [VM] * 2,
        [dma((16,))],
    )
    rim_details, payload = _call(
        _rim_kernel, "rim", 16, (sc, rim_in, from_left, from_right, low0, a1l, sums, rim_table, w, back_table), [SM] + [VM] * 8 + [ANY],
        [(378, 8, 128), (512, 128)], [VM] * 2,
        [(SEG, 8, 128), (SEG, 8, 128), (96, 8, 128), (48, 8, 256), (48, 8, 128), (24, 8, 128), (12, 8, 128),
         (6, 8, 256), (3, 8, 256), (3, 8, 256), (24, 128)],
    )
    everyone = lax.all_to_all(payload, ("chan", "tm"), split_axis=0, concat_axis=0, tiled=True)
    (out,) = _call(
        _back_kernel, "back", 24, (sc, everyone, coarse_table, back_table, own_details, rim_details, w),
        [SM] + [VM] * 6, [(OWN, 256)], [HBM],
        [
            (2, 2, 128, 128), (2, 32, 128), (32, 128), (3, 8, 128), (3, 8, 128),
            (6, 8, 128), (12, 8, 128), (24, 8, 128), (48, 8, 128), (96, 8, 256), (SEG, 8, 384),
            (6, 8, 128), (12, 8, 128), (24, 8, 128), (48, 8, 256), (96, 8, 256),
            (8 * SEG, 128), (8 * SEG, 128), dma((2,)),
        ],
    )
    return out


def solution(mesh):
    return jax.shard_map(
        shards,
        mesh=mesh,
        in_specs=(P("chan", "tm"), P(), P()),
        out_specs=P("chan", "tm"),
        check_vma=False,
    )
```

```python
import functools

import jax
import jax.numpy as jnp
import ml_dtypes
import numpy as np
from jax import lax
from jax.experimental import pallas as pl
from jax.experimental.pallas import tpu as pltpu
from jax.sharding import PartitionSpec as P

LEVELS = 6
COARSE = 6
GTAB = 8
NBLK = 32
C = 2048
S = 32768
NT = 128
OWN = 1024
HALO = 512
SEG = 192
A1 = -1.586134342059924
B1 = -0.052980118572961
A2 = 0.882911075530934
B2 = 0.443506852043971
KS = 1.149604398860241
FLOOR = 1e-06
F32 = jnp.float32
BF16 = jnp.bfloat16


def _next(e):
    return np.concatenate((e[1:], e[-1:]))


def _prev(o):
    return np.concatenate((o[:1], o[:-1]))


def _lift(x):
    e, o = x[0::2], x[1::2]
    o = o + A1 * (e + _next(e))
    e = e + B1 * (_prev(o) + o)
    o = o + A2 * (e + _next(e))
    e = e + B2 * (_prev(o) + o)
    return KS * e, o / KS


def _unlift(low, high):
    e, o = low / KS, high * KS
    e = e - B2 * (_prev(o) + o)
    o = o - A2 * (e + _next(e))
    e = e - B1 * (_prev(o) + o)
    o = o - A1 * (e + _next(e))
    return np.stack((e, o), axis=1).reshape((2 * e.shape[0],) + e.shape[1:])


def _forward(inputs, lows, highs, rows, cols, start, stop, scale):
    pairs = list(lows) + list(highs)
    a = max(2 * min(pairs) - 16, start)
    b = min(2 * max(pairs) + 16, stop)
    low, high = _lift(np.eye(b - a))
    out = np.zeros((rows, cols))
    for band, places in ((low, lows), (high, highs)):
        for pair, col in places.items():
            if a <= 2 * pair < b:
                line = band[pair - a // 2]
                for i in np.nonzero(line)[0]:
                    out[inputs[a + int(i)], col] += scale * line[i]
    return out


def _inverse(lows, highs, outputs, rows, cols, start, stop, scale):
    a = max(2 * (min(outputs) // 2) - 16, start) // 2
    b = min(2 * (max(outputs) // 2) + 18, stop) // 2
    n = b - a
    eye, zero = np.eye(n), np.zeros((n, n))
    from_low, from_high = _unlift(eye, zero), _unlift(zero, eye)
    out = np.zeros((rows, cols))
    for sample, col in outputs.items():
        if 2 * a <= sample < 2 * b:
            for lines, places in ((from_low, lows), (from_high, highs)):
                line = lines[sample - 2 * a]
                for i in np.nonzero(line)[0]:
                    out[places[a + int(i)], col] += scale * line[i]
    return out


def _pair(m):
    hi = m.astype(ml_dtypes.bfloat16)
    lo = (m - hi.astype(np.float64)).astype(ml_dtypes.bfloat16)
    return np.stack((hi, lo))


def _run(first, last, at):
    return {k: at + k - first for k in range(first, last)}


OWN_LOW0 = _run(2, 126, 2)
OWN_HIGH0 = _run(2, 126, 130)
RIM_LOW0 = {**_run(-10, 2, 0), **_run(126, 137, 12)}
RIM_HIGH0 = {**_run(-2, 2, 23), **_run(126, 130, 27)}
RIM_IN0 = {**_run(-32, 0, 0), **_run(0, 32, 128), **_run(224, 256, 256), **_run(256, 288, 384)}
OWN_LOW1 = _run(3, 61, 3)
OWN_HIGH1 = _run(2, 61, 66)
RIM_LOW1 = {**_run(-3, 3, 64), **_run(61, 67, 70)}
RIM_HIGH1 = {**_run(-3, 2, 80), **_run(61, 67, 85)}
IN1 = {**OWN_LOW0, **{k: 128 + v for k, v in RIM_LOW0.items()}}
IN2 = {
    **OWN_LOW1, **_run(67, 125, 67), **_run(-61, -3, 131), **{k: 128 + v for k, v in RIM_LOW1.items()}
}
LOW2 = _run(-28, 61, 0)
HIGH2 = _run(-3, 36, 89)
LOW3 = _run(-12, 29, 0)
HIGH3 = _run(-3, 20, 64)
LOW4 = _run(-4, 13, 0)
HIGH4 = _run(-3, 12, 32)
LOW5 = _run(-4, 8, 0)
HIGH5 = _run(-4, 8, 16)


def _part(places, first, last):
    return {k: places[k] for k in range(first, last)}


def _edges(width):
    far = 1 << 20
    return ((0, far), (-far, far), (-far, width))


def _bundle(parts, rows, cols):
    out = np.zeros((rows, cols))
    for r, c, m in parts:
        out[r : r + m.shape[0], c : c + m.shape[1]] = m
    return _pair(out)


@functools.cache
def _tables():
    fw, inv = _forward, _inverse
    far = 1 << 20
    out = {}
    out["own"] = _bundle(
        (
            (0, 0, fw(_run(0, 256, 0), OWN_LOW0, OWN_HIGH0, 256, 256, -far, far, 1.0)),
            (256, 0, fw(OWN_LOW0, OWN_LOW1, OWN_HIGH1, 128, 128, -far, far, KS)),
        ),
        384,
        256,
    )
    rim, back = [], []
    for v in range(3):
        a, b = zip(*(_edges(256 >> l)[v] for l in range(LEVELS)))
        t5 = fw(LOW4, _part(LOW5, 0, 5), _part(HIGH5, 0, 5), 128, 256, a[5], b[5], KS)
        lows, highs = t5[:, 4:8].copy(), t5[:, 20:24].copy()
        sixteen = np.concatenate([lows, highs[:, 1:], lows[:, 1:], highs[:, 1:], np.zeros((128, 3))], axis=1)
        t5[:, 128:] = np.tile(sixteen, (1, 8))
        one = fw(RIM_IN0, RIM_LOW0, RIM_HIGH0, 512, 128, a[0], b[0], 1.0)
        rim0 = sum(np.roll(one, (32 * g, 32 * g), (0, 1)) for g in range(4))
        rim.append(
            _bundle(
                (
                    (0, 0, fw(IN1, RIM_LOW1, RIM_HIGH1, 256, 128, a[1], b[1], KS)),
                    (0, 128, fw(IN2, LOW2, HIGH2, 256, 128, a[2], b[2], KS)),
                    (0, 256, fw(LOW2, LOW3, HIGH3, 128, 128, a[3], b[3], KS)),
                    (128, 256, fw(LOW3, LOW4, HIGH4, 128, 128, a[4], b[4], KS)),
                    (256, 0, t5),
                    (384, 0, rim0),
                ),
                896,
                384,
            )
        )
        low0 = {**OWN_LOW0, **{k: 256 + v for k, v in RIM_LOW0.items() if -2 <= k < 130}}
        high0 = {**OWN_HIGH0, **{k: 256 + v for k, v in RIM_HIGH0.items()}}
        low1 = {**OWN_LOW1, **{k: 128 + v for k, v in RIM_LOW1.items()}}
        high1 = {**OWN_HIGH1, **{k: 128 + v for k, v in RIM_HIGH1.items()}}
        full = inv(low0, high0, _run(0, 256, 0), 288, 256, a[0], b[0], 1.0)
        ends = np.zeros((128, 128))
        for i in range(32):
            for c in range(-7, 8):
                ends[i, c % 128] = full[256 + i, c % 256]
        ends = sum(np.roll(ends, (32 * g, 32 * g), (0, 1)) for g in range(4))
        s1 = inv(low1, high1, _part(IN1, -1, 130), 256, 256, a[1], b[1], 1.0 / KS)
        s1[:, 128:] = np.tile(s1[:, 128:160], (1, 4))
        back.append(
            _bundle(
                (
                    (0, 0, full[:256]),
                    (256, 0, s1),
                    (512, 0, inv(LOW2, HIGH2, _part(low1, -2, 67), 128, 256, a[2], b[2], 1.0 / KS)),
                    (640, 0, inv(LOW3, HIGH3, _part(LOW2, -2, 36), 128, 128, a[3], b[3], 1.0 / KS)),
                    (640, 128, inv(LOW4, HIGH4, _part(LOW3, -2, 20), 128, 128, a[4], b[4], 1.0 / KS)),
                    (768, 0, inv(LOW5, HIGH5, _part(LOW4, -2, 12), 128, 128, a[5], b[5], 1.0 / KS)),
                    (768, 128, ends),
                ),
                896,
                256,
            )
        )
    out["rim"], out["back"] = np.stack(rim), np.stack(back)
    n = S >> LEVELS
    bands = []
    current = np.eye(n)
    for _ in range(COARSE):
        current, high = _lift(current)
        bands.append(high)
    coarse = np.concatenate([current] + bands[::-1])
    order = (np.arange(n) % NT) * 4 + np.arange(n) // NT
    last = n >> COARSE
    current = np.eye(n)[:last]
    for step in range(COARSE):
        size = last << step
        current = _unlift(current, np.eye(n)[size : 2 * size])
    both = np.zeros((n + 640, n))
    both[:n] = (KS * coarse.T)[order]
    both[n + 4 : 2 * n + 4] = current / KS
    out["coarse"] = _pair(both)
    return out


def _mask(lane, places, first, last, base=0):
    lanes = sorted(v - base for k, v in places.items() if first <= k < last)
    out, i = None, 0
    while i < len(lanes):
        j = i
        while j + 1 < len(lanes) and lanes[j + 1] == lanes[j] + 1:
            j += 1
        hit = (lane >= lanes[i]) & (lane <= lanes[j])
        out = hit if out is None else out | hit
        i = j + 1
    return out


def _ones(hit):
    return jnp.where(hit, 1.0, 0.0)


def _dot3(x, t):
    hi = x.astype(BF16)
    lo = (x - hi.astype(F32)).astype(BF16)
    d = functools.partial(jnp.dot, preferred_element_type=F32)
    both = d(jnp.concatenate([hi, lo], axis=0), t(0))
    return both[: x.shape[0]] + both[x.shape[0] :] + d(hi, t(1))


def _time(load, t, y, step, j):
    x = load(j, step)
    y[pl.ds(j, step)] = _dot3(x.reshape(step * 8, x.shape[2]), t).reshape(step, 8, y.shape[2])


class _Forward:
    def __init__(self, load, t, y, step):
        self.load, self.t, self.y, self.step, self.done = load, t, y, step, 0

    def __call__(self, j):
        ahead = min(j + self.step, self.y.shape[0] - 1)
        while self.done <= ahead:
            _time(self.load, self.t, self.y, self.step, self.done)
            self.done += self.step
        return self.y[j]


class _Backward:
    def __init__(self, y, t, store, step):
        self.y, self.t, self.store, self.step, self.left = y, t, store, step, {}

    def __call__(self, j, value):
        self.y[j] = value
        chunk = j // self.step
        self.left[chunk] = self.left.get(chunk, self.step) - 1
        if not self.left[chunk]:
            x = self.y[pl.ds(chunk * self.step, self.step)]
            out = _dot3(x.reshape(self.step * 8, x.shape[2]), self.t)
            self.store(chunk * self.step, self.step, out.reshape(self.step, 8, out.shape[1]))


def _table(ref, rows, cols, *lead):
    r, c = pl.ds(*rows), pl.ds(*cols)
    return lambda i: ref[(*lead, i, r, c)]


def _sublane(lanes):
    return lax.broadcasted_iota(jnp.int32, (8, lanes), 0)


def _lane(rows=8):
    return lax.broadcasted_iota(jnp.int32, (rows, 128), 1)


def _wide(v, lanes):
    return v if lanes == 128 else jnp.concatenate([v] * (lanes // 128), axis=1)


class _QuarterWrap:
    def __init__(self):
        self.sub, self.group = _sublane(128), _lane() // 32

    def after(self, first, last):
        moved = pltpu.roll(first, 96, 1)
        moved = jnp.where(self.group == 3, pltpu.roll(moved, 7, 0), moved)
        return jnp.where((self.group == 3) & (self.sub == 7), last, moved)

    def before(self, last, first):
        moved = pltpu.roll(last, 32, 1)
        moved = jnp.where(self.group == 0, pltpu.roll(moved, 1, 0), moved)
        return jnp.where((self.group == 0) & (self.sub == 0), first, moved)


def _quarters(values):
    group = _lane() // 32
    out = []
    for c in range(3):
        v = values[0]
        for g in range(1, 4):
            v = jnp.where(group == g, values[(24 * g + 8 * c) // 32], v)
        out.append(v)
    return out


class _Wrap:
    def __init__(self, lanes):
        sub = _sublane(lanes)
        self.last, self.first = sub == 7, sub == 0

    def after(self, first, last):
        return jnp.where(self.last, last, pltpu.roll(first, 7, 0))

    def before(self, last, first):
        return jnp.where(self.first, first, pltpu.roll(last, 1, 0))


def _coefs(weights, lanes):
    return [[_wide(c * v, lanes) for v in weights] for c in (A1, B1, A2, B2)]


def _chan_forward(get, n, weights, lanes, put_low, put_high, wrap=None):
    wrap = wrap or _Wrap(lanes)
    ca, cb, cc, cd = _coefs(weights, lanes)
    per = n // 3
    first = get(0)
    e, o1, e1, o2 = {0: first}, {}, {}, {}

    def high(k, v):
        o2[k] = v
        put_high(k, k // per, v)

    def low(k):
        put_low(k, k // per, e1[k] + cd[k // per] * (o2[k - 1] + o2[k]))

    for k in range(n):
        q = k // per
        e[k + 1] = get(2 * k + 2) if k + 1 < n else wrap.after(first, e[k])
        o1[k] = get(2 * k + 1) + ca[q] * (e[k] + e[k + 1])
        if k >= 1:
            e1[k] = e[k] + cb[q] * (o1[k - 1] + o1[k])
        if k >= 2:
            high(k - 1, o1[k - 1] + cc[(k - 1) // per] * (e1[k - 1] + e1[k]))
        if k >= 3:
            low(k - 1)
    e1[0] = first + cb[0] * (wrap.before(o1[n - 1], o1[0]) + o1[0])
    high(0, o1[0] + cc[0] * (e1[0] + e1[1]))
    high(n - 1, o1[n - 1] + cc[2] * (e1[n - 1] + wrap.after(e1[0], e1[n - 1])))
    o2[-1] = wrap.before(o2[n - 1], o2[0])
    for k in (0, 1, n - 1):
        low(k)


def _chan_inverse(get_low, get_high, n, weights, lanes, put, wrap=None):
    wrap = wrap or _Wrap(lanes)
    ca, cb, cc, cd = _coefs(weights, lanes)
    per = n // 3
    o = {0: get_high(0)}
    o[-1] = wrap.before(get_high(n - 1), o[0])
    e1, o1, e2 = {}, {}, {}

    def even(k):
        e2[k] = e1[k] - cb[k // per] * (o1[k - 1] + o1[k])
        put(2 * k, e2[k])

    def odd(k):
        put(2 * k + 1, o1[k] - ca[k // per] * (e2[k] + e2[k + 1]))

    for k in range(n):
        q = k // per
        if k:
            o[k] = get_high(k)
        e1[k] = get_low(k) - cd[q] * (o[k - 1] + o[k])
        if k >= 1:
            o1[k - 1] = o[k - 1] - cc[(k - 1) // per] * (e1[k - 1] + e1[k])
        if k >= 2:
            even(k - 1)
        if k >= 3:
            odd(k - 2)
    o1[n - 1] = o[n - 1] - cc[2] * (e1[n - 1] + wrap.after(e1[0], e1[n - 1]))
    o1[-1] = wrap.before(o1[n - 1], o1[0])
    even(n - 1)
    if n > 2:
        odd(n - 2)
    even(0)
    odd(0)
    e2[n] = wrap.after(e2[0], e2[n - 1])
    odd(n - 1)


class _Squares:
    def __init__(self):
        self.acc = {}

    def add(self, key, v):
        self.acc[key] = v * v if key not in self.acc else self.acc[key] + v * v

    def total(self, rows, tiles):
        out = None
        for q in range(3):
            part = None
            for (band, tile), lanes in tiles.items():
                v = self.acc[(band, tile, q)] * (KS * KS if band == "low" else 1.0 / (KS * KS))
                v = v if lanes is None else v * lanes
                part = v if part is None else part + v
            part = part * rows[q]
            out = part if out is None else out + part
        return out


def _tile(v, i):
    return v[:, 128 * i : 128 * (i + 1)]


def _blocks(w, level):
    return [w[level, q] for q in range(3)]


def _own_rows(core):
    block = 3 * _sublane(128)
    return [
        jnp.where(core == 0, _ones(block + q < 16), _ones(block + q >= 8)) for q in range(3)
    ]


def _load_kernel(
    sc, x_all, gauge_table_all, gauge_index_all, own_all, rim_all,
    low, high, ends, own_table, rim_table, w,
    x, gauge_table, gauge_index, sems,
):
    core = sc[0]
    copies = [
        pltpu.make_async_copy(src, dst, sems.at[i])
        for i, (src, dst) in enumerate(
            (
                (gauge_index_all, gauge_index),
                (gauge_table_all, gauge_table),
                (own_all, own_table),
                *((x_all.at[pl.ds(256 * i, 256)], x.at[pl.ds(256 * i, 256)]) for i in range(4)),
                (rim_all.at[sc[1]], rim_table),
            )
        )
    ]
    for c in copies:
        c.start()
    for c in copies[:2]:
        c.wait()
    index = gauge_index[...]
    table_rows = gauge_table[...]
    weights = jnp.zeros(index.shape, F32)
    for g in range(GTAB):
        weights = weights + jnp.where(index == g, table_rows[:, g : g + 1], 0.0)
    block = lax.broadcasted_iota(jnp.int32, (8, NBLK), 1) - 3 * lax.broadcasted_iota(jnp.int32, (8, NBLK), 0)
    block = block - 8 * core
    for l in range(LEVELS):
        for q in range(3):
            hit = jnp.where(block == q, weights[l : l + 1], 0.0)
            w[l, q] = jnp.broadcast_to(jnp.sum(hit, axis=1, keepdims=True), (8, 128))
    copies[2].wait()
    for i in range(4):
        copies[3 + i].wait()
        _first(x, own_table, low, high, ends, 0, range(256 * i, 256 * i + 256, 128))
    copies[7].wait()


def _first(x, table, low, high, ends, at, blocks):
    lane = _lane(128)
    for r in blocks:
        v = x[pl.ds(r, 128), :]
        y = _dot3(v, _table(table, (0, 256), (0, 256)))
        rows = pl.ds(at + r, 128)
        low[rows, :] = y[:, 0:128]
        high[rows, :] = y[:, 128:256]
        ends[rows, :] = jnp.where(lane < 32, v[:, 0:128], v[:, 128:256])


def _own_kernel(
    sc, recv, own_low, own_high, own_ends, table, w,
    right, left, low0, a1l, fh, details, sums,
    fl, fe, y1,
):
    core = sc[0]
    at_own = pl.multiple_of(core * HALO, 8)
    at_recv = pl.multiple_of((1 - core) * OWN, 8)
    for src, dst in ((own_low, fl), (own_high, fh), (own_ends, fe)):
        for r in range(0, OWN, 128):
            dst[pl.ds(at_own + r, 128), :] = src[pl.ds(r, 128), :]
    theirs = recv.at[pl.ds(at_own, HALO)]
    _first(theirs, table, fl, fh, fe, at_recv, range(0, HALO, 128))
    lane = _lane()
    group = lane // 32
    for i in range(48):
        to_right, to_left = None, None
        for g in range(4):
            j = 48 * g + i
            v = fe[pl.ds(j, 8, stride=SEG), :]
            a = pltpu.roll(v, 32 * g, 1) if g else v
            b = pltpu.roll(v, (32 * g + 32) % 128, 1) if g != 3 else v
            to_left = a if to_left is None else jnp.where(group == g, a, to_left)
            to_right = b if to_right is None else jnp.where(group == g, b, to_right)
        right[i] = to_right
        left[i] = to_left
    rows = _own_rows(core)
    sq = _Squares()

    def put_low(k, q, v):
        low0[k] = v

    def put_high(k, q, v):
        details[k] = v
        sq.add(("high", 0, q), v)

    _chan_forward(lambda j: fl[pl.ds(j, 8, stride=SEG), :], 96, _blocks(w, 0), 128, put_low, put_high)
    sums[0] = sq.total(rows, {("high", 0): None})
    sq1 = _Squares()

    def put_low1(k, q, v):
        a1l[k] = v
        details[96 + k] = v
        sq1.add(("low", 0, q), v)
        if k >= 26:
            packed = jnp.where(lane < 64, a1l[k - 24], pltpu.roll(v, 64, 1))
            right[24 + k] = packed
            left[24 + k] = packed

    def put_high1(k, q, v):
        details[144 + k] = v
        sq1.add(("high", 0, q), v)

    get = _Forward(lambda j, n: low0[pl.ds(j, n)], _table(table, (256, 128), (0, 128)), y1, 24)
    _chan_forward(get, 48, _blocks(w, 1), 128, put_low1, put_high1)
    for k in (24, 25):
        packed = jnp.where(lane < 64, a1l[k - 24], pltpu.roll(a1l[k], 64, 1))
        right[24 + k] = packed
        left[24 + k] = packed
    sums[1] = sq1.total(rows, {("low", 0): _ones(_mask(lane, OWN_HIGH1, 0, 64)), ("high", 0): None})


def _bands(details):
    out, at = [], 0
    for n in (24, 48, 24, 12, 6, 3):
        out += [details.at[pl.ds(at, n)], details.at[pl.ds(at + n, n)]]
        at += 2 * n
    return out


def _aside_kernel(sc, fh, w, back_all, coarse_all, back_table, coarse_table, details, sums, sems):
    copies = []
    for src, dst, parts in ((back_all.at[sc[1]], back_table, 4), (coarse_all, coarse_table, 4)):
        n = dst.shape[1] // parts
        for i in range(2):
            for k in range(parts):
                rows = pl.ds(n * k, n)
                copies.append(pltpu.make_async_copy(src.at[i, rows], dst.at[i, rows], sems.at[len(copies)]))
    for c in copies:
        c.start()
    rows = _own_rows(sc[0])
    sq = _Squares()

    def put_low(k, q, v):
        details[k] = v
        sq.add(("low", 0, q), v)

    def put_high(k, q, v):
        details[96 + k] = v
        sq.add(("high", 0, q), v)

    _chan_forward(lambda j: fh[pl.ds(j, 8, stride=SEG), :], 96, _blocks(w, 0), 128, put_low, put_high)
    sums[...] = sq.total(rows, {("low", 0): None, ("high", 0): None})
    for c in copies:
        c.wait()


def _rim_kernel(
    sc, right, left, from_left, from_right, low0, a1l, own_sums, more_sums, table, w,
    details, payload,
    rim, y0, y1, x2, y2, y3, y4, y5, l5, h5, flat,
):
    core = sc[0]
    rlow0, rhigh0, r1l, r1h, a2l, a2h, a3l, a3h, a4l, a4h, a5l, a5h = _bands(details)
    lane = _lane()
    rows = _own_rows(core)
    totals = []

    def level(l, load, n, t, y, step, lanes, low, high, own_low, own_high, pairs):
        quarters = l == 0
        weights = _blocks(w, l)
        place = lane % 32 if quarters else lane
        sq = _Squares()

        def put_low(k, q, value):
            low[k] = value
            sq.add(("low", 0, q), _tile(value, 0))

        def put_high(k, q, value):
            high[k] = value
            sq.add(("high", 0, q), _tile(value, 0))

        wrap = _QuarterWrap() if quarters else None
        weights = _quarters(weights) if quarters else weights
        _chan_forward(_Forward(load, t, y, step), n, weights, lanes, put_low, put_high, wrap)
        is_high = _mask(place, own_high, 0, pairs)
        is_low = _mask(place, own_low, 0, pairs)
        total = sq.total(_quarters(rows) if quarters else rows, {("low", 0): _ones(is_high), ("high", 0): _ones(is_high | is_low)})
        totals.append(total + own_sums[l] if l < 2 else total)

    def pick(r, k, c, n):
        return _table(table, (r, k), (c, n))

    def load0(j, n):
        at = pl.ds(j, n)
        return jnp.concatenate([from_left[at], left[at], right[at], from_right[at]], axis=2)

    level(0, load0, 24, pick(384, 512, 0, 128), y0, 24, 128, rlow0, rhigh0, RIM_LOW0, RIM_HIGH0, 128)
    totals[0] = totals[0] + more_sums[...]
    for g in range(4):
        for i in range(24):
            rim[24 * g + i] = pltpu.roll(rlow0[i], 128 - 32 * g, 1) if g else rlow0[i]

    def load1(j, n):
        return jnp.concatenate([low0[pl.ds(j, n)], rim[pl.ds(j, n)]], axis=2)

    level(1, load1, 48, pick(0, 256, 0, 128), y1, 24, 128, r1l, r1h, RIM_LOW1, RIM_HIGH1, 64)
    for j in range(48):
        h, i = j // 24, 48 + j % 24
        b, a = from_left[i], from_right[i]
        if h == 0:
            a = pltpu.roll(a, 64, 1)
        else:
            b = pltpu.roll(b, 64, 1)
        x2[j, :, 0:128] = jnp.where(lane < 64, a1l[j], a)
        x2[j, :, 128:256] = jnp.where(lane < 64, b, r1l[j])
    level(2, lambda j, n: x2[pl.ds(j, n)], 24, pick(0, 256, 128, 128), y2, 24, 128, a2l, a2h, LOW2, HIGH2, 32)
    level(3, lambda j, n: a2l[pl.ds(j, n)], 12, pick(0, 128, 256, 128), y3, 24, 128, a3l, a3h, LOW3, HIGH3, 16)
    level(4, lambda j, n: a3l[pl.ds(j, n)], 6, pick(128, 128, 256, 128), y4, 12, 128, a4l, a4h, LOW4, HIGH4, 8)
    level(5, lambda j, n: a4l[pl.ds(j, n)], 3, pick(256, 128, 0, 256), y5, 6, 256, l5, h5, LOW5, HIGH5, 4)
    sub = _sublane(128)
    for j in range(3):
        a5l[j] = l5[j, :, 0:128]
        a5h[j] = h5[j, :, 0:128]
        flat[pl.ds(j, 8, stride=3), :] = jnp.where(lane % 16 < 7, l5[j, :, 128:256], h5[j, :, 128:256])
    sums = jnp.zeros((8, 128), F32)
    for l in range(LEVELS):
        sums = jnp.where(sub == l, jnp.sum(totals[l], axis=0, keepdims=True), sums)
    sums = jnp.where((lane == 16 * sub + 13) & (sub < LEVELS), jnp.sum(sums, axis=1, keepdims=True), 0.0)
    lines = []
    for h in range(2):
        mine = flat[pl.ds(pl.multiple_of(8 * core + 8 * h, 8), 8), :]
        mine = jnp.where(lane // 16 == sub, mine, 0.0)
        lines.append(jnp.sum(mine + sums if h == 0 else mine, axis=0, keepdims=True))
    block = jnp.where(sub % 2 == 0, lines[0], lines[1])
    for i in range(32):
        payload[pl.ds(8 * i, 8), :] = block


def _shrink(v, limit):
    return v - jnp.minimum(jnp.maximum(v, -limit), limit)


def _back_kernel(
    sc, mine, theirs, coarse_table, table, own_details, more_details, rim_details, w,
    out,
    gt, nears, cur, x5l, x5h, y5, y4, y3, y2, y1, c4, c3, c2, c1, c0, f0, f1, f2, yr, stage, sems,
):
    core, place = sc[0], sc[2]
    rlow0, rhigh0, r1l, r1h, a2l, a2h, a3l, a3h, a4l, a4h, a5l, a5h = _bands(rim_details)
    dhigh0, dlow0, dhigh1 = own_details.at[pl.ds(0, 96)], more_details.at[pl.ds(0, 96)], more_details.at[pl.ds(96, 96)]
    a1l, a1h = (own_details.at[pl.ds(96 + 48 * i, 48)] for i in range(2))
    lane = _lane()
    lane1 = _lane(1)
    sub = _sublane(128)
    for h in range(2):
        halves = [g[pl.ds(h, NT, stride=2), :] for g in (mine, theirs)]
        if h == 0:
            total = jnp.sum(halves[0] + halves[1], axis=0, keepdims=True)
        for c in range(2):
            gt[c, h] = jnp.transpose(jnp.where(core == c, halves[0], halves[1]))
    limits = []
    for l in range(LEVELS):
        entries = 3 * (C >> (l + 1)) * (S >> (l + 1))
        s = jnp.sum(jnp.where(lane1 == 16 * l + 13, total, 0.0), axis=1, keepdims=True)
        limits.append(jnp.sqrt(s * (1.0 / entries) + FLOOR))
    rows = [
        jnp.concatenate([gt[c, h, pl.ds(m, 8, stride=16), :] for m in range(4)], axis=1)
        for c in range(2)
        for h in range(2)
    ]
    coarse = _dot3(jnp.concatenate(rows, axis=0), lambda i: coarse_table[i, 0:512, :])
    highs = lax.broadcasted_iota(jnp.int32, (32, 512), 1) >= (S >> (LEVELS + COARSE))
    square = jnp.sum(jnp.where(highs, coarse * coarse, 0.0), axis=0, keepdims=True)
    square = jnp.sum(square, axis=1, keepdims=True)
    entries = (C >> LEVELS) * ((S >> LEVELS) - (S >> (LEVELS + COARSE)))
    limit = jnp.sqrt(square * (1.0 / entries) + FLOOR)
    coarse = jnp.where(highs, _shrink(coarse, limit), coarse)
    hi = coarse.astype(BF16)
    lo = (coarse - hi.astype(F32)).astype(BF16)
    for side, other in enumerate((jnp.maximum(place - 1, 0), jnp.minimum(place + 1, NT - 1))):
        for c in range(2):
            for h in range(2):
                row = pl.ds(2 * other + h, 1)
                line = jnp.broadcast_to(jnp.where(core == c, mine[row, :], theirs[row, :]), (8, 128))
                near = line
                for k in range(1, 8):
                    near = jnp.where(sub == k, pltpu.roll(line, 128 - 16 * k, 1), near)
                nears[side, pl.ds(16 * c + 8 * h, 8), :] = near
    for k in range(3):
        rows = pl.ds(8 * core + k, 8, stride=3)
        before, after = nears[0, rows, :], nears[1, rows, :]
        v = a5h[k]
        for at, near, shift in ((1, before, 122), (9, after, 2), (17, before, 7), (25, after, 15)):
            v = jnp.where((lane >= at) & (lane < at + 3), pltpu.roll(near, shift, 1), v)
        x5h[k] = v
        v = a5l[k]
        for at, near, shift in ((17, before, 13), (25, after, 21)):
            v = jnp.where((lane >= at) & (lane < at + 3), pltpu.roll(near, shift, 1), v)
        x5l[k] = v

    def nt(a, b):
        return lax.dot_general(a, b, (((1,), (1,)), ((), ())), preferred_element_type=F32)

    rows = pl.ds(pl.multiple_of(512 + 16 * (place // 4), 16), 128)
    current = nt(hi, coarse_table[0, rows, :]) + nt(lo, coarse_table[0, rows, :]) + nt(hi, coarse_table[1, rows, :])
    cur[...] = pltpu.roll(current, (128 - 4 * (place % 4)) % 128, 1)

    def level(l, get_current, low, high, n, y, t, nxt, step, needed):
        tl = jnp.broadcast_to(limits[l] * (1.0 / KS), (8, 128))
        th = jnp.broadcast_to(limits[l] * KS, (8, 128))
        is_low = needed(lane)

        def get_low(k):
            return jnp.where(is_low, get_current(k), _shrink(low[k], tl))

        def store(j, m, value):
            nxt[pl.ds(j, m)] = value

        put = _Backward(y, t, store, step)
        _chan_inverse(get_low, lambda k: _shrink(high[k], th), n, _blocks(w, l), 128, put)

    def pick(r, k, c, n):
        return _table(table, (r, k), (c, n))

    level(
        5, lambda k: cur[pl.ds(8 * core + k, 8, stride=3), :], x5l, x5h, 3, y5, pick(768, 128, 0, 128), c4, 6, lambda i: i < 12
    )
    level(4, lambda k: c4[k], a4l, a4h, 6, y4, pick(640, 128, 128, 128), c3, 12, lambda i: i < 32)
    level(3, lambda k: c3[k], a3l, a3h, 12, y3, pick(640, 128, 0, 128), c2, 24, lambda i: i < 64)
    level(2, lambda k: c2[k], a2l, a2h, 24, y2, pick(512, 128, 0, 256), c1, 24, lambda i: i < 89)
    tl = jnp.broadcast_to(limits[1] * (1.0 / KS), (8, 256))
    th = jnp.broadcast_to(limits[1] * KS, (8, 256))
    lane2 = lax.broadcasted_iota(jnp.int32, (8, 256), 1)
    is_low1 = (lane2 < 64) | ((lane2 >= 192) & (lane2 < 208))

    def get_low1(k):
        v1 = jnp.concatenate([a1l[k], r1l[k]], axis=1)
        return jnp.where(is_low1, c1[k], _shrink(v1, tl))

    def get_high1(k):
        return _shrink(jnp.concatenate([a1h[k], r1h[k]], axis=1), th)

    def store1(j, m, value):
        c0[pl.ds(j, m)] = value

    put1 = _Backward(y1, pick(256, 256, 0, 256), store1, 24)
    _chan_inverse(get_low1, get_high1, 48, _blocks(w, 1), 256, put1)
    tl0 = jnp.broadcast_to(limits[0] * (1.0 / KS), (8, 128))
    th0 = jnp.broadcast_to(limits[0] * KS, (8, 256))
    group = lane // 32
    rim_low = lane % 32 < 23

    def get_low_rim(k):
        now = c0[k, :, 128:256]
        for q in range(1, 4):
            now = jnp.where(group == q, c0[24 * q + k, :, 128:256], now)
        return jnp.where(rim_low, now, _shrink(rlow0[k], tl0))

    def store_rim(j, m, value):
        for i in range(m):
            for q in range(4):
                v = pltpu.roll(value[i], 128 - 32 * q, 1) if q else value[i]
                f2[pl.ds(48 * q + j + i, 8, stride=SEG), :] = v

    put_rim = _Backward(yr, pick(768, 128, 128, 128), store_rim, 24)
    _chan_inverse(
        get_low_rim, lambda k: _shrink(rhigh0[k], th0[:, 0:128]), 24, _quarters(_blocks(w, 0)), 128, put_rim, _QuarterWrap()
    )

    def get_low0(k):
        return jnp.concatenate([c0[k, :, 0:128], _shrink(dlow0[k], tl0)], axis=1)

    def get_high0(k):
        return _shrink(jnp.concatenate([dhigh0[k], dhigh1[k]], axis=1), th0)

    def put0(j, value):
        for i, buf in enumerate((f0, f1)):
            buf[pl.ds(j, 8, stride=SEG), :] = _tile(value, i)

    _chan_inverse(get_low0, get_high0, 96, _blocks(w, 0), 256, put0)
    at_own = pl.multiple_of(core * HALO, 8)
    t = pick(0, 256, 0, 256)
    wide = _lane(128)
    copies = []
    for r in range(0, OWN, 128):
        rows = pl.ds(at_own + r, 128)
        done = pl.ds(r, 128)
        ends = f2[rows, :]
        v = _dot3(jnp.concatenate([f0[rows, :], f1[rows, :]], axis=1), t)
        stage[done, 0:128] = _tile(v, 0) + jnp.where(wide < 8, ends, 0.0)
        stage[done, 128:256] = _tile(v, 1) + jnp.where(wide >= 121, ends, 0.0)
        copies.append(pltpu.make_async_copy(stage.at[done], out.at[done], sems.at[r // 128]))
        copies[-1].start()
    for c in copies:
        c.wait()


VM = pl.BlockSpec(memory_space=pltpu.VMEM)
SM = pl.BlockSpec(memory_space=pltpu.SMEM)
ANY = pl.BlockSpec(memory_space=pl.ANY)
HBM = pl.BlockSpec(memory_space=pltpu.HBM)


def _call(kernel, name, limit, args, specs, outs, out_specs, scratch):
    args = [
        pltpu.with_memory_space_constraint(x, pltpu.HBM) if spec is HBM else x for x, spec in zip(args, specs)
    ]
    outs = [jax.ShapeDtypeStruct(s, F32) if isinstance(s, tuple) else s for s in outs]
    return pl.pallas_call(
        kernel,
        out_shape=[pltpu.HBM(s.shape, s.dtype) if spec is HBM else s for s, spec in zip(outs, out_specs)],
        in_specs=specs,
        out_specs=out_specs,
        scratch_shapes=[pltpu.VMEM(s, F32) if isinstance(s, tuple) else s for s in scratch],
        compiler_params=pltpu.CompilerParams(vmem_limit_bytes=limit << 20),
        name=name,
    )(*args)


def _shift(v, by):
    return lax.ppermute(v, "tm", [(i, i + by) for i in range(NT) if 0 <= i + by < NT])


def shards(record, gauge_table, gauge_index):
    tables = _tables()
    core = lax.axis_index("chan")
    place = lax.axis_index("tm")
    variant = jnp.where(place == 0, 0, jnp.where(place == NT - 1, 2, 1))
    sc = jnp.stack([core, variant, place]).astype(jnp.int32)
    dma = pltpu.SemaphoreType.DMA
    recv = lax.ppermute(record, "chan", [(0, 1), (1, 0)])
    low, high, ends, own_table, rim_table, w = _call(
        _load_kernel, "load", 12, (sc, record, gauge_table, gauge_index, tables["own"], tables["rim"]),
        [SM] + [HBM] * 5,
        [(OWN, 128), (OWN, 128), (OWN, 128), jax.ShapeDtypeStruct((2, 384, 256), BF16),
         jax.ShapeDtypeStruct((2, 896, 384), BF16), (LEVELS, 3, 8, 128)],
        [VM] * 6,
        [(OWN, 256), (LEVELS, GTAB), pltpu.VMEM((LEVELS, NBLK), jnp.int32), dma((8,))],
    )
    right, left, low0, a1l, fh, own_details, sums = _call(
        _own_kernel, "own", 12, (sc, recv, low, high, ends, own_table, w), [SM] + [VM] * 6,
        [(72, 8, 128), (72, 8, 128), (96, 8, 128), (48, 8, 128), (8 * SEG, 128), (192, 8, 128), (2, 8, 128)],
        [VM] * 7,
        [(8 * SEG, 128), (8 * SEG, 128), (96, 8, 128)],
    )
    from_left, from_right = _shift(right, 1), _shift(left, -1)
    back_table, coarse_table, more_details, more_sums = _call(
        _aside_kernel, "aside", 6, (sc, fh, w, tables["back"], tables["coarse"]), [SM, VM, VM, HBM, HBM],
        [jax.ShapeDtypeStruct((2, 896, 256), BF16), jax.ShapeDtypeStruct((2, 1152, 512), BF16), (192, 8, 128), (8, 128)],
        [VM] * 4,
        [dma((16,))],
    )
    rim_details, payload = _call(
        _rim_kernel, "rim", 16,
        (sc, right, left, from_left, from_right, low0, a1l, sums, more_sums, rim_table, w), [SM] + [VM] * 10,
        [(234, 8, 128), (256, 128)], [VM] * 2,
        [(96, 8, 128), (48, 8, 128), (96, 8, 128), (48, 8, 256), (48, 8, 128), (24, 8, 128), (12, 8, 128),
         (6, 8, 256), (3, 8, 256), (3, 8, 256), (24, 128)],
    )
    mine = lax.all_to_all(payload, "tm", split_axis=0, concat_axis=0, tiled=True)
    theirs = lax.ppermute(mine, "chan", [(0, 1), (1, 0)])
    (out,) = _call(
        _back_kernel, "back", 24, (sc, mine, theirs, coarse_table, back_table, own_details, more_details, rim_details, w),
        [SM] + [VM] * 8, [(OWN, 256)], [HBM],
        [
            (2, 2, 128, 128), (2, 32, 128), (32, 128), (3, 8, 128), (3, 8, 128),
            (6, 8, 128), (12, 8, 128), (24, 8, 128), (48, 8, 128), (96, 8, 256),
            (6, 8, 128), (12, 8, 128), (24, 8, 128), (48, 8, 256), (96, 8, 256),
            (8 * SEG, 128), (8 * SEG, 128), (8 * SEG, 128), (48, 8, 128), (OWN, 256), dma((8,)),
        ],
    )
    return out


def solution(mesh):
    return jax.shard_map(
        shards,
        mesh=mesh,
        in_specs=(P("chan", "tm"), P(), P()),
        out_specs=P("chan", "tm"),
        check_vma=False,
    )
```

```python
import functools

import jax
import jax.numpy as jnp
import ml_dtypes
import numpy as np
from jax import lax
from jax.experimental import pallas as pl
from jax.experimental.pallas import tpu as pltpu
from jax.sharding import PartitionSpec as P

LEVELS = 6
COARSE = 6
GTAB = 8
NBLK = 32
C = 2048
S = 32768
NT = 128
OWN = 1024
HALO = 512
SEG = 192
A1 = -1.586134342059924
B1 = -0.052980118572961
A2 = 0.882911075530934
B2 = 0.443506852043971
KS = 1.149604398860241
FLOOR = 1e-06
F32 = jnp.float32
BF16 = jnp.bfloat16


def _next(e):
    return np.concatenate((e[1:], e[-1:]))


def _prev(o):
    return np.concatenate((o[:1], o[:-1]))


def _lift(x):
    e, o = x[0::2], x[1::2]
    o = o + A1 * (e + _next(e))
    e = e + B1 * (_prev(o) + o)
    o = o + A2 * (e + _next(e))
    e = e + B2 * (_prev(o) + o)
    return KS * e, o / KS


def _unlift(low, high):
    e, o = low / KS, high * KS
    e = e - B2 * (_prev(o) + o)
    o = o - A2 * (e + _next(e))
    e = e - B1 * (_prev(o) + o)
    o = o - A1 * (e + _next(e))
    return np.stack((e, o), axis=1).reshape((2 * e.shape[0],) + e.shape[1:])


def _forward(inputs, lows, highs, rows, cols, start, stop, scale):
    pairs = list(lows) + list(highs)
    a = max(2 * min(pairs) - 16, start)
    b = min(2 * max(pairs) + 16, stop)
    low, high = _lift(np.eye(b - a))
    out = np.zeros((rows, cols))
    for band, places in ((low, lows), (high, highs)):
        for pair, col in places.items():
            if a <= 2 * pair < b:
                line = band[pair - a // 2]
                for i in np.nonzero(line)[0]:
                    out[inputs[a + int(i)], col] += scale * line[i]
    return out


def _inverse(lows, highs, outputs, rows, cols, start, stop, scale):
    a = max(2 * (min(outputs) // 2) - 16, start) // 2
    b = min(2 * (max(outputs) // 2) + 18, stop) // 2
    n = b - a
    eye, zero = np.eye(n), np.zeros((n, n))
    from_low, from_high = _unlift(eye, zero), _unlift(zero, eye)
    out = np.zeros((rows, cols))
    for sample, col in outputs.items():
        if 2 * a <= sample < 2 * b:
            for lines, places in ((from_low, lows), (from_high, highs)):
                line = lines[sample - 2 * a]
                for i in np.nonzero(line)[0]:
                    out[places[a + int(i)], col] += scale * line[i]
    return out


def _pair(m):
    hi = m.astype(ml_dtypes.bfloat16)
    lo = (m - hi.astype(np.float64)).astype(ml_dtypes.bfloat16)
    return np.stack((hi, lo))


def _run(first, last, at):
    return {k: at + k - first for k in range(first, last)}


OWN_LOW0 = _run(2, 126, 2)
OWN_HIGH0 = _run(2, 126, 130)
RIM_LOW0 = {**_run(-10, 2, 0), **_run(126, 137, 12)}
RIM_HIGH0 = {**_run(-2, 2, 23), **_run(126, 130, 27)}
RIM_IN0 = {**_run(-32, 0, 0), **_run(0, 32, 128), **_run(224, 256, 256), **_run(256, 288, 384)}
OWN_LOW1 = _run(3, 61, 3)
OWN_HIGH1 = _run(2, 61, 66)
RIM_LOW1 = {**_run(-3, 3, 64), **_run(61, 67, 70)}
RIM_HIGH1 = {**_run(-3, 2, 80), **_run(61, 67, 85)}
IN1 = {**OWN_LOW0, **{k: 128 + v for k, v in RIM_LOW0.items()}}
IN2 = {
    **OWN_LOW1, **_run(67, 125, 67), **_run(-61, -3, 131), **{k: 128 + v for k, v in RIM_LOW1.items()}
}
LOW2 = _run(-28, 61, 0)
HIGH2 = _run(-3, 36, 89)
LOW3 = _run(-12, 29, 0)
HIGH3 = _run(-3, 20, 64)
LOW4 = _run(-4, 13, 0)
HIGH4 = _run(-3, 12, 32)
LOW5 = _run(-4, 8, 0)
HIGH5 = _run(-4, 8, 16)


def _part(places, first, last):
    return {k: places[k] for k in range(first, last)}


def _edges(width):
    far = 1 << 20
    return ((0, far), (-far, far), (-far, width))


def _bundle(parts, rows, cols):
    out = np.zeros((rows, cols))
    for r, c, m in parts:
        out[r : r + m.shape[0], c : c + m.shape[1]] = m
    return _pair(out)


@functools.cache
def _tables():
    fw, inv = _forward, _inverse
    far = 1 << 20
    out = {}
    out["own"] = _bundle(
        (
            (0, 0, fw(_run(0, 256, 0), OWN_LOW0, OWN_HIGH0, 256, 256, -far, far, 1.0)),
            (256, 0, fw(OWN_LOW0, OWN_LOW1, OWN_HIGH1, 128, 128, -far, far, KS)),
        ),
        384,
        256,
    )
    rim, back = [], []
    for v in range(3):
        a, b = zip(*(_edges(256 >> l)[v] for l in range(LEVELS)))
        t5 = fw(LOW4, _part(LOW5, 0, 5), _part(HIGH5, 0, 5), 128, 256, a[5], b[5], KS)
        lows, highs = t5[:, 4:8].copy(), t5[:, 20:24].copy()
        sixteen = np.concatenate([lows, highs[:, 1:], lows[:, 1:], highs[:, 1:], np.zeros((128, 3))], axis=1)
        t5[:, 128:] = np.tile(sixteen, (1, 8))
        one = fw(RIM_IN0, RIM_LOW0, RIM_HIGH0, 512, 128, a[0], b[0], 1.0)
        rim0 = sum(np.roll(one, (32 * g, 32 * g), (0, 1)) for g in range(4))
        rim.append(
            _bundle(
                (
                    (0, 0, fw(IN1, RIM_LOW1, RIM_HIGH1, 256, 128, a[1], b[1], KS)),
                    (0, 128, fw(IN2, LOW2, HIGH2, 256, 128, a[2], b[2], KS)),
                    (0, 256, fw(LOW2, LOW3, HIGH3, 128, 128, a[3], b[3], KS)),
                    (128, 256, fw(LOW3, LOW4, HIGH4, 128, 128, a[4], b[4], KS)),
                    (256, 0, t5),
                    (384, 0, rim0),
                ),
                896,
                384,
            )
        )
        low0 = {**OWN_LOW0, **{k: 256 + v for k, v in RIM_LOW0.items() if -2 <= k < 130}}
        high0 = {**OWN_HIGH0, **{k: 256 + v for k, v in RIM_HIGH0.items()}}
        low1 = {**OWN_LOW1, **{k: 128 + v for k, v in RIM_LOW1.items()}}
        high1 = {**OWN_HIGH1, **{k: 128 + v for k, v in RIM_HIGH1.items()}}
        full = inv(low0, high0, _run(0, 256, 0), 288, 256, a[0], b[0], 1.0)
        ends = np.zeros((128, 128))
        for i in range(32):
            for c in range(-7, 8):
                ends[i, c % 128] = full[256 + i, c % 256]
        ends = sum(np.roll(ends, (32 * g, 32 * g), (0, 1)) for g in range(4))
        s1 = inv(low1, high1, _part(IN1, -1, 130), 256, 256, a[1], b[1], 1.0 / KS)
        s1[:, 128:] = np.tile(s1[:, 128:160], (1, 4))
        back.append(
            _bundle(
                (
                    (0, 0, full[:256]),
                    (256, 0, s1),
                    (512, 0, inv(LOW2, HIGH2, _part(low1, -2, 67), 128, 256, a[2], b[2], 1.0 / KS)),
                    (640, 0, inv(LOW3, HIGH3, _part(LOW2, -2, 36), 128, 128, a[3], b[3], 1.0 / KS)),
                    (640, 128, inv(LOW4, HIGH4, _part(LOW3, -2, 20), 128, 128, a[4], b[4], 1.0 / KS)),
                    (768, 0, inv(LOW5, HIGH5, _part(LOW4, -2, 12), 128, 128, a[5], b[5], 1.0 / KS)),
                    (768, 128, ends),
                ),
                896,
                256,
            )
        )
    out["rim"], out["back"] = np.stack(rim), np.stack(back)
    n = S >> LEVELS
    bands = []
    current = np.eye(n)
    for _ in range(COARSE):
        current, high = _lift(current)
        bands.append(high)
    coarse = np.concatenate([current] + bands[::-1])
    order = (np.arange(n) % NT) * 4 + np.arange(n) // NT
    last = n >> COARSE
    current = np.eye(n)[:last]
    for step in range(COARSE):
        size = last << step
        current = _unlift(current, np.eye(n)[size : 2 * size])
    both = np.zeros((n + 640, n))
    both[:n] = (KS * coarse.T)[order]
    both[n + 4 : 2 * n + 4] = current / KS
    out["coarse"] = _pair(both)
    return out


def _mask(lane, places, first, last, base=0):
    lanes = sorted(v - base for k, v in places.items() if first <= k < last)
    out, i = None, 0
    while i < len(lanes):
        j = i
        while j + 1 < len(lanes) and lanes[j + 1] == lanes[j] + 1:
            j += 1
        hit = (lane >= lanes[i]) & (lane <= lanes[j])
        out = hit if out is None else out | hit
        i = j + 1
    return out


def _ones(hit):
    return jnp.where(hit, 1.0, 0.0)


def _dot3(x, t):
    hi = x.astype(BF16)
    lo = (x - hi.astype(F32)).astype(BF16)
    d = functools.partial(jnp.dot, preferred_element_type=F32)
    both = d(jnp.concatenate([hi, lo], axis=0), t(0))
    return both[: x.shape[0]] + both[x.shape[0] :] + d(hi, t(1))


def _time(load, t, y, step, j):
    x = load(j, step)
    y[pl.ds(j, step)] = _dot3(x.reshape(step * 8, x.shape[2]), t).reshape(step, 8, y.shape[2])


class _Forward:
    def __init__(self, load, t, y, step):
        self.load, self.t, self.y, self.step, self.done = load, t, y, step, 0

    def __call__(self, j):
        ahead = min(j + self.step, self.y.shape[0] - 1)
        while self.done <= ahead:
            _time(self.load, self.t, self.y, self.step, self.done)
            self.done += self.step
        return self.y[j]


class _Backward:
    def __init__(self, y, t, store, step):
        self.y, self.t, self.store, self.step, self.left = y, t, store, step, {}

    def __call__(self, j, value):
        self.y[j] = value
        chunk = j // self.step
        self.left[chunk] = self.left.get(chunk, self.step) - 1
        if not self.left[chunk]:
            x = self.y[pl.ds(chunk * self.step, self.step)]
            out = _dot3(x.reshape(self.step * 8, x.shape[2]), self.t)
            self.store(chunk * self.step, self.step, out.reshape(self.step, 8, out.shape[1]))


def _table(ref, rows, cols, *lead):
    r, c = pl.ds(*rows), pl.ds(*cols)
    return lambda i: ref[(*lead, i, r, c)]


def _sublane(lanes):
    return lax.broadcasted_iota(jnp.int32, (8, lanes), 0)


def _lane(rows=8):
    return lax.broadcasted_iota(jnp.int32, (rows, 128), 1)


def _wide(v, lanes):
    return v if lanes == 128 else jnp.concatenate([v] * (lanes // 128), axis=1)


class _QuarterWrap:
    def __init__(self):
        self.sub, self.group = _sublane(128), _lane() // 32

    def after(self, first, last):
        moved = pltpu.roll(first, 96, 1)
        moved = jnp.where(self.group == 3, pltpu.roll(moved, 7, 0), moved)
        return jnp.where((self.group == 3) & (self.sub == 7), last, moved)

    def before(self, last, first):
        moved = pltpu.roll(last, 32, 1)
        moved = jnp.where(self.group == 0, pltpu.roll(moved, 1, 0), moved)
        return jnp.where((self.group == 0) & (self.sub == 0), first, moved)


def _quarters(values):
    group = _lane() // 32
    out = []
    for c in range(3):
        v = values[0]
        for g in range(1, 4):
            v = jnp.where(group == g, values[(24 * g + 8 * c) // 32], v)
        out.append(v)
    return out


class _Wrap:
    def __init__(self, lanes):
        sub = _sublane(lanes)
        self.last, self.first = sub == 7, sub == 0

    def after(self, first, last):
        return jnp.where(self.last, last, pltpu.roll(first, 7, 0))

    def before(self, last, first):
        return jnp.where(self.first, first, pltpu.roll(last, 1, 0))


def _coefs(weights, lanes):
    return [[_wide(c * v, lanes) for v in weights] for c in (A1, B1, A2, B2)]


def _chan_forward(get, n, weights, lanes, put_low, put_high, wrap=None):
    wrap = wrap or _Wrap(lanes)
    ca, cb, cc, cd = _coefs(weights, lanes)
    per = n // 3
    first = get(0)
    e, o1, e1, o2 = {0: first}, {}, {}, {}

    def high(k, v):
        o2[k] = v
        put_high(k, k // per, v)

    def low(k):
        put_low(k, k // per, e1[k] + cd[k // per] * (o2[k - 1] + o2[k]))

    for k in range(n):
        q = k // per
        e[k + 1] = get(2 * k + 2) if k + 1 < n else wrap.after(first, e[k])
        o1[k] = get(2 * k + 1) + ca[q] * (e[k] + e[k + 1])
        if k >= 1:
            e1[k] = e[k] + cb[q] * (o1[k - 1] + o1[k])
        if k >= 2:
            high(k - 1, o1[k - 1] + cc[(k - 1) // per] * (e1[k - 1] + e1[k]))
        if k >= 3:
            low(k - 1)
    e1[0] = first + cb[0] * (wrap.before(o1[n - 1], o1[0]) + o1[0])
    high(0, o1[0] + cc[0] * (e1[0] + e1[1]))
    high(n - 1, o1[n - 1] + cc[2] * (e1[n - 1] + wrap.after(e1[0], e1[n - 1])))
    o2[-1] = wrap.before(o2[n - 1], o2[0])
    for k in (0, 1, n - 1):
        low(k)


def _chan_inverse(get_low, get_high, n, weights, lanes, put, wrap=None):
    wrap = wrap or _Wrap(lanes)
    ca, cb, cc, cd = _coefs(weights, lanes)
    per = n // 3
    o = {0: get_high(0)}
    o[-1] = wrap.before(get_high(n - 1), o[0])
    e1, o1, e2 = {}, {}, {}

    def even(k):
        e2[k] = e1[k] - cb[k // per] * (o1[k - 1] + o1[k])
        put(2 * k, e2[k])

    def odd(k):
        put(2 * k + 1, o1[k] - ca[k // per] * (e2[k] + e2[k + 1]))

    for k in range(n):
        q = k // per
        if k:
            o[k] = get_high(k)
        e1[k] = get_low(k) - cd[q] * (o[k - 1] + o[k])
        if k >= 1:
            o1[k - 1] = o[k - 1] - cc[(k - 1) // per] * (e1[k - 1] + e1[k])
        if k >= 2:
            even(k - 1)
        if k >= 3:
            odd(k - 2)
    o1[n - 1] = o[n - 1] - cc[2] * (e1[n - 1] + wrap.after(e1[0], e1[n - 1]))
    o1[-1] = wrap.before(o1[n - 1], o1[0])
    even(n - 1)
    if n > 2:
        odd(n - 2)
    even(0)
    odd(0)
    e2[n] = wrap.after(e2[0], e2[n - 1])
    odd(n - 1)


class _Squares:
    def __init__(self):
        self.acc = {}

    def add(self, key, v):
        self.acc[key] = v * v if key not in self.acc else self.acc[key] + v * v

    def total(self, rows, tiles):
        out = None
        for q in range(3):
            part = None
            for (band, tile), lanes in tiles.items():
                v = self.acc[(band, tile, q)] * (KS * KS if band == "low" else 1.0 / (KS * KS))
                v = v if lanes is None else v * lanes
                part = v if part is None else part + v
            part = part * rows[q]
            out = part if out is None else out + part
        return out


def _tile(v, i):
    return v[:, 128 * i : 128 * (i + 1)]


def _blocks(w, level):
    return [w[level, q] for q in range(3)]


def _own_rows(core):
    block = 3 * _sublane(128)
    return [
        jnp.where(core == 0, _ones(block + q < 16), _ones(block + q >= 8)) for q in range(3)
    ]


def _load_kernel(
    sc, x_all, gauge_table_all, gauge_index_all, own_all, rim_all,
    low, high, ends, own_table, rim_table, w,
    x, gauge_table, gauge_index, sems,
):
    core = sc[0]
    copies = [
        pltpu.make_async_copy(src, dst, sems.at[i])
        for i, (src, dst) in enumerate(
            (
                (gauge_index_all, gauge_index),
                (gauge_table_all, gauge_table),
                (own_all, own_table),
                *((x_all.at[pl.ds(256 * i, 256)], x.at[pl.ds(256 * i, 256)]) for i in range(4)),
                (rim_all.at[sc[1]], rim_table),
            )
        )
    ]
    for c in copies:
        c.start()
    for c in copies[:2]:
        c.wait()
    index = gauge_index[...]
    table_rows = gauge_table[...]
    weights = jnp.zeros(index.shape, F32)
    for g in range(GTAB):
        weights = weights + jnp.where(index == g, table_rows[:, g : g + 1], 0.0)
    block = lax.broadcasted_iota(jnp.int32, (8, NBLK), 1) - 3 * lax.broadcasted_iota(jnp.int32, (8, NBLK), 0)
    block = block - 8 * core
    for l in range(LEVELS):
        for q in range(3):
            hit = jnp.where(block == q, weights[l : l + 1], 0.0)
            w[l, q] = jnp.broadcast_to(jnp.sum(hit, axis=1, keepdims=True), (8, 128))
    copies[2].wait()
    for i in range(4):
        copies[3 + i].wait()
        _first(x, own_table, low, high, ends, 0, range(256 * i, 256 * i + 256, 128))
    copies[7].wait()


def _first(x, table, low, high, ends, at, blocks):
    lane = _lane(128)
    for r in blocks:
        v = x[pl.ds(r, 128), :]
        y = _dot3(v, _table(table, (0, 256), (0, 256)))
        rows = pl.ds(at + r, 128)
        low[rows, :] = y[:, 0:128]
        high[rows, :] = y[:, 128:256]
        ends[rows, :] = jnp.where(lane < 32, v[:, 0:128], v[:, 128:256])


def _own_kernel(
    sc, recv, own_low, own_high, own_ends, table, w,
    right, left, low0, a1l, fh, details, sums,
    fl, fe, y1,
):
    core = sc[0]
    at_own = pl.multiple_of(core * HALO, 8)
    at_recv = pl.multiple_of((1 - core) * OWN, 8)
    for src, dst in ((own_low, fl), (own_high, fh), (own_ends, fe)):
        for r in range(0, OWN, 128):
            dst[pl.ds(at_own + r, 128), :] = src[pl.ds(r, 128), :]
    theirs = recv.at[pl.ds(at_own, HALO)]
    _first(theirs, table, fl, fh, fe, at_recv, range(0, HALO, 128))
    lane = _lane()
    group = lane // 32
    for i in range(48):
        to_right, to_left = None, None
        for g in range(4):
            j = 48 * g + i
            v = fe[pl.ds(j, 8, stride=SEG), :]
            a = pltpu.roll(v, 32 * g, 1) if g else v
            b = pltpu.roll(v, (32 * g + 32) % 128, 1) if g != 3 else v
            to_left = a if to_left is None else jnp.where(group == g, a, to_left)
            to_right = b if to_right is None else jnp.where(group == g, b, to_right)
        right[i] = to_right
        left[i] = to_left
    rows = _own_rows(core)
    sq = _Squares()

    def put_low(k, q, v):
        low0[k] = v

    def put_high(k, q, v):
        details[k] = v
        sq.add(("high", 0, q), v)

    _chan_forward(lambda j: fl[pl.ds(j, 8, stride=SEG), :], 96, _blocks(w, 0), 128, put_low, put_high)
    sums[0] = sq.total(rows, {("high", 0): None})
    sq1 = _Squares()

    def put_low1(k, q, v):
        a1l[k] = v
        details[96 + k] = v
        sq1.add(("low", 0, q), v)
        if k >= 26:
            packed = jnp.where(lane < 64, a1l[k - 24], pltpu.roll(v, 64, 1))
            right[24 + k] = packed
            left[24 + k] = packed

    def put_high1(k, q, v):
        details[144 + k] = v
        sq1.add(("high", 0, q), v)

    get = _Forward(lambda j, n: low0[pl.ds(j, n)], _table(table, (256, 128), (0, 128)), y1, 24)
    _chan_forward(get, 48, _blocks(w, 1), 128, put_low1, put_high1)
    for k in (24, 25):
        packed = jnp.where(lane < 64, a1l[k - 24], pltpu.roll(a1l[k], 64, 1))
        right[24 + k] = packed
        left[24 + k] = packed
    sums[1] = sq1.total(rows, {("low", 0): _ones(_mask(lane, OWN_HIGH1, 0, 64)), ("high", 0): None})


def _bands(details):
    out, at = [], 0
    for n in (24, 48, 24, 12, 6, 3):
        out += [details.at[pl.ds(at, n)], details.at[pl.ds(at + n, n)]]
        at += 2 * n
    return out


def _aside_kernel(sc, fh, w, back_all, coarse_all, back_table, coarse_table, details, sums, sems):
    copies = []
    for src, dst, parts in ((back_all.at[sc[1]], back_table, 4), (coarse_all, coarse_table, 4)):
        n = dst.shape[1] // parts
        for i in range(2):
            for k in range(parts):
                rows = pl.ds(n * k, n)
                copies.append(pltpu.make_async_copy(src.at[i, rows], dst.at[i, rows], sems.at[len(copies)]))
    for c in copies:
        c.start()
    rows = _own_rows(sc[0])
    sq = _Squares()

    def put_low(k, q, v):
        details[k] = v
        sq.add(("low", 0, q), v)

    def put_high(k, q, v):
        details[96 + k] = v
        sq.add(("high", 0, q), v)

    _chan_forward(lambda j: fh[pl.ds(j, 8, stride=SEG), :], 96, _blocks(w, 0), 128, put_low, put_high)
    sums[...] = sq.total(rows, {("low", 0): None, ("high", 0): None})
    for c in copies:
        c.wait()


def _rim_kernel(
    sc, right, left, from_left, from_right, low0, a1l, own_sums, more_sums, table, w,
    details, payload,
    rim, y0, y1, x2, y2, y3, y4, y5, l5, h5, flat,
):
    core = sc[0]
    rlow0, rhigh0, r1l, r1h, a2l, a2h, a3l, a3h, a4l, a4h, a5l, a5h = _bands(details)
    lane = _lane()
    rows = _own_rows(core)
    totals = []

    def level(l, load, n, t, y, step, lanes, low, high, own_low, own_high, pairs):
        quarters = l == 0
        weights = _blocks(w, l)
        place = lane % 32 if quarters else lane
        sq = _Squares()

        def put_low(k, q, value):
            low[k] = value
            sq.add(("low", 0, q), _tile(value, 0))

        def put_high(k, q, value):
            high[k] = value
            sq.add(("high", 0, q), _tile(value, 0))

        wrap = _QuarterWrap() if quarters else None
        weights = _quarters(weights) if quarters else weights
        _chan_forward(_Forward(load, t, y, step), n, weights, lanes, put_low, put_high, wrap)
        is_high = _mask(place, own_high, 0, pairs)
        is_low = _mask(place, own_low, 0, pairs)
        total = sq.total(_quarters(rows) if quarters else rows, {("low", 0): _ones(is_high), ("high", 0): _ones(is_high | is_low)})
        totals.append(total + own_sums[l] if l < 2 else total)

    def pick(r, k, c, n):
        return _table(table, (r, k), (c, n))

    def load0(j, n):
        at = pl.ds(j, n)
        return jnp.concatenate([from_left[at], left[at], right[at], from_right[at]], axis=2)

    level(0, load0, 24, pick(384, 512, 0, 128), y0, 24, 128, rlow0, rhigh0, RIM_LOW0, RIM_HIGH0, 128)
    totals[0] = totals[0] + more_sums[...]
    for g in range(4):
        for i in range(24):
            rim[24 * g + i] = pltpu.roll(rlow0[i], 128 - 32 * g, 1) if g else rlow0[i]

    def load1(j, n):
        return jnp.concatenate([low0[pl.ds(j, n)], rim[pl.ds(j, n)]], axis=2)

    level(1, load1, 48, pick(0, 256, 0, 128), y1, 24, 128, r1l, r1h, RIM_LOW1, RIM_HIGH1, 64)
    for j in range(48):
        h, i = j // 24, 48 + j % 24
        b, a = from_left[i], from_right[i]
        if h == 0:
            a = pltpu.roll(a, 64, 1)
        else:
            b = pltpu.roll(b, 64, 1)
        x2[j, :, 0:128] = jnp.where(lane < 64, a1l[j], a)
        x2[j, :, 128:256] = jnp.where(lane < 64, b, r1l[j])
    level(2, lambda j, n: x2[pl.ds(j, n)], 24, pick(0, 256, 128, 128), y2, 24, 128, a2l, a2h, LOW2, HIGH2, 32)
    level(3, lambda j, n: a2l[pl.ds(j, n)], 12, pick(0, 128, 256, 128), y3, 24, 128, a3l, a3h, LOW3, HIGH3, 16)
    level(4, lambda j, n: a3l[pl.ds(j, n)], 6, pick(128, 128, 256, 128), y4, 12, 128, a4l, a4h, LOW4, HIGH4, 8)
    level(5, lambda j, n: a4l[pl.ds(j, n)], 3, pick(256, 128, 0, 256), y5, 6, 256, l5, h5, LOW5, HIGH5, 4)
    sub = _sublane(128)
    for j in range(3):
        a5l[j] = l5[j, :, 0:128]
        a5h[j] = h5[j, :, 0:128]
        flat[pl.ds(j, 8, stride=3), :] = jnp.where(lane % 16 < 7, l5[j, :, 128:256], h5[j, :, 128:256])
    sums = jnp.zeros((8, 128), F32)
    for l in range(LEVELS):
        sums = jnp.where(sub == l, jnp.sum(totals[l], axis=0, keepdims=True), sums)
    sums = jnp.where((lane == 16 * sub + 13) & (sub < LEVELS), jnp.sum(sums, axis=1, keepdims=True), 0.0)
    lines = []
    for h in range(2):
        mine = flat[pl.ds(pl.multiple_of(8 * core + 8 * h, 8), 8), :]
        mine = jnp.where(lane // 16 == sub, mine, 0.0)
        lines.append(jnp.sum(mine + sums if h == 0 else mine, axis=0, keepdims=True))
    block = jnp.where(sub % 2 == 0, lines[0], lines[1])
    for i in range(32):
        payload[pl.ds(8 * i, 8), :] = block


def _shrink(v, limit):
    return v - jnp.minimum(jnp.maximum(v, -limit), limit)


def _back_kernel(
    sc, mine, theirs, coarse_table, table, own_details, more_details, rim_details, w,
    out,
    gt, nears, cur, x5l, x5h, y5, y4, y3, y2, y1, c4, c3, c2, c1, c0, f0, f1, f2, yr, stage, sems,
):
    core, place = sc[0], sc[2]
    rlow0, rhigh0, r1l, r1h, a2l, a2h, a3l, a3h, a4l, a4h, a5l, a5h = _bands(rim_details)
    dhigh0, dlow0, dhigh1 = own_details.at[pl.ds(0, 96)], more_details.at[pl.ds(0, 96)], more_details.at[pl.ds(96, 96)]
    a1l, a1h = (own_details.at[pl.ds(96 + 48 * i, 48)] for i in range(2))
    lane = _lane()
    lane1 = _lane(1)
    sub = _sublane(128)
    for h in range(2):
        halves = [g[pl.ds(h, NT, stride=2), :] for g in (mine, theirs)]
        if h == 0:
            total = jnp.sum(halves[0] + halves[1], axis=0, keepdims=True)
        for c in range(2):
            gt[c, h] = jnp.transpose(jnp.where(core == c, halves[0], halves[1]))
    limits = []
    for l in range(LEVELS):
        entries = 3 * (C >> (l + 1)) * (S >> (l + 1))
        s = jnp.sum(jnp.where(lane1 == 16 * l + 13, total, 0.0), axis=1, keepdims=True)
        limits.append(jnp.sqrt(s * (1.0 / entries) + FLOOR))
    rows = [
        jnp.concatenate([gt[c, h, pl.ds(m, 8, stride=16), :] for m in range(4)], axis=1)
        for c in range(2)
        for h in range(2)
    ]
    coarse = _dot3(jnp.concatenate(rows, axis=0), lambda i: coarse_table[i, 0:512, :])
    highs = lax.broadcasted_iota(jnp.int32, (32, 512), 1) >= (S >> (LEVELS + COARSE))
    square = jnp.sum(jnp.where(highs, coarse * coarse, 0.0), axis=0, keepdims=True)
    square = jnp.sum(square, axis=1, keepdims=True)
    entries = (C >> LEVELS) * ((S >> LEVELS) - (S >> (LEVELS + COARSE)))
    limit = jnp.sqrt(square * (1.0 / entries) + FLOOR)
    coarse = jnp.where(highs, _shrink(coarse, limit), coarse)
    hi = coarse.astype(BF16)
    lo = (coarse - hi.astype(F32)).astype(BF16)
    for side, other in enumerate((jnp.maximum(place - 1, 0), jnp.minimum(place + 1, NT - 1))):
        for c in range(2):
            for h in range(2):
                row = pl.ds(2 * other + h, 1)
                line = jnp.broadcast_to(jnp.where(core == c, mine[row, :], theirs[row, :]), (8, 128))
                near = line
                for k in range(1, 8):
                    near = jnp.where(sub == k, pltpu.roll(line, 128 - 16 * k, 1), near)
                nears[side, pl.ds(16 * c + 8 * h, 8), :] = near
    for k in range(3):
        rows = pl.ds(8 * core + k, 8, stride=3)
        before, after = nears[0, rows, :], nears[1, rows, :]
        v = a5h[k]
        for at, near, shift in ((1, before, 122), (9, after, 2), (17, before, 7), (25, after, 15)):
            v = jnp.where((lane >= at) & (lane < at + 3), pltpu.roll(near, shift, 1), v)
        x5h[k] = v
        v = a5l[k]
        for at, near, shift in ((17, before, 13), (25, after, 21)):
            v = jnp.where((lane >= at) & (lane < at + 3), pltpu.roll(near, shift, 1), v)
        x5l[k] = v

    def nt(a, b):
        return lax.dot_general(a, b, (((1,), (1,)), ((), ())), preferred_element_type=F32)

    rows = pl.ds(pl.multiple_of(512 + 16 * (place // 4), 16), 128)
    current = nt(hi, coarse_table[0, rows, :]) + nt(lo, coarse_table[0, rows, :]) + nt(hi, coarse_table[1, rows, :])
    cur[...] = pltpu.roll(current, (128 - 4 * (place % 4)) % 128, 1)

    def level(l, get_current, low, high, n, y, t, nxt, step, needed):
        tl = jnp.broadcast_to(limits[l] * (1.0 / KS), (8, 128))
        th = jnp.broadcast_to(limits[l] * KS, (8, 128))
        is_low = needed(lane)

        def get_low(k):
            return jnp.where(is_low, get_current(k), _shrink(low[k], tl))

        def store(j, m, value):
            nxt[pl.ds(j, m)] = value

        put = _Backward(y, t, store, step)
        _chan_inverse(get_low, lambda k: _shrink(high[k], th), n, _blocks(w, l), 128, put)

    def pick(r, k, c, n):
        return _table(table, (r, k), (c, n))

    level(
        5, lambda k: cur[pl.ds(8 * core + k, 8, stride=3), :], x5l, x5h, 3, y5, pick(768, 128, 0, 128), c4, 6, lambda i: i < 12
    )
    level(4, lambda k: c4[k], a4l, a4h, 6, y4, pick(640, 128, 128, 128), c3, 12, lambda i: i < 32)
    level(3, lambda k: c3[k], a3l, a3h, 12, y3, pick(640, 128, 0, 128), c2, 24, lambda i: i < 64)
    level(2, lambda k: c2[k], a2l, a2h, 24, y2, pick(512, 128, 0, 256), c1, 24, lambda i: i < 89)
    tl = jnp.broadcast_to(limits[1] * (1.0 / KS), (8, 256))
    th = jnp.broadcast_to(limits[1] * KS, (8, 256))
    lane2 = lax.broadcasted_iota(jnp.int32, (8, 256), 1)
    is_low1 = (lane2 < 64) | ((lane2 >= 192) & (lane2 < 208))

    def get_low1(k):
        v1 = jnp.concatenate([a1l[k], r1l[k]], axis=1)
        return jnp.where(is_low1, c1[k], _shrink(v1, tl))

    def get_high1(k):
        return _shrink(jnp.concatenate([a1h[k], r1h[k]], axis=1), th)

    def store1(j, m, value):
        c0[pl.ds(j, m)] = value

    put1 = _Backward(y1, pick(256, 256, 0, 256), store1, 24)
    _chan_inverse(get_low1, get_high1, 48, _blocks(w, 1), 256, put1)
    tl0 = jnp.broadcast_to(limits[0] * (1.0 / KS), (8, 128))
    th0 = jnp.broadcast_to(limits[0] * KS, (8, 256))
    group = lane // 32
    rim_low = lane % 32 < 23

    def get_low_rim(k):
        now = c0[k, :, 128:256]
        for q in range(1, 4):
            now = jnp.where(group == q, c0[24 * q + k, :, 128:256], now)
        return jnp.where(rim_low, now, _shrink(rlow0[k], tl0))

    def store_rim(j, m, value):
        for i in range(m):
            for q in range(4):
                v = pltpu.roll(value[i], 128 - 32 * q, 1) if q else value[i]
                f2[pl.ds(48 * q + j + i, 8, stride=SEG), :] = v

    put_rim = _Backward(yr, pick(768, 128, 128, 128), store_rim, 24)
    _chan_inverse(
        get_low_rim, lambda k: _shrink(rhigh0[k], th0[:, 0:128]), 24, _quarters(_blocks(w, 0)), 128, put_rim, _QuarterWrap()
    )

    def get_low0(k):
        return jnp.concatenate([c0[k, :, 0:128], _shrink(dlow0[k], tl0)], axis=1)

    def get_high0(k):
        return _shrink(jnp.concatenate([dhigh0[k], dhigh1[k]], axis=1), th0)

    def put0(j, value):
        for i, buf in enumerate((f0, f1)):
            buf[pl.ds(j, 8, stride=SEG), :] = _tile(value, i)

    _chan_inverse(get_low0, get_high0, 96, _blocks(w, 0), 256, put0)
    at_own = pl.multiple_of(core * HALO, 8)
    t = pick(0, 256, 0, 256)
    wide = _lane(128)
    copies = []
    for r in range(0, OWN, 128):
        rows = pl.ds(at_own + r, 128)
        done = pl.ds(r, 128)
        ends = f2[rows, :]
        v = _dot3(jnp.concatenate([f0[rows, :], f1[rows, :]], axis=1), t)
        stage[done, 0:128] = _tile(v, 0) + jnp.where(wide < 8, ends, 0.0)
        stage[done, 128:256] = _tile(v, 1) + jnp.where(wide >= 121, ends, 0.0)
        copies.append(pltpu.make_async_copy(stage.at[done], out.at[done], sems.at[r // 128]))
        copies[-1].start()
    for c in copies:
        c.wait()


VM = pl.BlockSpec(memory_space=pltpu.VMEM)
SM = pl.BlockSpec(memory_space=pltpu.SMEM)
ANY = pl.BlockSpec(memory_space=pl.ANY)
HBM = pl.BlockSpec(memory_space=pltpu.HBM)


def _call(kernel, name, limit, args, specs, outs, out_specs, scratch):
    args = [
        pltpu.with_memory_space_constraint(x, pltpu.HBM) if spec is HBM else x for x, spec in zip(args, specs)
    ]
    outs = [jax.ShapeDtypeStruct(s, F32) if isinstance(s, tuple) else s for s in outs]
    return pl.pallas_call(
        kernel,
        out_shape=[pltpu.HBM(s.shape, s.dtype) if spec is HBM else s for s, spec in zip(outs, out_specs)],
        in_specs=specs,
        out_specs=out_specs,
        scratch_shapes=[pltpu.VMEM(s, F32) if isinstance(s, tuple) else s for s in scratch],
        compiler_params=pltpu.CompilerParams(vmem_limit_bytes=limit << 20),
        name=name,
    )(*args)


def _shift(v, by):
    return lax.ppermute(v, "tm", [(i, (i + by) % NT) for i in range(NT)])


def shards(record, gauge_table, gauge_index):
    tables = _tables()
    core = lax.axis_index("chan")
    place = lax.axis_index("tm")
    variant = jnp.where(place == 0, 0, jnp.where(place == NT - 1, 2, 1))
    sc = jnp.stack([core, variant, place]).astype(jnp.int32)
    dma = pltpu.SemaphoreType.DMA
    recv = lax.ppermute(record, "chan", [(0, 1), (1, 0)])
    low, high, ends, own_table, rim_table, w = _call(
        _load_kernel, "load", 12, (sc, record, gauge_table, gauge_index, tables["own"], tables["rim"]),
        [SM] + [HBM] * 5,
        [(OWN, 128), (OWN, 128), (OWN, 128), jax.ShapeDtypeStruct((2, 384, 256), BF16),
         jax.ShapeDtypeStruct((2, 896, 384), BF16), (LEVELS, 3, 8, 128)],
        [VM] * 6,
        [(OWN, 256), (LEVELS, GTAB), pltpu.VMEM((LEVELS, NBLK), jnp.int32), dma((8,))],
    )
    right, left, low0, a1l, fh, own_details, sums = _call(
        _own_kernel, "own", 12, (sc, recv, low, high, ends, own_table, w), [SM] + [VM] * 6,
        [(72, 8, 128), (72, 8, 128), (96, 8, 128), (48, 8, 128), (8 * SEG, 128), (192, 8, 128), (2, 8, 128)],
        [VM] * 7,
        [(8 * SEG, 128), (8 * SEG, 128), (96, 8, 128)],
    )
    from_left, from_right = _shift(right, 1), _shift(left, -1)
    back_table, coarse_table, more_details, more_sums = _call(
        _aside_kernel, "aside", 6, (sc, fh, w, tables["back"], tables["coarse"]), [SM, VM, VM, HBM, HBM],
        [jax.ShapeDtypeStruct((2, 896, 256), BF16), jax.ShapeDtypeStruct((2, 1152, 512), BF16), (192, 8, 128), (8, 128)],
        [VM] * 4,
        [dma((16,))],
    )
    rim_details, payload = _call(
        _rim_kernel, "rim", 16,
        (sc, right, left, from_left, from_right, low0, a1l, sums, more_sums, rim_table, w), [SM] + [VM] * 10,
        [(234, 8, 128), (256, 128)], [VM] * 2,
        [(96, 8, 128), (48, 8, 128), (96, 8, 128), (48, 8, 256), (48, 8, 128), (24, 8, 128), (12, 8, 128),
         (6, 8, 256), (3, 8, 256), (3, 8, 256), (24, 128)],
    )
    mine = lax.all_to_all(payload, "tm", split_axis=0, concat_axis=0, tiled=True)
    theirs = lax.ppermute(mine, "chan", [(0, 1), (1, 0)])
    (out,) = _call(
        _back_kernel, "back", 24, (sc, mine, theirs, coarse_table, back_table, own_details, more_details, rim_details, w),
        [SM] + [VM] * 8, [(OWN, 256)], [HBM],
        [
            (2, 2, 128, 128), (2, 32, 128), (32, 128), (3, 8, 128), (3, 8, 128),
            (6, 8, 128), (12, 8, 128), (24, 8, 128), (48, 8, 128), (96, 8, 256),
            (6, 8, 128), (12, 8, 128), (24, 8, 128), (48, 8, 256), (96, 8, 256),
            (8 * SEG, 128), (8 * SEG, 128), (8 * SEG, 128), (48, 8, 128), (OWN, 256), dma((8,)),
        ],
    )
    return out


def solution(mesh):
    return jax.shard_map(
        shards,
        mesh=mesh,
        in_specs=(P("chan", "tm"), P(), P()),
        out_specs=P("chan", "tm"),
        check_vma=False,
    )
```

```python
import functools

import jax
import jax.numpy as jnp
import ml_dtypes
import numpy as np
from jax import lax
from jax.experimental import pallas as pl
from jax.experimental.pallas import tpu as pltpu
from jax.sharding import PartitionSpec as P

LEVELS = 6
COARSE = 6
GTAB = 8
NBLK = 32
C = 2048
S = 32768
NT = 128
OWN = 1024
HALO = 512
SEG = 192
A1 = -1.586134342059924
B1 = -0.052980118572961
A2 = 0.882911075530934
B2 = 0.443506852043971
KS = 1.149604398860241
FLOOR = 1e-06
F32 = jnp.float32
BF16 = jnp.bfloat16


def _next(e):
    return np.concatenate((e[1:], e[-1:]))


def _prev(o):
    return np.concatenate((o[:1], o[:-1]))


def _lift(x):
    e, o = x[0::2], x[1::2]
    o = o + A1 * (e + _next(e))
    e = e + B1 * (_prev(o) + o)
    o = o + A2 * (e + _next(e))
    e = e + B2 * (_prev(o) + o)
    return KS * e, o / KS


def _unlift(low, high):
    e, o = low / KS, high * KS
    e = e - B2 * (_prev(o) + o)
    o = o - A2 * (e + _next(e))
    e = e - B1 * (_prev(o) + o)
    o = o - A1 * (e + _next(e))
    return np.stack((e, o), axis=1).reshape((2 * e.shape[0],) + e.shape[1:])


def _forward(inputs, lows, highs, rows, cols, start, stop, scale):
    pairs = list(lows) + list(highs)
    a = max(2 * min(pairs) - 16, start)
    b = min(2 * max(pairs) + 16, stop)
    low, high = _lift(np.eye(b - a))
    out = np.zeros((rows, cols))
    for band, places in ((low, lows), (high, highs)):
        for pair, col in places.items():
            if a <= 2 * pair < b:
                line = band[pair - a // 2]
                for i in np.nonzero(line)[0]:
                    out[inputs[a + int(i)], col] += scale * line[i]
    return out


def _inverse(lows, highs, outputs, rows, cols, start, stop, scale):
    a = max(2 * (min(outputs) // 2) - 16, start) // 2
    b = min(2 * (max(outputs) // 2) + 18, stop) // 2
    n = b - a
    eye, zero = np.eye(n), np.zeros((n, n))
    from_low, from_high = _unlift(eye, zero), _unlift(zero, eye)
    out = np.zeros((rows, cols))
    for sample, col in outputs.items():
        if 2 * a <= sample < 2 * b:
            for lines, places in ((from_low, lows), (from_high, highs)):
                line = lines[sample - 2 * a]
                for i in np.nonzero(line)[0]:
                    out[places[a + int(i)], col] += scale * line[i]
    return out


def _pair(m):
    hi = m.astype(ml_dtypes.bfloat16)
    lo = (m - hi.astype(np.float64)).astype(ml_dtypes.bfloat16)
    return np.stack((hi, lo))


def _run(first, last, at):
    return {k: at + k - first for k in range(first, last)}


OWN_LOW0 = _run(2, 126, 2)
OWN_HIGH0 = _run(2, 126, 130)
RIM_LOW0 = {**_run(-2, 2, 0), **_run(126, 130, 4)}
RIM_HIGH0 = {**_run(-2, 2, 8), **_run(126, 130, 12)}
RIM_IN0 = {**_run(-8, 0, 0), **_run(0, 8, 128), **_run(248, 256, 256), **_run(256, 264, 384)}
OWN_LOW1 = _run(3, 61, 3)
OWN_HIGH1 = _run(2, 61, 66)
RIM_LOW1 = {**_run(-3, 3, 64), **_run(61, 67, 70)}
RIM_HIGH1 = {**_run(-3, 2, 80), **_run(61, 67, 85)}
IN1 = {**OWN_LOW0, **{k: 128 + v for k, v in RIM_LOW0.items()}, **_run(-10, -2, 160), **_run(130, 138, 168)}
IN2 = {
    **OWN_LOW1, **_run(67, 125, 67), **_run(-61, -3, 131), **{k: 128 + v for k, v in RIM_LOW1.items()}
}
LOW2 = _run(-28, 61, 0)
HIGH2 = _run(-3, 36, 89)
LOW3 = _run(-12, 29, 0)
HIGH3 = _run(-3, 20, 64)
LOW4 = _run(-4, 13, 0)
HIGH4 = _run(-3, 12, 32)
LOW5 = _run(-4, 8, 0)
HIGH5 = _run(-4, 8, 16)


def _part(places, first, last):
    return {k: places[k] for k in range(first, last)}


def _edges(width):
    far = 1 << 20
    return ((0, far), (-far, far), (-far, width))


def _bundle(parts, rows, cols):
    out = np.zeros((rows, cols))
    for r, c, m in parts:
        out[r : r + m.shape[0], c : c + m.shape[1]] = m
    return _pair(out)


@functools.cache
def _tables():
    fw, inv = _forward, _inverse
    far = 1 << 20
    out = {}
    out["own"] = _bundle(
        (
            (0, 0, fw(_run(0, 256, 0), OWN_LOW0, OWN_HIGH0, 256, 256, -far, far, 1.0)),
            (256, 0, fw(OWN_LOW0, OWN_LOW1, OWN_HIGH1, 128, 128, -far, far, KS)),
        ),
        384,
        256,
    )
    rim, back = [], []
    for v in range(3):
        a, b = zip(*(_edges(256 >> l)[v] for l in range(LEVELS)))
        t5 = fw(LOW4, _part(LOW5, 0, 5), _part(HIGH5, 0, 5), 128, 256, a[5], b[5], KS)
        lows, highs = t5[:, 4:8].copy(), t5[:, 20:24].copy()
        sixteen = np.concatenate([lows, highs[:, 1:], lows[:, 1:], highs[:, 1:], np.zeros((128, 3))], axis=1)
        t5[:, 128:] = np.tile(sixteen, (1, 8))
        one = fw(RIM_IN0, RIM_LOW0, RIM_HIGH0, 512, 128, a[0], b[0], 1.0)
        rim0 = [sum(np.roll(one, (8 * (4 * g + h), 32 * g), (0, 1)) for g in range(4)) for h in range(4)]
        rim.append(
            _bundle(
                (
                    (0, 0, fw(IN1, RIM_LOW1, RIM_HIGH1, 256, 128, a[1], b[1], KS)),
                    (0, 128, fw(IN2, LOW2, HIGH2, 256, 128, a[2], b[2], KS)),
                    (0, 256, fw(LOW2, LOW3, HIGH3, 128, 128, a[3], b[3], KS)),
                    (128, 256, fw(LOW3, LOW4, HIGH4, 128, 128, a[4], b[4], KS)),
                    (256, 0, t5),
                    (384, 0, np.concatenate(rim0, axis=1)),
                ),
                896,
                512,
            )
        )
        low0 = {**OWN_LOW0, **{k: 256 + v for k, v in RIM_LOW0.items() if -2 <= k < 130}}
        high0 = {**OWN_HIGH0, **{k: 256 + v for k, v in RIM_HIGH0.items()}}
        low1 = {**OWN_LOW1, **{k: 128 + v for k, v in RIM_LOW1.items()}}
        high1 = {**OWN_HIGH1, **{k: 128 + v for k, v in RIM_HIGH1.items()}}
        full = inv(low0, high0, _run(0, 256, 0), 288, 256, a[0], b[0], 1.0)
        ends = np.zeros((128, 128))
        for i in range(32):
            for c in range(-7, 8):
                ends[i, c % 128] = full[256 + i, c % 256]
        ends = sum(np.roll(ends, (32 * g, 32 * g), (0, 1)) for g in range(4))
        s1 = inv(low1, high1, _part(IN1, -1, 130), 256, 256, a[1], b[1], 1.0 / KS)
        s1[:, 128:] = np.tile(s1[:, 128:160], (1, 4))
        back.append(
            _bundle(
                (
                    (0, 0, full[:256]),
                    (256, 0, s1),
                    (512, 0, inv(LOW2, HIGH2, _part(low1, -2, 67), 128, 256, a[2], b[2], 1.0 / KS)),
                    (640, 0, inv(LOW3, HIGH3, _part(LOW2, -2, 36), 128, 128, a[3], b[3], 1.0 / KS)),
                    (640, 128, inv(LOW4, HIGH4, _part(LOW3, -2, 20), 128, 128, a[4], b[4], 1.0 / KS)),
                    (768, 0, inv(LOW5, HIGH5, _part(LOW4, -2, 12), 128, 128, a[5], b[5], 1.0 / KS)),
                    (768, 128, ends),
                ),
                896,
                256,
            )
        )
    out["rim"], out["back"] = np.stack(rim), np.stack(back)
    n = S >> LEVELS
    bands = []
    current = np.eye(n)
    for _ in range(COARSE):
        current, high = _lift(current)
        bands.append(high)
    coarse = np.concatenate([current] + bands[::-1])
    order = (np.arange(n) % NT) * 4 + np.arange(n) // NT
    last = n >> COARSE
    current = np.eye(n)[:last]
    for step in range(COARSE):
        size = last << step
        current = _unlift(current, np.eye(n)[size : 2 * size])
    both = np.zeros((n + 640, n))
    both[:n] = (KS * coarse.T)[order]
    both[n + 4 : 2 * n + 4] = current / KS
    out["coarse"] = _pair(both)
    return out


def _mask(lane, places, first, last, base=0):
    lanes = sorted(v - base for k, v in places.items() if first <= k < last)
    out, i = None, 0
    while i < len(lanes):
        j = i
        while j + 1 < len(lanes) and lanes[j + 1] == lanes[j] + 1:
            j += 1
        hit = (lane >= lanes[i]) & (lane <= lanes[j])
        out = hit if out is None else out | hit
        i = j + 1
    return out


def _ones(hit):
    return jnp.where(hit, 1.0, 0.0)


def _dot3(x, t):
    hi = x.astype(BF16)
    lo = (x - hi.astype(F32)).astype(BF16)
    d = functools.partial(jnp.dot, preferred_element_type=F32)
    both = d(jnp.concatenate([hi, lo], axis=0), t(0))
    return both[: x.shape[0]] + both[x.shape[0] :] + d(hi, t(1))


def _time(load, t, y, step, j):
    x = load(j, step)
    y[pl.ds(j, step)] = _dot3(x.reshape(step * 8, x.shape[2]), t).reshape(step, 8, y.shape[2])


class _Forward:
    def __init__(self, load, t, y, step):
        self.load, self.t, self.y, self.step, self.done = load, t, y, step, 0

    def __call__(self, j):
        ahead = min(j + self.step, self.y.shape[0] - 1)
        while self.done <= ahead:
            _time(self.load, self.t, self.y, self.step, self.done)
            self.done += self.step
        return self.y[j]


class _Backward:
    def __init__(self, y, t, store, step):
        self.y, self.t, self.store, self.step, self.left = y, t, store, step, {}

    def __call__(self, j, value):
        self.y[j] = value
        chunk = j // self.step
        self.left[chunk] = self.left.get(chunk, self.step) - 1
        if not self.left[chunk]:
            x = self.y[pl.ds(chunk * self.step, self.step)]
            out = _dot3(x.reshape(self.step * 8, x.shape[2]), self.t)
            self.store(chunk * self.step, self.step, out.reshape(self.step, 8, out.shape[1]))


def _table(ref, rows, cols, *lead):
    r, c = pl.ds(*rows), pl.ds(*cols)
    return lambda i: ref[(*lead, i, r, c)]


def _sublane(lanes):
    return lax.broadcasted_iota(jnp.int32, (8, lanes), 0)


def _lane(rows=8):
    return lax.broadcasted_iota(jnp.int32, (rows, 128), 1)


def _wide(v, lanes):
    return v if lanes == 128 else jnp.concatenate([v] * (lanes // 128), axis=1)


class _QuarterWrap:
    def __init__(self):
        self.sub, self.group = _sublane(128), _lane() // 32

    def after(self, first, last):
        moved = pltpu.roll(first, 96, 1)
        moved = jnp.where(self.group == 3, pltpu.roll(moved, 7, 0), moved)
        return jnp.where((self.group == 3) & (self.sub == 7), last, moved)

    def before(self, last, first):
        moved = pltpu.roll(last, 32, 1)
        moved = jnp.where(self.group == 0, pltpu.roll(moved, 1, 0), moved)
        return jnp.where((self.group == 0) & (self.sub == 0), first, moved)


def _quarters(values):
    group = _lane() // 32
    out = []
    for c in range(3):
        v = values[0]
        for g in range(1, 4):
            v = jnp.where(group == g, values[(24 * g + 8 * c) // 32], v)
        out.append(v)
    return out


class _Wrap:
    def __init__(self, lanes):
        sub = _sublane(lanes)
        self.last, self.first = sub == 7, sub == 0

    def after(self, first, last):
        return jnp.where(self.last, last, pltpu.roll(first, 7, 0))

    def before(self, last, first):
        return jnp.where(self.first, first, pltpu.roll(last, 1, 0))


def _coefs(weights, lanes):
    return [[_wide(c * v, lanes) for v in weights] for c in (A1, B1, A2, B2)]


def _chan_forward(get, n, weights, lanes, put_low, put_high, wrap=None):
    wrap = wrap or _Wrap(lanes)
    ca, cb, cc, cd = _coefs(weights, lanes)
    per = n // 3
    first = get(0)
    e, o1, e1, o2 = {0: first}, {}, {}, {}

    def high(k, v):
        o2[k] = v
        put_high(k, k // per, v)

    def low(k):
        put_low(k, k // per, e1[k] + cd[k // per] * (o2[k - 1] + o2[k]))

    for k in range(n):
        q = k // per
        e[k + 1] = get(2 * k + 2) if k + 1 < n else wrap.after(first, e[k])
        o1[k] = get(2 * k + 1) + ca[q] * (e[k] + e[k + 1])
        if k >= 1:
            e1[k] = e[k] + cb[q] * (o1[k - 1] + o1[k])
        if k >= 2:
            high(k - 1, o1[k - 1] + cc[(k - 1) // per] * (e1[k - 1] + e1[k]))
        if k >= 3:
            low(k - 1)
    e1[0] = first + cb[0] * (wrap.before(o1[n - 1], o1[0]) + o1[0])
    high(0, o1[0] + cc[0] * (e1[0] + e1[1]))
    high(n - 1, o1[n - 1] + cc[2] * (e1[n - 1] + wrap.after(e1[0], e1[n - 1])))
    o2[-1] = wrap.before(o2[n - 1], o2[0])
    for k in (0, 1, n - 1):
        low(k)


def _chan_inverse(get_low, get_high, n, weights, lanes, put, wrap=None):
    wrap = wrap or _Wrap(lanes)
    ca, cb, cc, cd = _coefs(weights, lanes)
    per = n // 3
    o = {0: get_high(0)}
    o[-1] = wrap.before(get_high(n - 1), o[0])
    e1, o1, e2 = {}, {}, {}

    def even(k):
        e2[k] = e1[k] - cb[k // per] * (o1[k - 1] + o1[k])
        put(2 * k, e2[k])

    def odd(k):
        put(2 * k + 1, o1[k] - ca[k // per] * (e2[k] + e2[k + 1]))

    for k in range(n):
        q = k // per
        if k:
            o[k] = get_high(k)
        e1[k] = get_low(k) - cd[q] * (o[k - 1] + o[k])
        if k >= 1:
            o1[k - 1] = o[k - 1] - cc[(k - 1) // per] * (e1[k - 1] + e1[k])
        if k >= 2:
            even(k - 1)
        if k >= 3:
            odd(k - 2)
    o1[n - 1] = o[n - 1] - cc[2] * (e1[n - 1] + wrap.after(e1[0], e1[n - 1]))
    o1[-1] = wrap.before(o1[n - 1], o1[0])
    even(n - 1)
    if n > 2:
        odd(n - 2)
    even(0)
    odd(0)
    e2[n] = wrap.after(e2[0], e2[n - 1])
    odd(n - 1)


class _Squares:
    def __init__(self):
        self.acc = {}

    def add(self, key, v):
        self.acc[key] = v * v if key not in self.acc else self.acc[key] + v * v

    def total(self, rows, tiles):
        out = None
        for q in range(3):
            part = None
            for (band, tile), lanes in tiles.items():
                v = self.acc[(band, tile, q)] * (KS * KS if band == "low" else 1.0 / (KS * KS))
                v = v if lanes is None else v * lanes
                part = v if part is None else part + v
            part = part * rows[q]
            out = part if out is None else out + part
        return out


def _tile(v, i):
    return v[:, 128 * i : 128 * (i + 1)]


def _blocks(w, level):
    return [w[level, q] for q in range(3)]


def _own_rows(core):
    block = 3 * _sublane(128)
    return [
        jnp.where(core == 0, _ones(block + q < 16), _ones(block + q >= 8)) for q in range(3)
    ]


def _load_kernel(
    sc, x_all, gauge_table_all, gauge_index_all, own_all,
    low, high, ends, own_table, w,
    x, gauge_table, gauge_index, sems,
):
    core = sc[0]
    copies = [
        pltpu.make_async_copy(src, dst, sems.at[i])
        for i, (src, dst) in enumerate(
            (
                (gauge_index_all, gauge_index),
                (gauge_table_all, gauge_table),
                (own_all, own_table),
                *((x_all.at[pl.ds(256 * i, 256)], x.at[pl.ds(256 * i, 256)]) for i in range(4)),
            )
        )
    ]
    for c in copies:
        c.start()
    for c in copies[:2]:
        c.wait()
    index = gauge_index[...]
    table_rows = gauge_table[...]
    weights = jnp.zeros(index.shape, F32)
    for g in range(GTAB):
        weights = weights + jnp.where(index == g, table_rows[:, g : g + 1], 0.0)
    block = lax.broadcasted_iota(jnp.int32, (8, NBLK), 1) - 3 * lax.broadcasted_iota(jnp.int32, (8, NBLK), 0)
    block = block - 8 * core
    for l in range(LEVELS):
        for q in range(3):
            hit = jnp.where(block == q, weights[l : l + 1], 0.0)
            w[l, q] = jnp.broadcast_to(jnp.sum(hit, axis=1, keepdims=True), (8, 128))
    copies[2].wait()
    for i in range(4):
        copies[3 + i].wait()
        _first(x, own_table, low, high, ends, 0, range(256 * i, 256 * i + 256, 128))


def _first(x, table, low, high, ends, at, blocks):
    lane = _lane(128)
    for r in blocks:
        v = x[pl.ds(r, 128), :]
        y = _dot3(v, _table(table, (0, 256), (0, 256)))
        rows = pl.ds(at + r, 128)
        low[rows, :] = y[:, 0:128]
        high[rows, :] = y[:, 128:256]
        ends[rows, :] = jnp.where(lane < 32, v[:, 0:128], v[:, 128:256])


def _own_kernel(
    sc, recv, own_low, own_high, own_ends, table, w,
    right, left, low0, a1l, fh, details, sums,
    fl, fe, y1,
):
    core = sc[0]
    at_own = pl.multiple_of(core * HALO, 8)
    at_recv = pl.multiple_of((1 - core) * OWN, 8)
    for src, dst in ((own_low, fl), (own_high, fh), (own_ends, fe)):
        for r in range(0, OWN, 128):
            dst[pl.ds(at_own + r, 128), :] = src[pl.ds(r, 128), :]
    theirs = recv.at[pl.ds(at_own, HALO)]
    _first(theirs, table, fl, fh, fe, at_recv, range(0, HALO, 128))
    lane = _lane()
    group = lane // 8
    for i in range(12):
        to_right, to_left = None, None
        for g in range(16):
            v = fe[pl.ds(12 * g + i, 8, stride=SEG), :]
            a = pltpu.roll(v, 8 * g, 1) if g else v
            b = pltpu.roll(v, (8 * g + 8) % 128, 1) if g != 15 else v
            to_left = a if to_left is None else jnp.where(group == g, a, to_left)
            to_right = b if to_right is None else jnp.where(group == g, b, to_right)
        right[i] = to_right
        left[i] = to_left
    rows = _own_rows(core)
    sq = _Squares()

    def put_low(k, q, v):
        low0[k] = v

    def put_high(k, q, v):
        details[k] = v
        sq.add(("high", 0, q), v)

    _chan_forward(lambda j: fl[pl.ds(j, 8, stride=SEG), :], 96, _blocks(w, 0), 128, put_low, put_high)
    sums[0] = sq.total(rows, {("high", 0): None})
    for i in range(6):
        to_right, to_left = None, None
        for g in range(16):
            v = low0[6 * g + i]
            a = pltpu.roll(v, (8 * g - 118) % 128, 1)
            b = pltpu.roll(v, (8 * g + 6) % 128, 1)
            to_right = a if to_right is None else jnp.where(group == g, a, to_right)
            to_left = b if to_left is None else jnp.where(group == (g + 1) % 16, b, to_left)
        right[12 + i] = to_right
        left[12 + i] = to_left
    sq1 = _Squares()

    def put_low1(k, q, v):
        a1l[k] = v
        details[96 + k] = v
        sq1.add(("low", 0, q), v)
        if k >= 26:
            packed = jnp.where(lane < 64, a1l[k - 24], pltpu.roll(v, 64, 1))
            right[k - 6] = packed
            left[k - 6] = packed

    def put_high1(k, q, v):
        details[144 + k] = v
        sq1.add(("high", 0, q), v)

    get = _Forward(lambda j, n: low0[pl.ds(j, n)], _table(table, (256, 128), (0, 128)), y1, 24)
    _chan_forward(get, 48, _blocks(w, 1), 128, put_low1, put_high1)
    for k in (24, 25):
        packed = jnp.where(lane < 64, a1l[k - 24], pltpu.roll(a1l[k], 64, 1))
        right[k - 6] = packed
        left[k - 6] = packed
    sums[1] = sq1.total(rows, {("low", 0): _ones(_mask(lane, OWN_HIGH1, 0, 64)), ("high", 0): None})


def _bands(details):
    out, at = [], 0
    for n in (24, 48, 24, 12, 6, 3):
        out += [details.at[pl.ds(at, n)], details.at[pl.ds(at + n, n)]]
        at += 2 * n
    return out


def _aside_kernel(
    sc, fh, w, rim_all, back_all, coarse_all, rim_table, back_table, coarse_table, details, sums, sems
):
    copies = []
    mine = pl.multiple_of(512 + 16 * (sc[2] // 4), 16)
    for i in range(2):
        for src, dst, start, n in (
            (rim_all.at[sc[1], i], rim_table.at[i], 0, 448),
            (rim_all.at[sc[1], i], rim_table.at[i], 448, 448),
            (back_all.at[sc[1], i], back_table.at[i], 0, 896),
            (coarse_all.at[i], coarse_table.at[i], 0, 512),
        ):
            rows = pl.ds(start, n)
            copies.append(pltpu.make_async_copy(src.at[rows], dst.at[rows], sems.at[len(copies)]))
        src, dst = coarse_all.at[i, pl.ds(mine, 128)], coarse_table.at[i, pl.ds(512, 128)]
        copies.append(pltpu.make_async_copy(src, dst, sems.at[len(copies)]))
    for c in copies:
        c.start()
    rows = _own_rows(sc[0])
    sq = _Squares()

    def put_low(k, q, v):
        details[k] = v
        sq.add(("low", 0, q), v)

    def put_high(k, q, v):
        details[96 + k] = v
        sq.add(("high", 0, q), v)

    _chan_forward(lambda j: fh[pl.ds(j, 8, stride=SEG), :], 96, _blocks(w, 0), 128, put_low, put_high)
    sums[...] = sq.total(rows, {("low", 0): None, ("high", 0): None})
    for c in copies:
        c.wait()


def _rim_kernel(
    sc, right, left, from_left, from_right, low0, a1l, own_sums, more_sums, table, w,
    details, payload,
    rim, y0, y1, x2, y2, y3, y4, y5, l5, h5, flat,
):
    core = sc[0]
    rlow0, rhigh0, r1l, r1h, a2l, a2h, a3l, a3h, a4l, a4h, a5l, a5h = _bands(details)
    lane = _lane()
    rows = _own_rows(core)
    totals = []

    def level(l, load, n, t, y, step, lanes, low, high, own_low, own_high, pairs):
        quarters = l == 0
        weights = _blocks(w, l)
        place = lane % 32 if quarters else lane
        sq = _Squares()

        def put_low(k, q, value):
            low[k] = value
            sq.add(("low", 0, q), _tile(value, 0))

        def put_high(k, q, value):
            high[k] = value
            sq.add(("high", 0, q), _tile(value, 0))

        wrap = _QuarterWrap() if quarters else None
        weights = _quarters(weights) if quarters else weights
        get = y.__getitem__ if quarters else _Forward(load, t, y, step)
        _chan_forward(get, n, weights, lanes, put_low, put_high, wrap)
        is_high = _mask(place, own_high, 0, pairs)
        is_low = _mask(place, own_low, 0, pairs)
        total = sq.total(_quarters(rows) if quarters else rows, {("low", 0): _ones(is_high), ("high", 0): _ones(is_high | is_low)})
        totals.append(total + own_sums[l] if l < 2 else total)

    def pick(r, k, c, n):
        return _table(table, (r, k), (c, n))

    raw = pl.ds(0, 12)
    raw = jnp.concatenate([from_left[raw], left[raw], right[raw], from_right[raw]], axis=2)
    raw = _dot3(raw.reshape(96, 512), pick(384, 512, 0, 512))
    for h in range(4):
        y0[pl.ds(12 * h, 12)] = _tile(raw, h).reshape(12, 8, 128)
    level(0, None, 24, None, y0, 24, 128, rlow0, rhigh0, RIM_LOW0, RIM_HIGH0, 128)
    totals[0] = totals[0] + more_sums[...]
    for j in range(96):
        g, i = j // 24, j % 24
        mine = pltpu.roll(rlow0[i], 128 - 32 * g, 1) if g else rlow0[i]
        g, i = j // 6, 12 + j % 6
        theirs = jnp.where(lane // 8 == g, from_left[i], from_right[i])
        theirs = pltpu.roll(theirs, (32 - 8 * g) % 128, 1) if g != 4 else theirs
        rim[j] = jnp.where(lane < 32, mine, theirs)

    def load1(j, n):
        return jnp.concatenate([low0[pl.ds(j, n)], rim[pl.ds(j, n)]], axis=2)

    level(1, load1, 48, pick(0, 256, 0, 128), y1, 24, 128, r1l, r1h, RIM_LOW1, RIM_HIGH1, 64)
    for j in range(48):
        h, i = j // 24, 18 + j % 24
        b, a = from_left[i], from_right[i]
        if h == 0:
            a = pltpu.roll(a, 64, 1)
        else:
            b = pltpu.roll(b, 64, 1)
        x2[j, :, 0:128] = jnp.where(lane < 64, a1l[j], a)
        x2[j, :, 128:256] = jnp.where(lane < 64, b, r1l[j])
    level(2, lambda j, n: x2[pl.ds(j, n)], 24, pick(0, 256, 128, 128), y2, 24, 128, a2l, a2h, LOW2, HIGH2, 32)
    level(3, lambda j, n: a2l[pl.ds(j, n)], 12, pick(0, 128, 256, 128), y3, 24, 128, a3l, a3h, LOW3, HIGH3, 16)
    level(4, lambda j, n: a3l[pl.ds(j, n)], 6, pick(128, 128, 256, 128), y4, 12, 128, a4l, a4h, LOW4, HIGH4, 8)
    level(5, lambda j, n: a4l[pl.ds(j, n)], 3, pick(256, 128, 0, 256), y5, 6, 256, l5, h5, LOW5, HIGH5, 4)
    sub = _sublane(128)
    for j in range(3):
        a5l[j] = l5[j, :, 0:128]
        a5h[j] = h5[j, :, 0:128]
        flat[pl.ds(j, 8, stride=3), :] = jnp.where(lane % 16 < 7, l5[j, :, 128:256], h5[j, :, 128:256])
    sums = jnp.zeros((8, 128), F32)
    for l in range(LEVELS):
        sums = jnp.where(sub == l, jnp.sum(totals[l], axis=0, keepdims=True), sums)
    sums = jnp.where((lane == 16 * sub + 13) & (sub < LEVELS), jnp.sum(sums, axis=1, keepdims=True), 0.0)
    lines = []
    for h in range(2):
        mine = flat[pl.ds(pl.multiple_of(8 * core + 8 * h, 8), 8), :]
        mine = jnp.where(lane // 16 == sub, mine, 0.0)
        lines.append(jnp.sum(mine + sums if h == 0 else mine, axis=0, keepdims=True))
    block = jnp.where(sub % 2 == 0, lines[0], lines[1])
    for i in range(32):
        payload[pl.ds(8 * i, 8), :] = block


def _shrink(v, limit):
    return v - jnp.minimum(jnp.maximum(v, -limit), limit)


def _back_kernel(
    sc, mine, theirs, coarse_table, table, own_details, more_details, rim_details, w,
    out,
    gt, nears, cur, x5l, x5h, y5, y4, y3, y2, y1, c4, c3, c2, c1, c0, f0, f1, f2, yr, stage, sems,
):
    core, place = sc[0], sc[2]
    rlow0, rhigh0, r1l, r1h, a2l, a2h, a3l, a3h, a4l, a4h, a5l, a5h = _bands(rim_details)
    dhigh0, dlow0, dhigh1 = own_details.at[pl.ds(0, 96)], more_details.at[pl.ds(0, 96)], more_details.at[pl.ds(96, 96)]
    a1l, a1h = (own_details.at[pl.ds(96 + 48 * i, 48)] for i in range(2))
    lane = _lane()
    lane1 = _lane(1)
    sub = _sublane(128)
    for h in range(2):
        halves = [g[pl.ds(h, NT, stride=2), :] for g in (mine, theirs)]
        if h == 0:
            total = jnp.sum(halves[0] + halves[1], axis=0, keepdims=True)
        for c in range(2):
            gt[c, h] = jnp.transpose(jnp.where(core == c, halves[0], halves[1]))
    limits = []
    for l in range(LEVELS):
        entries = 3 * (C >> (l + 1)) * (S >> (l + 1))
        s = jnp.sum(jnp.where(lane1 == 16 * l + 13, total, 0.0), axis=1, keepdims=True)
        limits.append(jnp.sqrt(s * (1.0 / entries) + FLOOR))
    rows = [
        jnp.concatenate([gt[c, h, pl.ds(m, 8, stride=16), :] for m in range(4)], axis=1)
        for c in range(2)
        for h in range(2)
    ]
    coarse = _dot3(jnp.concatenate(rows, axis=0), lambda i: coarse_table[i, 0:512, :])
    highs = lax.broadcasted_iota(jnp.int32, (32, 512), 1) >= (S >> (LEVELS + COARSE))
    square = jnp.sum(jnp.where(highs, coarse * coarse, 0.0), axis=0, keepdims=True)
    square = jnp.sum(square, axis=1, keepdims=True)
    entries = (C >> LEVELS) * ((S >> LEVELS) - (S >> (LEVELS + COARSE)))
    limit = jnp.sqrt(square * (1.0 / entries) + FLOOR)
    coarse = jnp.where(highs, _shrink(coarse, limit), coarse)
    hi = coarse.astype(BF16)
    lo = (coarse - hi.astype(F32)).astype(BF16)
    for side, other in enumerate((jnp.maximum(place - 1, 0), jnp.minimum(place + 1, NT - 1))):
        for c in range(2):
            for h in range(2):
                row = pl.ds(2 * other + h, 1)
                line = jnp.broadcast_to(jnp.where(core == c, mine[row, :], theirs[row, :]), (8, 128))
                near = line
                for k in range(1, 8):
                    near = jnp.where(sub == k, pltpu.roll(line, 128 - 16 * k, 1), near)
                nears[side, pl.ds(16 * c + 8 * h, 8), :] = near
    for k in range(3):
        rows = pl.ds(8 * core + k, 8, stride=3)
        before, after = nears[0, rows, :], nears[1, rows, :]
        v = a5h[k]
        for at, near, shift in ((1, before, 122), (9, after, 2), (17, before, 7), (25, after, 15)):
            v = jnp.where((lane >= at) & (lane < at + 3), pltpu.roll(near, shift, 1), v)
        x5h[k] = v
        v = a5l[k]
        for at, near, shift in ((17, before, 13), (25, after, 21)):
            v = jnp.where((lane >= at) & (lane < at + 3), pltpu.roll(near, shift, 1), v)
        x5l[k] = v

    def nt(a, b):
        return lax.dot_general(a, b, (((1,), (1,)), ((), ())), preferred_element_type=F32)

    rows = pl.ds(512, 128)
    current = nt(hi, coarse_table[0, rows, :]) + nt(lo, coarse_table[0, rows, :]) + nt(hi, coarse_table[1, rows, :])
    cur[...] = pltpu.roll(current, (128 - 4 * (place % 4)) % 128, 1)

    def level(l, get_current, low, high, n, y, t, nxt, step, needed):
        tl = jnp.broadcast_to(limits[l] * (1.0 / KS), (8, 128))
        th = jnp.broadcast_to(limits[l] * KS, (8, 128))
        is_low = needed(lane)

        def get_low(k):
            return jnp.where(is_low, get_current(k), _shrink(low[k], tl))

        def store(j, m, value):
            nxt[pl.ds(j, m)] = value

        put = _Backward(y, t, store, step)
        _chan_inverse(get_low, lambda k: _shrink(high[k], th), n, _blocks(w, l), 128, put)

    def pick(r, k, c, n):
        return _table(table, (r, k), (c, n))

    level(
        5, lambda k: cur[pl.ds(8 * core + k, 8, stride=3), :], x5l, x5h, 3, y5, pick(768, 128, 0, 128), c4, 6, lambda i: i < 12
    )
    level(4, lambda k: c4[k], a4l, a4h, 6, y4, pick(640, 128, 128, 128), c3, 12, lambda i: i < 32)
    level(3, lambda k: c3[k], a3l, a3h, 12, y3, pick(640, 128, 0, 128), c2, 24, lambda i: i < 64)
    level(2, lambda k: c2[k], a2l, a2h, 24, y2, pick(512, 128, 0, 256), c1, 24, lambda i: i < 89)
    tl = jnp.broadcast_to(limits[1] * (1.0 / KS), (8, 256))
    th = jnp.broadcast_to(limits[1] * KS, (8, 256))
    lane2 = lax.broadcasted_iota(jnp.int32, (8, 256), 1)
    is_low1 = (lane2 < 64) | ((lane2 >= 192) & (lane2 < 208))

    def get_low1(k):
        v1 = jnp.concatenate([a1l[k], r1l[k]], axis=1)
        return jnp.where(is_low1, c1[k], _shrink(v1, tl))

    def get_high1(k):
        return _shrink(jnp.concatenate([a1h[k], r1h[k]], axis=1), th)

    def store1(j, m, value):
        c0[pl.ds(j, m)] = value

    put1 = _Backward(y1, pick(256, 256, 0, 256), store1, 24)
    _chan_inverse(get_low1, get_high1, 48, _blocks(w, 1), 256, put1)
    tl0 = jnp.broadcast_to(limits[0] * (1.0 / KS), (8, 128))
    th0 = jnp.broadcast_to(limits[0] * KS, (8, 256))
    group = lane // 32
    rim_low = lane % 32 < 8

    def get_low_rim(k):
        now = c0[k, :, 128:256]
        for q in range(1, 4):
            now = jnp.where(group == q, c0[24 * q + k, :, 128:256], now)
        return jnp.where(rim_low, now, _shrink(rlow0[k], tl0))

    def store_rim(j, m, value):
        for i in range(m):
            for q in range(4):
                v = pltpu.roll(value[i], 128 - 32 * q, 1) if q else value[i]
                f2[pl.ds(48 * q + j + i, 8, stride=SEG), :] = v

    put_rim = _Backward(yr, pick(768, 128, 128, 128), store_rim, 24)
    _chan_inverse(
        get_low_rim, lambda k: _shrink(rhigh0[k], th0[:, 0:128]), 24, _quarters(_blocks(w, 0)), 128, put_rim, _QuarterWrap()
    )

    def get_low0(k):
        return jnp.concatenate([c0[k, :, 0:128], _shrink(dlow0[k], tl0)], axis=1)

    def get_high0(k):
        return _shrink(jnp.concatenate([dhigh0[k], dhigh1[k]], axis=1), th0)

    def put0(j, value):
        for i, buf in enumerate((f0, f1)):
            buf[pl.ds(j, 8, stride=SEG), :] = _tile(value, i)

    _chan_inverse(get_low0, get_high0, 96, _blocks(w, 0), 256, put0)
    at_own = pl.multiple_of(core * HALO, 8)
    t = pick(0, 256, 0, 256)
    wide = _lane(128)
    copies = []
    for r in range(0, OWN, 128):
        rows = pl.ds(at_own + r, 128)
        done = pl.ds(r, 128)
        ends = f2[rows, :]
        v = _dot3(jnp.concatenate([f0[rows, :], f1[rows, :]], axis=1), t)
        stage[done, 0:128] = _tile(v, 0) + jnp.where(wide < 8, ends, 0.0)
        stage[done, 128:256] = _tile(v, 1) + jnp.where(wide >= 121, ends, 0.0)
        copies.append(pltpu.make_async_copy(stage.at[done], out.at[done], sems.at[r // 128]))
        copies[-1].start()
    for c in copies:
        c.wait()


VM = pl.BlockSpec(memory_space=pltpu.VMEM)
SM = pl.BlockSpec(memory_space=pltpu.SMEM)
ANY = pl.BlockSpec(memory_space=pl.ANY)
HBM = pl.BlockSpec(memory_space=pltpu.HBM)


def _call(kernel, name, limit, args, specs, outs, out_specs, scratch):
    args = [
        pltpu.with_memory_space_constraint(x, pltpu.HBM) if spec is HBM else x for x, spec in zip(args, specs)
    ]
    outs = [jax.ShapeDtypeStruct(s, F32) if isinstance(s, tuple) else s for s in outs]
    return pl.pallas_call(
        kernel,
        out_shape=[pltpu.HBM(s.shape, s.dtype) if spec is HBM else s for s, spec in zip(outs, out_specs)],
        in_specs=specs,
        out_specs=out_specs,
        scratch_shapes=[pltpu.VMEM(s, F32) if isinstance(s, tuple) else s for s in scratch],
        compiler_params=pltpu.CompilerParams(vmem_limit_bytes=limit << 20),
        name=name,
    )(*args)


def _shift(v, by):
    return lax.ppermute(v, "tm", [(i, (i + by) % NT) for i in range(NT)])


def shards(record, gauge_table, gauge_index):
    tables = _tables()
    core = lax.axis_index("chan")
    place = lax.axis_index("tm")
    variant = jnp.where(place == 0, 0, jnp.where(place == NT - 1, 2, 1))
    sc = jnp.stack([core, variant, place]).astype(jnp.int32)
    dma = pltpu.SemaphoreType.DMA
    recv = lax.ppermute(record, "chan", [(0, 1), (1, 0)])
    low, high, ends, own_table, w = _call(
        _load_kernel, "load", 12, (sc, record, gauge_table, gauge_index, tables["own"]),
        [SM] + [HBM] * 4,
        [(OWN, 128), (OWN, 128), (OWN, 128), jax.ShapeDtypeStruct((2, 384, 256), BF16), (LEVELS, 3, 8, 128)],
        [VM] * 5,
        [(OWN, 256), (LEVELS, GTAB), pltpu.VMEM((LEVELS, NBLK), jnp.int32), dma((7,))],
    )
    right, left, low0, a1l, fh, own_details, sums = _call(
        _own_kernel, "own", 12, (sc, recv, low, high, ends, own_table, w), [SM] + [VM] * 6,
        [(42, 8, 128), (42, 8, 128), (96, 8, 128), (48, 8, 128), (8 * SEG, 128), (192, 8, 128), (2, 8, 128)],
        [VM] * 7,
        [(8 * SEG, 128), (8 * SEG, 128), (96, 8, 128)],
    )
    from_left, from_right = _shift(right, 1), _shift(left, -1)
    rim_table, back_table, coarse_table, more_details, more_sums = _call(
        _aside_kernel, "aside", 6, (sc, fh, w, tables["rim"], tables["back"], tables["coarse"]),
        [SM, VM, VM, HBM, HBM, HBM],
        [jax.ShapeDtypeStruct((2, 896, 512), BF16), jax.ShapeDtypeStruct((2, 896, 256), BF16),
         jax.ShapeDtypeStruct((2, 640, 512), BF16), (192, 8, 128), (8, 128)],
        [VM] * 5,
        [dma((10,))],
    )
    rim_details, payload = _call(
        _rim_kernel, "rim", 16,
        (sc, right, left, from_left, from_right, low0, a1l, sums, more_sums, rim_table, w), [SM] + [VM] * 10,
        [(234, 8, 128), (256, 128)], [VM] * 2,
        [(96, 8, 128), (48, 8, 128), (96, 8, 128), (48, 8, 256), (48, 8, 128), (24, 8, 128), (12, 8, 128),
         (6, 8, 256), (3, 8, 256), (3, 8, 256), (24, 128)],
    )
    mine = lax.all_to_all(payload, "tm", split_axis=0, concat_axis=0, tiled=True)
    theirs = lax.ppermute(mine, "chan", [(0, 1), (1, 0)])
    (out,) = _call(
        _back_kernel, "back", 24, (sc, mine, theirs, coarse_table, back_table, own_details, more_details, rim_details, w),
        [SM] + [VM] * 8, [(OWN, 256)], [HBM],
        [
            (2, 2, 128, 128), (2, 32, 128), (32, 128), (3, 8, 128), (3, 8, 128),
            (6, 8, 128), (12, 8, 128), (24, 8, 128), (48, 8, 128), (96, 8, 256),
            (6, 8, 128), (12, 8, 128), (24, 8, 128), (48, 8, 256), (96, 8, 256),
            (8 * SEG, 128), (8 * SEG, 128), (8 * SEG, 128), (48, 8, 128), (OWN, 256), dma((8,)),
        ],
    )
    return out


def solution(mesh):
    return jax.shard_map(
        shards,
        mesh=mesh,
        in_specs=(P("chan", "tm"), P(), P()),
        out_specs=P("chan", "tm"),
        check_vma=False,
    )
```

```python
import functools

import jax
import jax.numpy as jnp
import ml_dtypes
import numpy as np
from jax import lax
from jax.experimental import pallas as pl
from jax.experimental.pallas import tpu as pltpu
from jax.sharding import PartitionSpec as P

LEVELS = 6
COARSE = 6
GTAB = 8
NBLK = 32
C = 2048
S = 32768
NT = 128
OWN = 1024
HALO = 512
SEG = 192
A1 = -1.586134342059924
B1 = -0.052980118572961
A2 = 0.882911075530934
B2 = 0.443506852043971
KS = 1.149604398860241
FLOOR = 1e-06
F32 = jnp.float32
BF16 = jnp.bfloat16


def _next(e):
    return np.concatenate((e[1:], e[-1:]))


def _prev(o):
    return np.concatenate((o[:1], o[:-1]))


def _lift(x):
    e, o = x[0::2], x[1::2]
    o = o + A1 * (e + _next(e))
    e = e + B1 * (_prev(o) + o)
    o = o + A2 * (e + _next(e))
    e = e + B2 * (_prev(o) + o)
    return KS * e, o / KS


def _unlift(low, high):
    e, o = low / KS, high * KS
    e = e - B2 * (_prev(o) + o)
    o = o - A2 * (e + _next(e))
    e = e - B1 * (_prev(o) + o)
    o = o - A1 * (e + _next(e))
    return np.stack((e, o), axis=1).reshape((2 * e.shape[0],) + e.shape[1:])


def _forward(inputs, lows, highs, rows, cols, start, stop, scale):
    pairs = list(lows) + list(highs)
    a = max(2 * min(pairs) - 16, start)
    b = min(2 * max(pairs) + 16, stop)
    low, high = _lift(np.eye(b - a))
    out = np.zeros((rows, cols))
    for band, places in ((low, lows), (high, highs)):
        for pair, col in places.items():
            if a <= 2 * pair < b:
                line = band[pair - a // 2]
                for i in np.nonzero(line)[0]:
                    out[inputs[a + int(i)], col] += scale * line[i]
    return out


def _inverse(lows, highs, outputs, rows, cols, start, stop, scale):
    a = max(2 * (min(outputs) // 2) - 16, start) // 2
    b = min(2 * (max(outputs) // 2) + 18, stop) // 2
    n = b - a
    eye, zero = np.eye(n), np.zeros((n, n))
    from_low, from_high = _unlift(eye, zero), _unlift(zero, eye)
    out = np.zeros((rows, cols))
    for sample, col in outputs.items():
        if 2 * a <= sample < 2 * b:
            for lines, places in ((from_low, lows), (from_high, highs)):
                line = lines[sample - 2 * a]
                for i in np.nonzero(line)[0]:
                    out[places[a + int(i)], col] += scale * line[i]
    return out


def _pair(m):
    hi = m.astype(ml_dtypes.bfloat16)
    lo = (m - hi.astype(np.float64)).astype(ml_dtypes.bfloat16)
    return np.stack((hi, lo))


def _run(first, last, at):
    return {k: at + k - first for k in range(first, last)}


OWN_LOW0 = _run(2, 126, 2)
OWN_HIGH0 = _run(2, 126, 130)
RIM_LOW0 = {**_run(-2, 2, 0), **_run(126, 130, 4)}
RIM_HIGH0 = {**_run(-2, 2, 8), **_run(126, 130, 12)}
RIM_IN0 = {**_run(-8, 0, 0), **_run(0, 8, 128), **_run(248, 256, 256), **_run(256, 264, 384)}
OWN_LOW1 = _run(3, 61, 3)
OWN_HIGH1 = _run(2, 61, 66)
RIM_LOW1 = {**_run(-3, 3, 64), **_run(61, 67, 70)}
RIM_HIGH1 = {**_run(-3, 2, 80), **_run(61, 67, 85)}
IN1 = {**OWN_LOW0, **{k: 128 + v for k, v in RIM_LOW0.items()}, **_run(-10, -2, 160), **_run(130, 138, 168)}
IN2 = {
    **OWN_LOW1, **_run(67, 125, 67), **_run(-61, -3, 131), **{k: 128 + v for k, v in RIM_LOW1.items()}
}
LOW2 = _run(-28, 61, 0)
HIGH2 = _run(-3, 36, 89)
LOW3 = _run(-12, 29, 0)
HIGH3 = _run(-3, 20, 64)
LOW4 = _run(-4, 13, 0)
HIGH4 = _run(-3, 12, 32)
LOW5 = _run(-4, 8, 0)
HIGH5 = _run(-4, 8, 16)


def _part(places, first, last):
    return {k: places[k] for k in range(first, last)}


def _edges(width):
    far = 1 << 20
    return ((0, far), (-far, far), (-far, width))


def _bundle(parts, rows, cols):
    out = np.zeros((rows, cols))
    for r, c, m in parts:
        out[r : r + m.shape[0], c : c + m.shape[1]] = m
    return _pair(out)


@functools.cache
def _tables():
    fw, inv = _forward, _inverse
    far = 1 << 20
    out = {}
    out["own"] = _bundle(
        (
            (0, 0, fw(_run(0, 256, 0), OWN_LOW0, OWN_HIGH0, 256, 256, -far, far, 1.0)),
            (256, 0, fw(OWN_LOW0, OWN_LOW1, OWN_HIGH1, 128, 128, -far, far, KS)),
        ),
        384,
        256,
    )
    rim, back = [], []
    for v in range(3):
        a, b = zip(*(_edges(256 >> l)[v] for l in range(LEVELS)))
        t5 = fw(LOW4, _part(LOW5, 0, 5), _part(HIGH5, 0, 5), 128, 256, a[5], b[5], KS)
        lows, highs = t5[:, 4:8].copy(), t5[:, 20:24].copy()
        sixteen = np.concatenate([lows, highs[:, 1:], lows[:, 1:], highs[:, 1:], np.zeros((128, 3))], axis=1)
        t5[:, 128:] = np.tile(sixteen, (1, 8))
        one = fw(RIM_IN0, RIM_LOW0, RIM_HIGH0, 512, 128, a[0], b[0], 1.0)
        rim0 = [sum(np.roll(one, (8 * (4 * g + h), 32 * g), (0, 1)) for g in range(4)) for h in range(4)]
        rim.append(
            _bundle(
                (
                    (0, 0, fw(IN1, RIM_LOW1, RIM_HIGH1, 256, 128, a[1], b[1], KS)),
                    (0, 128, fw(IN2, LOW2, HIGH2, 256, 128, a[2], b[2], KS)),
                    (0, 256, fw(LOW2, LOW3, HIGH3, 128, 128, a[3], b[3], KS)),
                    (128, 256, fw(LOW3, LOW4, HIGH4, 128, 128, a[4], b[4], KS)),
                    (256, 0, t5),
                    (384, 0, np.concatenate(rim0, axis=1)),
                ),
                896,
                512,
            )
        )
        low0 = {**OWN_LOW0, **{k: 256 + v for k, v in RIM_LOW0.items() if -2 <= k < 130}}
        high0 = {**OWN_HIGH0, **{k: 256 + v for k, v in RIM_HIGH0.items()}}
        low1 = {**OWN_LOW1, **{k: 128 + v for k, v in RIM_LOW1.items()}}
        high1 = {**OWN_HIGH1, **{k: 128 + v for k, v in RIM_HIGH1.items()}}
        full = inv(low0, high0, _run(0, 256, 0), 288, 256, a[0], b[0], 1.0)
        ends = np.zeros((128, 128))
        for i in range(32):
            for c in range(-7, 8):
                ends[i, c % 128] = full[256 + i, c % 256]
        ends = sum(np.roll(ends, (32 * g, 32 * g), (0, 1)) for g in range(4))
        s1 = inv(low1, high1, _part(IN1, -1, 130), 256, 256, a[1], b[1], 1.0 / KS)
        s1[:, 128:] = np.tile(s1[:, 128:160], (1, 4))
        back.append(
            _bundle(
                (
                    (0, 0, full[:256]),
                    (256, 0, s1),
                    (512, 0, inv(LOW2, HIGH2, _part(low1, -2, 67), 128, 256, a[2], b[2], 1.0 / KS)),
                    (640, 0, inv(LOW3, HIGH3, _part(LOW2, -2, 36), 128, 128, a[3], b[3], 1.0 / KS)),
                    (640, 128, inv(LOW4, HIGH4, _part(LOW3, -2, 20), 128, 128, a[4], b[4], 1.0 / KS)),
                    (768, 0, inv(LOW5, HIGH5, _part(LOW4, -2, 12), 128, 128, a[5], b[5], 1.0 / KS)),
                    (768, 128, ends),
                ),
                896,
                256,
            )
        )
    out["rim"], out["back"] = np.stack(rim), np.stack(back)
    n = S >> LEVELS
    bands = []
    current = np.eye(n)
    for _ in range(COARSE):
        current, high = _lift(current)
        bands.append(high)
    coarse = np.concatenate([current] + bands[::-1])
    order = (np.arange(n) % NT) * 4 + np.arange(n) // NT
    last = n >> COARSE
    current = np.eye(n)[:last]
    for step in range(COARSE):
        size = last << step
        current = _unlift(current, np.eye(n)[size : 2 * size])
    both = np.zeros((n + 640, n))
    both[:n] = (KS * coarse.T)[order]
    both[n + 4 : 2 * n + 4] = current / KS
    out["coarse"] = _pair(both)
    return out


def _mask(lane, places, first, last, base=0):
    lanes = sorted(v - base for k, v in places.items() if first <= k < last)
    out, i = None, 0
    while i < len(lanes):
        j = i
        while j + 1 < len(lanes) and lanes[j + 1] == lanes[j] + 1:
            j += 1
        hit = (lane >= lanes[i]) & (lane <= lanes[j])
        out = hit if out is None else out | hit
        i = j + 1
    return out


def _ones(hit):
    return jnp.where(hit, 1.0, 0.0)


def _dot3(x, t):
    hi = x.astype(BF16)
    lo = (x - hi.astype(F32)).astype(BF16)
    d = functools.partial(jnp.dot, preferred_element_type=F32)
    both = d(jnp.concatenate([hi, lo], axis=0), t(0))
    return both[: x.shape[0]] + both[x.shape[0] :] + d(hi, t(1))


def _time(load, t, y, step, j):
    x = load(j, step)
    y[pl.ds(j, step)] = _dot3(x.reshape(step * 8, x.shape[2]), t).reshape(step, 8, y.shape[2])


class _Forward:
    def __init__(self, load, t, y, step):
        self.load, self.t, self.y, self.step, self.done = load, t, y, step, 0

    def __call__(self, j):
        ahead = min(j + self.step, self.y.shape[0] - 1)
        while self.done <= ahead:
            _time(self.load, self.t, self.y, self.step, self.done)
            self.done += self.step
        return self.y[j]


class _Backward:
    def __init__(self, y, t, store, step):
        self.y, self.t, self.store, self.step, self.left = y, t, store, step, {}

    def __call__(self, j, value):
        self.y[j] = value
        chunk = j // self.step
        self.left[chunk] = self.left.get(chunk, self.step) - 1
        if not self.left[chunk]:
            x = self.y[pl.ds(chunk * self.step, self.step)]
            out = _dot3(x.reshape(self.step * 8, x.shape[2]), self.t)
            self.store(chunk * self.step, self.step, out.reshape(self.step, 8, out.shape[1]))


def _table(ref, rows, cols, *lead):
    r, c = pl.ds(*rows), pl.ds(*cols)
    return lambda i: ref[(*lead, i, r, c)]


def _sublane(lanes):
    return lax.broadcasted_iota(jnp.int32, (8, lanes), 0)


def _lane(rows=8):
    return lax.broadcasted_iota(jnp.int32, (rows, 128), 1)


def _wide(v, lanes):
    return v if lanes == 128 else jnp.concatenate([v] * (lanes // 128), axis=1)


class _QuarterWrap:
    def __init__(self):
        self.sub, self.group = _sublane(128), _lane() // 32

    def after(self, first, last):
        moved = pltpu.roll(first, 96, 1)
        moved = jnp.where(self.group == 3, pltpu.roll(moved, 7, 0), moved)
        return jnp.where((self.group == 3) & (self.sub == 7), last, moved)

    def before(self, last, first):
        moved = pltpu.roll(last, 32, 1)
        moved = jnp.where(self.group == 0, pltpu.roll(moved, 1, 0), moved)
        return jnp.where((self.group == 0) & (self.sub == 0), first, moved)


def _quarters(values):
    group = _lane() // 32
    out = []
    for c in range(3):
        v = values[0]
        for g in range(1, 4):
            v = jnp.where(group == g, values[(24 * g + 8 * c) // 32], v)
        out.append(v)
    return out


class _Wrap:
    def __init__(self, lanes):
        sub = _sublane(lanes)
        self.last, self.first = sub == 7, sub == 0

    def after(self, first, last):
        return jnp.where(self.last, last, pltpu.roll(first, 7, 0))

    def before(self, last, first):
        return jnp.where(self.first, first, pltpu.roll(last, 1, 0))


def _coefs(weights, lanes):
    return [[_wide(c * v, lanes) for v in weights] for c in (A1, B1, A2, B2)]


def _chan_forward(get, n, weights, lanes, put_low, put_high, wrap=None):
    wrap = wrap or _Wrap(lanes)
    ca, cb, cc, cd = _coefs(weights, lanes)
    per = n // 3
    first = get(0)
    e, o1, e1, o2 = {0: first}, {}, {}, {}

    def high(k, v):
        o2[k] = v
        put_high(k, k // per, v)

    def low(k):
        put_low(k, k // per, e1[k] + cd[k // per] * (o2[k - 1] + o2[k]))

    for k in range(n):
        q = k // per
        e[k + 1] = get(2 * k + 2) if k + 1 < n else wrap.after(first, e[k])
        o1[k] = get(2 * k + 1) + ca[q] * (e[k] + e[k + 1])
        if k >= 1:
            e1[k] = e[k] + cb[q] * (o1[k - 1] + o1[k])
        if k >= 2:
            high(k - 1, o1[k - 1] + cc[(k - 1) // per] * (e1[k - 1] + e1[k]))
        if k >= 3:
            low(k - 1)
    e1[0] = first + cb[0] * (wrap.before(o1[n - 1], o1[0]) + o1[0])
    high(0, o1[0] + cc[0] * (e1[0] + e1[1]))
    high(n - 1, o1[n - 1] + cc[2] * (e1[n - 1] + wrap.after(e1[0], e1[n - 1])))
    o2[-1] = wrap.before(o2[n - 1], o2[0])
    for k in (0, 1, n - 1):
        low(k)


def _chan_inverse(get_low, get_high, n, weights, lanes, put, wrap=None):
    wrap = wrap or _Wrap(lanes)
    ca, cb, cc, cd = _coefs(weights, lanes)
    per = n // 3
    o = {0: get_high(0)}
    o[-1] = wrap.before(get_high(n - 1), o[0])
    e1, o1, e2 = {}, {}, {}

    def even(k):
        e2[k] = e1[k] - cb[k // per] * (o1[k - 1] + o1[k])
        put(2 * k, e2[k])

    def odd(k):
        put(2 * k + 1, o1[k] - ca[k // per] * (e2[k] + e2[k + 1]))

    for k in range(n):
        q = k // per
        if k:
            o[k] = get_high(k)
        e1[k] = get_low(k) - cd[q] * (o[k - 1] + o[k])
        if k >= 1:
            o1[k - 1] = o[k - 1] - cc[(k - 1) // per] * (e1[k - 1] + e1[k])
        if k >= 2:
            even(k - 1)
        if k >= 3:
            odd(k - 2)
    o1[n - 1] = o[n - 1] - cc[2] * (e1[n - 1] + wrap.after(e1[0], e1[n - 1]))
    o1[-1] = wrap.before(o1[n - 1], o1[0])
    even(n - 1)
    if n > 2:
        odd(n - 2)
    even(0)
    odd(0)
    e2[n] = wrap.after(e2[0], e2[n - 1])
    odd(n - 1)


class _Squares:
    def __init__(self):
        self.acc = {}

    def add(self, key, v):
        self.acc[key] = v * v if key not in self.acc else self.acc[key] + v * v

    def total(self, rows, tiles):
        out = None
        for q in range(3):
            part = None
            for (band, tile), lanes in tiles.items():
                v = self.acc[(band, tile, q)] * (KS * KS if band == "low" else 1.0 / (KS * KS))
                v = v if lanes is None else v * lanes
                part = v if part is None else part + v
            part = part * rows[q]
            out = part if out is None else out + part
        return out


def _tile(v, i):
    return v[:, 128 * i : 128 * (i + 1)]


def _blocks(w, level):
    return [w[level, q] for q in range(3)]


def _own_rows(core):
    block = 3 * _sublane(128)
    return [
        jnp.where(core == 0, _ones(block + q < 16), _ones(block + q >= 8)) for q in range(3)
    ]


def _load_kernel(
    sc, x_all, gauge_table_all, gauge_index_all, own_all,
    low, high, ends, own_table, w,
    x, gauge_table, gauge_index, sems,
):
    core = sc[0]
    copies = [
        pltpu.make_async_copy(src, dst, sems.at[i])
        for i, (src, dst) in enumerate(
            (
                (gauge_index_all, gauge_index),
                (gauge_table_all, gauge_table),
                (own_all, own_table),
                *((x_all.at[pl.ds(256 * i, 256)], x.at[pl.ds(256 * i, 256)]) for i in range(4)),
            )
        )
    ]
    for c in copies:
        c.start()
    for c in copies[:2]:
        c.wait()
    index = gauge_index[...]
    table_rows = gauge_table[...]
    weights = jnp.zeros(index.shape, F32)
    for g in range(GTAB):
        weights = weights + jnp.where(index == g, table_rows[:, g : g + 1], 0.0)
    block = lax.broadcasted_iota(jnp.int32, (8, NBLK), 1) - 3 * lax.broadcasted_iota(jnp.int32, (8, NBLK), 0)
    block = block - 8 * core
    for l in range(LEVELS):
        for q in range(3):
            hit = jnp.where(block == q, weights[l : l + 1], 0.0)
            w[l, q] = jnp.broadcast_to(jnp.sum(hit, axis=1, keepdims=True), (8, 128))
    copies[2].wait()
    for i in range(4):
        copies[3 + i].wait()
        _first(x, own_table, low, high, ends, 0, range(256 * i, 256 * i + 256, 128))


def _first(x, table, low, high, ends, at, blocks):
    lane = _lane(128)
    for r in blocks:
        v = x[pl.ds(r, 128), :]
        y = _dot3(v, _table(table, (0, 256), (0, 256)))
        rows = pl.ds(at + r, 128)
        low[rows, :] = y[:, 0:128]
        high[rows, :] = y[:, 128:256]
        ends[rows, :] = jnp.where(lane < 32, v[:, 0:128], v[:, 128:256])


def _own_kernel(
    sc, recv, own_low, own_high, own_ends, table, w,
    right, left, low0, a1l, fh, details, sums,
    fl, fe, y1,
):
    core = sc[0]
    at_own = pl.multiple_of(core * HALO, 8)
    at_recv = pl.multiple_of((1 - core) * OWN, 8)
    for src, dst in ((own_low, fl), (own_high, fh), (own_ends, fe)):
        for r in range(0, OWN, 128):
            dst[pl.ds(at_own + r, 128), :] = src[pl.ds(r, 128), :]
    theirs = recv.at[pl.ds(at_own, HALO)]
    _first(theirs, table, fl, fh, fe, at_recv, range(0, HALO, 128))
    lane = _lane()
    group = lane // 8
    for i in range(12):
        to_right, to_left = None, None
        for g in range(16):
            v = fe[pl.ds(12 * g + i, 8, stride=SEG), :]
            a = pltpu.roll(v, 8 * g, 1) if g else v
            b = pltpu.roll(v, (8 * g + 8) % 128, 1) if g != 15 else v
            to_left = a if to_left is None else jnp.where(group == g, a, to_left)
            to_right = b if to_right is None else jnp.where(group == g, b, to_right)
        right[i] = to_right
        left[i] = to_left
    rows = _own_rows(core)
    sq = _Squares()

    def put_low(k, q, v):
        low0[k] = v

    def put_high(k, q, v):
        details[k] = v
        sq.add(("high", 0, q), v)

    _chan_forward(lambda j: fl[pl.ds(j, 8, stride=SEG), :], 96, _blocks(w, 0), 128, put_low, put_high)
    sums[0] = sq.total(rows, {("high", 0): None})
    for i in range(6):
        to_right, to_left = None, None
        for g in range(16):
            v = low0[6 * g + i]
            a = pltpu.roll(v, (8 * g - 118) % 128, 1)
            b = pltpu.roll(v, (8 * g + 6) % 128, 1)
            to_right = a if to_right is None else jnp.where(group == g, a, to_right)
            to_left = b if to_left is None else jnp.where(group == (g + 1) % 16, b, to_left)
        right[12 + i] = to_right
        left[12 + i] = to_left
    sq1 = _Squares()

    def put_low1(k, q, v):
        a1l[k] = v
        details[96 + k] = v
        sq1.add(("low", 0, q), v)
        if k >= 26:
            packed = jnp.where(lane < 64, a1l[k - 24], pltpu.roll(v, 64, 1))
            right[k - 6] = packed
            left[k - 6] = packed

    def put_high1(k, q, v):
        details[144 + k] = v
        sq1.add(("high", 0, q), v)

    get = _Forward(lambda j, n: low0[pl.ds(j, n)], _table(table, (256, 128), (0, 128)), y1, 24)
    _chan_forward(get, 48, _blocks(w, 1), 128, put_low1, put_high1)
    for k in (24, 25):
        packed = jnp.where(lane < 64, a1l[k - 24], pltpu.roll(a1l[k], 64, 1))
        right[k - 6] = packed
        left[k - 6] = packed
    sums[1] = sq1.total(rows, {("low", 0): _ones(_mask(lane, OWN_HIGH1, 0, 64)), ("high", 0): None})


def _bands(details):
    out, at = [], 0
    for n in (24, 48, 24, 12, 6, 3):
        out += [details.at[pl.ds(at, n)], details.at[pl.ds(at + n, n)]]
        at += 2 * n
    return out


def _aside_kernel(
    sc, fh, w, rim_all, back_all, coarse_all, rim_table, back_table, coarse_table, details, sums, sems
):
    copies = []
    mine = pl.multiple_of(512 + 16 * (sc[2] // 4), 16)
    for i in range(2):
        for src, dst, start, n in (
            (rim_all.at[sc[1], i], rim_table.at[i], 0, 448),
            (rim_all.at[sc[1], i], rim_table.at[i], 448, 448),
            (back_all.at[sc[1], i], back_table.at[i], 0, 896),
            (coarse_all.at[i], coarse_table.at[i], 0, 512),
        ):
            rows = pl.ds(start, n)
            copies.append(pltpu.make_async_copy(src.at[rows], dst.at[rows], sems.at[len(copies)]))
        src, dst = coarse_all.at[i, pl.ds(mine, 128)], coarse_table.at[i, pl.ds(512, 128)]
        copies.append(pltpu.make_async_copy(src, dst, sems.at[len(copies)]))
    for c in copies:
        c.start()
    rows = _own_rows(sc[0])
    sq = _Squares()

    def put_low(k, q, v):
        details[k] = v
        sq.add(("low", 0, q), v)

    def put_high(k, q, v):
        details[96 + k] = v
        sq.add(("high", 0, q), v)

    _chan_forward(lambda j: fh[pl.ds(j, 8, stride=SEG), :], 96, _blocks(w, 0), 128, put_low, put_high)
    sums[...] = sq.total(rows, {("low", 0): None, ("high", 0): None})
    for c in copies:
        c.wait()


def _rim_kernel(
    sc, right, left, from_left, from_right, low0, a1l, own_sums, more_sums, table, w,
    details, payload,
    rim, y0, y1, x2, y2, y3, y4, y5, l5, h5, flat,
):
    core = sc[0]
    rlow0, rhigh0, r1l, r1h, a2l, a2h, a3l, a3h, a4l, a4h, a5l, a5h = _bands(details)
    lane = _lane()
    rows = _own_rows(core)
    totals = []

    def level(l, load, n, t, y, step, lanes, low, high, own_low, own_high, pairs):
        quarters = l == 0
        weights = _blocks(w, l)
        place = lane % 32 if quarters else lane
        sq = _Squares()

        def put_low(k, q, value):
            low[k] = value
            sq.add(("low", 0, q), _tile(value, 0))

        def put_high(k, q, value):
            high[k] = value
            sq.add(("high", 0, q), _tile(value, 0))

        wrap = _QuarterWrap() if quarters else None
        weights = _quarters(weights) if quarters else weights
        get = y.__getitem__ if quarters else _Forward(load, t, y, step)
        _chan_forward(get, n, weights, lanes, put_low, put_high, wrap)
        is_high = _mask(place, own_high, 0, pairs)
        is_low = _mask(place, own_low, 0, pairs)
        total = sq.total(_quarters(rows) if quarters else rows, {("low", 0): _ones(is_high), ("high", 0): _ones(is_high | is_low)})
        totals.append(total + own_sums[l] if l < 2 else total)

    def pick(r, k, c, n):
        return _table(table, (r, k), (c, n))

    raw = pl.ds(0, 12)
    raw = jnp.concatenate([from_left[raw], left[raw], right[raw], from_right[raw]], axis=2)
    raw = _dot3(raw.reshape(96, 512), pick(384, 512, 0, 512))
    for h in range(4):
        y0[pl.ds(12 * h, 12)] = _tile(raw, h).reshape(12, 8, 128)
    level(0, None, 24, None, y0, 24, 128, rlow0, rhigh0, RIM_LOW0, RIM_HIGH0, 128)
    totals[0] = totals[0] + more_sums[...]
    for j in range(96):
        g, i = j // 24, j % 24
        mine = pltpu.roll(rlow0[i], 128 - 32 * g, 1) if g else rlow0[i]
        g, i = j // 6, 12 + j % 6
        theirs = jnp.where(lane // 8 == g, from_left[i], from_right[i])
        theirs = pltpu.roll(theirs, (32 - 8 * g) % 128, 1) if g != 4 else theirs
        rim[j] = jnp.where(lane < 32, mine, theirs)

    def load1(j, n):
        return jnp.concatenate([low0[pl.ds(j, n)], rim[pl.ds(j, n)]], axis=2)

    level(1, load1, 48, pick(0, 256, 0, 128), y1, 24, 128, r1l, r1h, RIM_LOW1, RIM_HIGH1, 64)
    for j in range(48):
        h, i = j // 24, 18 + j % 24
        b, a = from_left[i], from_right[i]
        if h == 0:
            a = pltpu.roll(a, 64, 1)
        else:
            b = pltpu.roll(b, 64, 1)
        x2[j, :, 0:128] = jnp.where(lane < 64, a1l[j], a)
        x2[j, :, 128:256] = jnp.where(lane < 64, b, r1l[j])
    level(2, lambda j, n: x2[pl.ds(j, n)], 24, pick(0, 256, 128, 128), y2, 24, 128, a2l, a2h, LOW2, HIGH2, 32)
    level(3, lambda j, n: a2l[pl.ds(j, n)], 12, pick(0, 128, 256, 128), y3, 24, 128, a3l, a3h, LOW3, HIGH3, 16)
    level(4, lambda j, n: a3l[pl.ds(j, n)], 6, pick(128, 128, 256, 128), y4, 12, 128, a4l, a4h, LOW4, HIGH4, 8)
    level(5, lambda j, n: a4l[pl.ds(j, n)], 3, pick(256, 128, 0, 256), y5, 6, 256, l5, h5, LOW5, HIGH5, 4)
    sub = _sublane(128)
    for j in range(3):
        a5l[j] = l5[j, :, 0:128]
        a5h[j] = h5[j, :, 0:128]
        flat[pl.ds(j, 8, stride=3), :] = jnp.where(lane % 16 < 7, l5[j, :, 128:256], h5[j, :, 128:256])
    sums = jnp.zeros((8, 128), F32)
    for l in range(LEVELS):
        sums = jnp.where(sub == l, jnp.sum(totals[l], axis=0, keepdims=True), sums)
    sums = jnp.where((lane == 16 * sub + 13) & (sub < LEVELS), jnp.sum(sums, axis=1, keepdims=True), 0.0)
    lines = []
    for h in range(2):
        mine = flat[pl.ds(pl.multiple_of(8 * core + 8 * h, 8), 8), :]
        mine = jnp.where(lane // 16 == sub, mine, 0.0)
        lines.append(jnp.sum(mine + sums if h == 0 else mine, axis=0, keepdims=True))
    block = jnp.where(sub % 2 == 0, lines[0], lines[1])
    for i in range(32):
        payload[pl.ds(8 * i, 8), :] = block


def _shrink(v, limit):
    return v - jnp.minimum(jnp.maximum(v, -limit), limit)


def _back_kernel(
    sc, mine, theirs, coarse_table, table, own_details, more_details, rim_details, w,
    out,
    both, gt, nears, cur, x5l, x5h, y5, y4, y3, y2, y1, c4, c3, c2, c1, c0, f0, f1, f2, yr, stage, sems,
):
    core, place = sc[0], sc[2]
    rlow0, rhigh0, r1l, r1h, a2l, a2h, a3l, a3h, a4l, a4h, a5l, a5h = _bands(rim_details)
    dhigh0, dlow0, dhigh1 = own_details.at[pl.ds(0, 96)], more_details.at[pl.ds(0, 96)], more_details.at[pl.ds(96, 96)]
    a1l, a1h = (own_details.at[pl.ds(96 + 48 * i, 48)] for i in range(2))
    lane = _lane()
    lane1 = _lane(1)
    sub = _sublane(128)
    both[0, 0:256, :] = mine[...]
    both[1, 0:256, :] = theirs[...]
    for h in range(2):
        halves = [both[g, pl.ds(h, NT, stride=2), :] for g in range(2)]
        if h == 0:
            total = jnp.sum(halves[0] + halves[1], axis=0, keepdims=True)
        for c in range(2):
            gt[c, h, 0:128, :] = jnp.transpose(jnp.where(core == c, halves[0], halves[1]))
    limits = []
    for l in range(LEVELS):
        entries = 3 * (C >> (l + 1)) * (S >> (l + 1))
        s = jnp.sum(jnp.where(lane1 == 16 * l + 13, total, 0.0), axis=1, keepdims=True)
        limits.append(jnp.sqrt(s * (1.0 / entries) + FLOOR))
    rows = [
        jnp.concatenate([gt[c, h, pl.ds(m, 8, stride=16), :] for m in range(4)], axis=1)
        for c in range(2)
        for h in range(2)
    ]
    coarse = _dot3(jnp.concatenate(rows, axis=0), lambda i: coarse_table[i, 0:512, :])
    highs = lax.broadcasted_iota(jnp.int32, (32, 512), 1) >= (S >> (LEVELS + COARSE))
    square = jnp.sum(jnp.where(highs, coarse * coarse, 0.0), axis=0, keepdims=True)
    square = jnp.sum(square, axis=1, keepdims=True)
    entries = (C >> LEVELS) * ((S >> LEVELS) - (S >> (LEVELS + COARSE)))
    limit = jnp.sqrt(square * (1.0 / entries) + FLOOR)
    coarse = jnp.where(highs, _shrink(coarse, limit), coarse)
    hi = coarse.astype(BF16)
    lo = (coarse - hi.astype(F32)).astype(BF16)
    for side, other in enumerate((jnp.maximum(place - 1, 0), jnp.minimum(place + 1, NT - 1))):
        for c in range(2):
            for h in range(2):
                row = pl.ds(2 * other + h, 1)
                line = jnp.broadcast_to(jnp.where(core == c, mine[row, :], theirs[row, :]), (8, 128))
                near = line
                for k in range(1, 8):
                    near = jnp.where(sub == k, pltpu.roll(line, 128 - 16 * k, 1), near)
                nears[side, pl.ds(16 * c + 8 * h, 8), :] = near
    for k in range(3):
        rows = pl.ds(8 * core + k, 8, stride=3)
        before, after = nears[0, rows, :], nears[1, rows, :]
        v = a5h[k]
        for at, near, shift in ((1, before, 122), (9, after, 2), (17, before, 7), (25, after, 15)):
            v = jnp.where((lane >= at) & (lane < at + 3), pltpu.roll(near, shift, 1), v)
        x5h[k] = v
        v = a5l[k]
        for at, near, shift in ((17, before, 13), (25, after, 21)):
            v = jnp.where((lane >= at) & (lane < at + 3), pltpu.roll(near, shift, 1), v)
        x5l[k] = v

    def nt(a, b):
        return lax.dot_general(a, b, (((1,), (1,)), ((), ())), preferred_element_type=F32)

    rows = pl.ds(512, 128)
    current = nt(hi, coarse_table[0, rows, :]) + nt(lo, coarse_table[0, rows, :]) + nt(hi, coarse_table[1, rows, :])
    cur[0:32, :] = pltpu.roll(current, (128 - 4 * (place % 4)) % 128, 1)

    def level(l, get_current, low, high, n, y, t, nxt, step, needed):
        tl = jnp.broadcast_to(limits[l] * (1.0 / KS), (8, 128))
        th = jnp.broadcast_to(limits[l] * KS, (8, 128))
        is_low = needed(lane)

        def get_low(k):
            return jnp.where(is_low, get_current(k), _shrink(low[k], tl))

        def store(j, m, value):
            nxt[pl.ds(j, m)] = value

        put = _Backward(y, t, store, step)
        _chan_inverse(get_low, lambda k: _shrink(high[k], th), n, _blocks(w, l), 128, put)

    def pick(r, k, c, n):
        return _table(table, (r, k), (c, n))

    level(
        5, lambda k: cur[pl.ds(8 * core + k, 8, stride=3), :], x5l, x5h, 3, y5, pick(768, 128, 0, 128), c4, 6, lambda i: i < 12
    )
    level(4, lambda k: c4[k], a4l, a4h, 6, y4, pick(640, 128, 128, 128), c3, 12, lambda i: i < 32)
    level(3, lambda k: c3[k], a3l, a3h, 12, y3, pick(640, 128, 0, 128), c2, 24, lambda i: i < 64)
    level(2, lambda k: c2[k], a2l, a2h, 24, y2, pick(512, 128, 0, 256), c1, 24, lambda i: i < 89)
    tl = jnp.broadcast_to(limits[1] * (1.0 / KS), (8, 256))
    th = jnp.broadcast_to(limits[1] * KS, (8, 256))
    lane2 = lax.broadcasted_iota(jnp.int32, (8, 256), 1)
    is_low1 = (lane2 < 64) | ((lane2 >= 192) & (lane2 < 208))

    def get_low1(k):
        v1 = jnp.concatenate([a1l[k], r1l[k]], axis=1)
        return jnp.where(is_low1, c1[k], _shrink(v1, tl))

    def get_high1(k):
        return _shrink(jnp.concatenate([a1h[k], r1h[k]], axis=1), th)

    def store1(j, m, value):
        c0[pl.ds(j, m)] = value

    put1 = _Backward(y1, pick(256, 256, 0, 256), store1, 24)
    _chan_inverse(get_low1, get_high1, 48, _blocks(w, 1), 256, put1)
    tl0 = jnp.broadcast_to(limits[0] * (1.0 / KS), (8, 128))
    th0 = jnp.broadcast_to(limits[0] * KS, (8, 256))
    group = lane // 32
    rim_low = lane % 32 < 8

    def get_low_rim(k):
        now = c0[k, :, 128:256]
        for q in range(1, 4):
            now = jnp.where(group == q, c0[24 * q + k, :, 128:256], now)
        return jnp.where(rim_low, now, _shrink(rlow0[k], tl0))

    def store_rim(j, m, value):
        for i in range(m):
            for q in range(4):
                v = pltpu.roll(value[i], 128 - 32 * q, 1) if q else value[i]
                f2[pl.ds(48 * q + j + i, 8, stride=SEG), :] = v

    put_rim = _Backward(yr, pick(768, 128, 128, 128), store_rim, 24)
    _chan_inverse(
        get_low_rim, lambda k: _shrink(rhigh0[k], th0[:, 0:128]), 24, _quarters(_blocks(w, 0)), 128, put_rim, _QuarterWrap()
    )

    def get_low0(k):
        return jnp.concatenate([c0[k, :, 0:128], _shrink(dlow0[k], tl0)], axis=1)

    def get_high0(k):
        return _shrink(jnp.concatenate([dhigh0[k], dhigh1[k]], axis=1), th0)

    def put0(j, value):
        for i, buf in enumerate((f0, f1)):
            buf[pl.ds(j, 8, stride=SEG), :] = _tile(value, i)

    _chan_inverse(get_low0, get_high0, 96, _blocks(w, 0), 256, put0)
    at_own = pl.multiple_of(core * HALO, 8)
    t = pick(0, 256, 0, 256)
    wide = _lane(128)
    copies = []
    for r in range(0, OWN, 128):
        rows = pl.ds(at_own + r, 128)
        done = pl.ds(r, 128)
        ends = f2[rows, :]
        v = _dot3(jnp.concatenate([f0[rows, :], f1[rows, :]], axis=1), t)
        stage[done, 0:128] = _tile(v, 0) + jnp.where(wide < 8, ends, 0.0)
        stage[done, 128:256] = _tile(v, 1) + jnp.where(wide >= 121, ends, 0.0)
        copies.append(pltpu.make_async_copy(stage.at[done], out.at[done], sems.at[r // 128]))
        copies[-1].start()
    for c in copies:
        c.wait()


VM = pl.BlockSpec(memory_space=pltpu.VMEM)
SM = pl.BlockSpec(memory_space=pltpu.SMEM)
HBM = pl.BlockSpec(memory_space=pltpu.HBM)
ROWS = (9 * SEG, 128)


def _call(kernel, name, limit, args, specs, outs, out_specs, scratch):
    args = [
        pltpu.with_memory_space_constraint(x, pltpu.HBM) if spec is HBM else x for x, spec in zip(args, specs)
    ]
    outs = [jax.ShapeDtypeStruct(s, F32) if isinstance(s, tuple) else s for s in outs]
    return pl.pallas_call(
        kernel,
        out_shape=[pltpu.HBM(s.shape, s.dtype) if spec is HBM else s for s, spec in zip(outs, out_specs)],
        in_specs=specs,
        out_specs=out_specs,
        scratch_shapes=[pltpu.VMEM(s, F32) if isinstance(s, tuple) else s for s in scratch],
        compiler_params=pltpu.CompilerParams(vmem_limit_bytes=limit << 20),
        name=name,
    )(*args)


def _shift(v, by):
    return lax.ppermute(v, "tm", [(i, (i + by) % NT) for i in range(NT)])


def shards(record, gauge_table, gauge_index):
    tables = _tables()
    core = lax.axis_index("chan")
    place = lax.axis_index("tm")
    variant = jnp.where(place == 0, 0, jnp.where(place == NT - 1, 2, 1))
    sc = jnp.stack([core, variant, place]).astype(jnp.int32)
    dma = pltpu.SemaphoreType.DMA
    recv = lax.ppermute(record, "chan", [(0, 1), (1, 0)])
    low, high, ends, own_table, w = _call(
        _load_kernel, "load", 12, (sc, record, gauge_table, gauge_index, tables["own"]),
        [SM] + [HBM] * 4,
        [(OWN, 128), (OWN, 128), (OWN, 128), jax.ShapeDtypeStruct((2, 384, 256), BF16), (LEVELS, 3, 8, 128)],
        [VM] * 5,
        [(OWN, 256), (LEVELS, GTAB), pltpu.VMEM((LEVELS, NBLK), jnp.int32), dma((7,))],
    )
    right, left, low0, a1l, fh, own_details, sums = _call(
        _own_kernel, "own", 12, (sc, recv, low, high, ends, own_table, w), [SM] + [VM] * 6,
        [(42, 8, 128), (42, 8, 128), (96, 8, 128), (48, 8, 128), ROWS, (192, 8, 128), (2, 8, 128)],
        [VM] * 7,
        [ROWS, ROWS, (96, 8, 128)],
    )
    from_left, from_right = _shift(right, 1), _shift(left, -1)
    rim_table, back_table, coarse_table, more_details, more_sums = _call(
        _aside_kernel, "aside", 6, (sc, fh, w, tables["rim"], tables["back"], tables["coarse"]),
        [SM, VM, VM, HBM, HBM, HBM],
        [jax.ShapeDtypeStruct((2, 896, 512), BF16), jax.ShapeDtypeStruct((2, 896, 256), BF16),
         jax.ShapeDtypeStruct((2, 640, 512), BF16), (192, 8, 128), (8, 128)],
        [VM] * 5,
        [dma((10,))],
    )
    rim_details, payload = _call(
        _rim_kernel, "rim", 16,
        (sc, right, left, from_left, from_right, low0, a1l, sums, more_sums, rim_table, w), [SM] + [VM] * 10,
        [(234, 8, 128), (256, 128)], [VM] * 2,
        [(96, 8, 128), (48, 8, 128), (96, 8, 128), (48, 8, 256), (48, 8, 128), (24, 8, 128), (12, 8, 128),
         (6, 8, 256), (3, 8, 256), (3, 8, 256), (32, 128)],
    )
    mine = lax.all_to_all(payload, "tm", split_axis=0, concat_axis=0, tiled=True)
    theirs = lax.ppermute(mine, "chan", [(0, 1), (1, 0)])
    (out,) = _call(
        _back_kernel, "back", 24, (sc, mine, theirs, coarse_table, back_table, own_details, more_details, rim_details, w),
        [SM] + [VM] * 8, [(OWN, 256)], [HBM],
        [
            (2, 264, 128), (2, 2, 144, 128), (2, 40, 128), (40, 128), (3, 8, 128), (3, 8, 128),
            (6, 8, 128), (12, 8, 128), (24, 8, 128), (48, 8, 128), (96, 8, 256),
            (6, 8, 128), (12, 8, 128), (24, 8, 128), (48, 8, 256), (96, 8, 256),
            ROWS, ROWS, ROWS, (48, 8, 128), (OWN, 256), dma((8,)),
        ],
    )
    return out


def solution(mesh):
    return jax.shard_map(
        shards,
        mesh=mesh,
        in_specs=(P("chan", "tm"), P(), P()),
        out_specs=P("chan", "tm"),
        check_vma=False,
    )
```

```python
import functools

import jax
import jax.numpy as jnp
import ml_dtypes
import numpy as np
from jax import lax
from jax.experimental import pallas as pl
from jax.experimental.pallas import tpu as pltpu
from jax.sharding import PartitionSpec as P

LEVELS = 6
COARSE = 6
GTAB = 8
NBLK = 32
C = 2048
S = 32768
NT = 128
OWN = 1024
HALO = 512
SEG = 192
A1 = -1.586134342059924
B1 = -0.052980118572961
A2 = 0.882911075530934
B2 = 0.443506852043971
KS = 1.149604398860241
FLOOR = 1e-06
F32 = jnp.float32
BF16 = jnp.bfloat16


def _next(e):
    return np.concatenate((e[1:], e[-1:]))


def _prev(o):
    return np.concatenate((o[:1], o[:-1]))


def _lift(x):
    e, o = x[0::2], x[1::2]
    o = o + A1 * (e + _next(e))
    e = e + B1 * (_prev(o) + o)
    o = o + A2 * (e + _next(e))
    e = e + B2 * (_prev(o) + o)
    return KS * e, o / KS


def _unlift(low, high):
    e, o = low / KS, high * KS
    e = e - B2 * (_prev(o) + o)
    o = o - A2 * (e + _next(e))
    e = e - B1 * (_prev(o) + o)
    o = o - A1 * (e + _next(e))
    return np.stack((e, o), axis=1).reshape((2 * e.shape[0],) + e.shape[1:])


def _forward(inputs, lows, highs, rows, cols, start, stop, scale):
    pairs = list(lows) + list(highs)
    a = max(2 * min(pairs) - 16, start)
    b = min(2 * max(pairs) + 16, stop)
    low, high = _lift(np.eye(b - a))
    out = np.zeros((rows, cols))
    for band, places in ((low, lows), (high, highs)):
        for pair, col in places.items():
            if a <= 2 * pair < b:
                line = band[pair - a // 2]
                for i in np.nonzero(line)[0]:
                    out[inputs[a + int(i)], col] += scale * line[i]
    return out


def _inverse(lows, highs, outputs, rows, cols, start, stop, scale):
    a = max(2 * (min(outputs) // 2) - 16, start) // 2
    b = min(2 * (max(outputs) // 2) + 18, stop) // 2
    n = b - a
    eye, zero = np.eye(n), np.zeros((n, n))
    from_low, from_high = _unlift(eye, zero), _unlift(zero, eye)
    out = np.zeros((rows, cols))
    for sample, col in outputs.items():
        if 2 * a <= sample < 2 * b:
            for lines, places in ((from_low, lows), (from_high, highs)):
                line = lines[sample - 2 * a]
                for i in np.nonzero(line)[0]:
                    out[places[a + int(i)], col] += scale * line[i]
    return out


def _pair(m):
    hi = m.astype(ml_dtypes.bfloat16)
    lo = (m - hi.astype(np.float64)).astype(ml_dtypes.bfloat16)
    return np.stack((hi, lo))


def _run(first, last, at):
    return {k: at + k - first for k in range(first, last)}


OWN_LOW0 = _run(2, 126, 2)
OWN_HIGH0 = _run(2, 126, 130)
RIM_LOW0 = {**_run(-2, 2, 0), **_run(126, 130, 4)}
RIM_HIGH0 = {**_run(-2, 2, 8), **_run(126, 130, 12)}
RIM_IN0 = {**_run(-8, 0, 0), **_run(0, 8, 128), **_run(248, 256, 256), **_run(256, 264, 384)}
OWN_LOW1 = _run(3, 61, 3)
OWN_HIGH1 = _run(2, 61, 66)
RIM_LOW1 = {**_run(-3, 3, 64), **_run(61, 67, 70)}
RIM_HIGH1 = {**_run(-3, 2, 80), **_run(61, 67, 85)}
IN1 = {**OWN_LOW0, **{k: 128 + v for k, v in RIM_LOW0.items()}, **_run(-10, -2, 160), **_run(130, 138, 168)}
IN2 = {
    **OWN_LOW1, **_run(67, 125, 67), **_run(-61, -3, 131), **{k: 128 + v for k, v in RIM_LOW1.items()}
}
LOW2 = _run(-28, 61, 0)
HIGH2 = _run(-3, 36, 89)
LOW3 = _run(-12, 29, 0)
HIGH3 = _run(-3, 20, 64)
LOW4 = _run(-4, 13, 0)
HIGH4 = _run(-3, 12, 32)
LOW5 = _run(-4, 8, 0)
HIGH5 = _run(-4, 8, 16)


def _part(places, first, last):
    return {k: places[k] for k in range(first, last)}


def _edges(width):
    far = 1 << 20
    return ((0, far), (-far, far), (-far, width))


def _bundle(parts, rows, cols):
    out = np.zeros((rows, cols))
    for r, c, m in parts:
        out[r : r + m.shape[0], c : c + m.shape[1]] = m
    return _pair(out)


@functools.cache
def _tables():
    fw, inv = _forward, _inverse
    far = 1 << 20
    out = {}
    out["own"] = _bundle(
        (
            (0, 0, fw(_run(0, 256, 0), OWN_LOW0, OWN_HIGH0, 256, 256, -far, far, 1.0)),
            (256, 0, fw(OWN_LOW0, OWN_LOW1, OWN_HIGH1, 128, 128, -far, far, KS)),
        ),
        384,
        256,
    )
    rim, back = [], []
    for v in range(3):
        a, b = zip(*(_edges(256 >> l)[v] for l in range(LEVELS)))
        t5 = fw(LOW4, _part(LOW5, 0, 5), _part(HIGH5, 0, 5), 128, 256, a[5], b[5], KS)
        lows, highs = t5[:, 4:8].copy(), t5[:, 20:24].copy()
        sixteen = np.concatenate([lows, highs[:, 1:], lows[:, 1:], highs[:, 1:], np.zeros((128, 3))], axis=1)
        t5[:, 128:] = np.tile(sixteen, (1, 8))
        one = fw(RIM_IN0, RIM_LOW0, RIM_HIGH0, 512, 128, a[0], b[0], 1.0)
        rim0 = [sum(np.roll(one, (8 * (4 * g + h), 32 * g), (0, 1)) for g in range(4)) for h in range(4)]
        rim.append(
            _bundle(
                (
                    (0, 0, fw(IN1, RIM_LOW1, RIM_HIGH1, 256, 128, a[1], b[1], KS)),
                    (0, 128, fw(IN2, LOW2, HIGH2, 256, 128, a[2], b[2], KS)),
                    (0, 256, fw(LOW2, LOW3, HIGH3, 128, 128, a[3], b[3], KS)),
                    (128, 256, fw(LOW3, LOW4, HIGH4, 128, 128, a[4], b[4], KS)),
                    (256, 0, t5),
                    (384, 0, np.concatenate(rim0, axis=1)),
                ),
                896,
                512,
            )
        )
        low0 = {**OWN_LOW0, **{k: 256 + v for k, v in RIM_LOW0.items() if -2 <= k < 130}}
        high0 = {**OWN_HIGH0, **{k: 256 + v for k, v in RIM_HIGH0.items()}}
        low1 = {**OWN_LOW1, **{k: 128 + v for k, v in RIM_LOW1.items()}}
        high1 = {**OWN_HIGH1, **{k: 128 + v for k, v in RIM_HIGH1.items()}}
        full = inv(low0, high0, _run(0, 256, 0), 288, 256, a[0], b[0], 1.0)
        ends = np.zeros((128, 128))
        for i in range(32):
            for c in range(-7, 8):
                ends[i, c % 128] = full[256 + i, c % 256]
        ends = sum(np.roll(ends, (32 * g, 32 * g), (0, 1)) for g in range(4))
        s1 = inv(low1, high1, _part(IN1, -1, 130), 256, 256, a[1], b[1], 1.0 / KS)
        s1[:, 128:] = np.tile(s1[:, 128:160], (1, 4))
        back.append(
            _bundle(
                (
                    (0, 0, full[:256]),
                    (256, 0, s1),
                    (512, 0, inv(LOW2, HIGH2, _part(low1, -2, 67), 128, 256, a[2], b[2], 1.0 / KS)),
                    (640, 0, inv(LOW3, HIGH3, _part(LOW2, -2, 36), 128, 128, a[3], b[3], 1.0 / KS)),
                    (640, 128, inv(LOW4, HIGH4, _part(LOW3, -2, 20), 128, 128, a[4], b[4], 1.0 / KS)),
                    (768, 0, inv(LOW5, HIGH5, _part(LOW4, -2, 12), 128, 128, a[5], b[5], 1.0 / KS)),
                    (768, 128, ends),
                ),
                896,
                256,
            )
        )
    out["rim"], out["back"] = np.stack(rim), np.stack(back)
    n = S >> LEVELS
    bands = []
    current = np.eye(n)
    for _ in range(COARSE):
        current, high = _lift(current)
        bands.append(high)
    coarse = np.concatenate([current] + bands[::-1])
    order = (np.arange(n) % NT) * 4 + np.arange(n) // NT
    last = n >> COARSE
    current = np.eye(n)[:last]
    for step in range(COARSE):
        size = last << step
        current = _unlift(current, np.eye(n)[size : 2 * size])
    both = np.zeros((n + 640, n))
    both[:n] = (KS * coarse.T)[order]
    both[n + 4 : 2 * n + 4] = current / KS
    out["coarse"] = _pair(both)
    return out


def _mask(lane, places, first, last, base=0):
    lanes = sorted(v - base for k, v in places.items() if first <= k < last)
    out, i = None, 0
    while i < len(lanes):
        j = i
        while j + 1 < len(lanes) and lanes[j + 1] == lanes[j] + 1:
            j += 1
        hit = (lane >= lanes[i]) & (lane <= lanes[j])
        out = hit if out is None else out | hit
        i = j + 1
    return out


def _ones(hit):
    return jnp.where(hit, 1.0, 0.0)


def _dot3(x, t):
    hi = x.astype(BF16)
    lo = (x - hi.astype(F32)).astype(BF16)
    d = functools.partial(jnp.dot, preferred_element_type=F32)
    both = d(jnp.concatenate([hi, lo], axis=0), t(0))
    return both[: x.shape[0]] + both[x.shape[0] :] + d(hi, t(1))


def _time(load, t, y, step, j):
    x = load(j, step)
    y[pl.ds(j, step)] = _dot3(x.reshape(step * 8, x.shape[2]), t).reshape(step, 8, y.shape[2])


class _Forward:
    def __init__(self, load, t, y, step):
        self.load, self.t, self.y, self.step, self.done = load, t, y, step, 0

    def __call__(self, j):
        ahead = min(j + self.step, self.y.shape[0] - 1)
        while self.done <= ahead:
            _time(self.load, self.t, self.y, self.step, self.done)
            self.done += self.step
        return self.y[j]


class _Backward:
    def __init__(self, y, t, store, step):
        self.y, self.t, self.store, self.step, self.left = y, t, store, step, {}

    def __call__(self, j, value):
        self.y[j] = value
        chunk = j // self.step
        self.left[chunk] = self.left.get(chunk, self.step) - 1
        if not self.left[chunk]:
            x = self.y[pl.ds(chunk * self.step, self.step)]
            out = _dot3(x.reshape(self.step * 8, x.shape[2]), self.t)
            self.store(chunk * self.step, self.step, out.reshape(self.step, 8, out.shape[1]))


def _table(ref, rows, cols, *lead):
    r, c = pl.ds(*rows), pl.ds(*cols)
    return lambda i: ref[(*lead, i, r, c)]


def _sublane(lanes):
    return lax.broadcasted_iota(jnp.int32, (8, lanes), 0)


def _lane(rows=8):
    return lax.broadcasted_iota(jnp.int32, (rows, 128), 1)


def _wide(v, lanes):
    return v if lanes == 128 else jnp.concatenate([v] * (lanes // 128), axis=1)


class _QuarterWrap:
    def __init__(self):
        self.sub, self.group = _sublane(128), _lane() // 32

    def after(self, first, last):
        moved = pltpu.roll(first, 96, 1)
        moved = jnp.where(self.group == 3, pltpu.roll(moved, 7, 0), moved)
        return jnp.where((self.group == 3) & (self.sub == 7), last, moved)

    def before(self, last, first):
        moved = pltpu.roll(last, 32, 1)
        moved = jnp.where(self.group == 0, pltpu.roll(moved, 1, 0), moved)
        return jnp.where((self.group == 0) & (self.sub == 0), first, moved)


def _quarters(values):
    group = _lane() // 32
    out = []
    for c in range(3):
        v = values[0]
        for g in range(1, 4):
            v = jnp.where(group == g, values[(24 * g + 8 * c) // 32], v)
        out.append(v)
    return out


class _Wrap:
    def __init__(self, lanes):
        sub = _sublane(lanes)
        self.last, self.first = sub == 7, sub == 0

    def after(self, first, last):
        return jnp.where(self.last, last, pltpu.roll(first, 7, 0))

    def before(self, last, first):
        return jnp.where(self.first, first, pltpu.roll(last, 1, 0))


def _coefs(weights, lanes):
    return [[_wide(c * v, lanes) for v in weights] for c in (A1, B1, A2, B2)]


def _chan_forward(get, n, weights, lanes, put_low, put_high, wrap=None):
    wrap = wrap or _Wrap(lanes)
    ca, cb, cc, cd = _coefs(weights, lanes)
    per = n // 3
    first = get(0)
    e, o1, e1, o2 = {0: first}, {}, {}, {}

    def high(k, v):
        o2[k] = v
        put_high(k, k // per, v)

    def low(k):
        put_low(k, k // per, e1[k] + cd[k // per] * (o2[k - 1] + o2[k]))

    for k in range(n):
        q = k // per
        e[k + 1] = get(2 * k + 2) if k + 1 < n else wrap.after(first, e[k])
        o1[k] = get(2 * k + 1) + ca[q] * (e[k] + e[k + 1])
        if k >= 1:
            e1[k] = e[k] + cb[q] * (o1[k - 1] + o1[k])
        if k >= 2:
            high(k - 1, o1[k - 1] + cc[(k - 1) // per] * (e1[k - 1] + e1[k]))
        if k >= 3:
            low(k - 1)
    e1[0] = first + cb[0] * (wrap.before(o1[n - 1], o1[0]) + o1[0])
    high(0, o1[0] + cc[0] * (e1[0] + e1[1]))
    high(n - 1, o1[n - 1] + cc[2] * (e1[n - 1] + wrap.after(e1[0], e1[n - 1])))
    o2[-1] = wrap.before(o2[n - 1], o2[0])
    for k in (0, 1, n - 1):
        low(k)


def _chan_inverse(get_low, get_high, n, weights, lanes, put, wrap=None):
    wrap = wrap or _Wrap(lanes)
    ca, cb, cc, cd = _coefs(weights, lanes)
    per = n // 3
    o = {0: get_high(0)}
    o[-1] = wrap.before(get_high(n - 1), o[0])
    e1, o1, e2 = {}, {}, {}

    def even(k):
        e2[k] = e1[k] - cb[k // per] * (o1[k - 1] + o1[k])
        put(2 * k, e2[k])

    def odd(k):
        put(2 * k + 1, o1[k] - ca[k // per] * (e2[k] + e2[k + 1]))

    for k in range(n):
        q = k // per
        if k:
            o[k] = get_high(k)
        e1[k] = get_low(k) - cd[q] * (o[k - 1] + o[k])
        if k >= 1:
            o1[k - 1] = o[k - 1] - cc[(k - 1) // per] * (e1[k - 1] + e1[k])
        if k >= 2:
            even(k - 1)
        if k >= 3:
            odd(k - 2)
    o1[n - 1] = o[n - 1] - cc[2] * (e1[n - 1] + wrap.after(e1[0], e1[n - 1]))
    o1[-1] = wrap.before(o1[n - 1], o1[0])
    even(n - 1)
    if n > 2:
        odd(n - 2)
    even(0)
    odd(0)
    e2[n] = wrap.after(e2[0], e2[n - 1])
    odd(n - 1)


class _Squares:
    def __init__(self):
        self.acc = {}

    def add(self, key, v):
        self.acc[key] = v * v if key not in self.acc else self.acc[key] + v * v

    def total(self, rows, tiles):
        out = None
        for q in range(3):
            part = None
            for (band, tile), lanes in tiles.items():
                v = self.acc[(band, tile, q)] * (KS * KS if band == "low" else 1.0 / (KS * KS))
                v = v if lanes is None else v * lanes
                part = v if part is None else part + v
            part = part * rows[q]
            out = part if out is None else out + part
        return out


def _tile(v, i):
    return v[:, 128 * i : 128 * (i + 1)]


def _blocks(w, level):
    return [w[level, q] for q in range(3)]


def _own_rows(core):
    block = 3 * _sublane(128)
    return [
        jnp.where(core == 0, _ones(block + q < 16), _ones(block + q >= 8)) for q in range(3)
    ]


def _load_kernel(
    sc, x_all, gauge_table_all, gauge_index_all, own_all,
    low, high, ends, own_table, w,
    x, gauge_table, gauge_index, sems,
):
    core = sc[0]
    copies = [
        pltpu.make_async_copy(src, dst, sems.at[i])
        for i, (src, dst) in enumerate(
            (
                (gauge_index_all, gauge_index),
                (gauge_table_all, gauge_table),
                (own_all, own_table),
                *((x_all.at[pl.ds(256 * i, 256)], x.at[pl.ds(256 * i, 256)]) for i in range(4)),
            )
        )
    ]
    for c in copies:
        c.start()
    for c in copies[:2]:
        c.wait()
    index = gauge_index[...]
    table_rows = gauge_table[...]
    weights = jnp.zeros(index.shape, F32)
    for g in range(GTAB):
        weights = weights + jnp.where(index == g, table_rows[:, g : g + 1], 0.0)
    block = lax.broadcasted_iota(jnp.int32, (8, NBLK), 1) - 3 * lax.broadcasted_iota(jnp.int32, (8, NBLK), 0)
    block = block - 8 * core
    for l in range(LEVELS):
        for q in range(3):
            hit = jnp.where(block == q, weights[l : l + 1], 0.0)
            w[l, q] = jnp.broadcast_to(jnp.sum(hit, axis=1, keepdims=True), (8, 128))
    copies[2].wait()
    for c in copies[3:]:
        c.wait()
    _first(x, own_table, low, high, ends, 0, range(0, OWN, 128))


def _first(x, table, low, high, ends, at, blocks):
    lane = _lane(128)
    for r in blocks:
        v = x[pl.ds(r, 128), :]
        y = _dot3(v, _table(table, (0, 256), (0, 256)))
        rows = pl.ds(at + r, 128)
        low[rows, :] = y[:, 0:128]
        high[rows, :] = y[:, 128:256]
        ends[rows, :] = jnp.where(lane < 32, v[:, 0:128], v[:, 128:256])


def _own_kernel(
    sc, recv, own_low, own_high, own_ends, table, w,
    right, left, low0, a1l, fh, details, sums,
    fl, fe, y1,
):
    core = sc[0]
    at_own = pl.multiple_of(core * HALO, 8)
    at_recv = pl.multiple_of((1 - core) * OWN, 8)
    for src, dst in ((own_low, fl), (own_high, fh), (own_ends, fe)):
        for r in range(0, OWN, 128):
            dst[pl.ds(at_own + r, 128), :] = src[pl.ds(r, 128), :]
    theirs = recv.at[pl.ds(at_own, HALO)]
    _first(theirs, table, fl, fh, fe, at_recv, range(0, HALO, 128))
    lane = _lane()
    group = lane // 8
    for i in range(12):
        to_right, to_left = None, None
        for g in range(16):
            v = fe[pl.ds(12 * g + i, 8, stride=SEG), :]
            a = pltpu.roll(v, 8 * g, 1) if g else v
            b = pltpu.roll(v, (8 * g + 8) % 128, 1) if g != 15 else v
            to_left = a if to_left is None else jnp.where(group == g, a, to_left)
            to_right = b if to_right is None else jnp.where(group == g, b, to_right)
        right[i] = to_right
        left[i] = to_left
    rows = _own_rows(core)
    sq = _Squares()

    def put_low(k, q, v):
        low0[k] = v

    def put_high(k, q, v):
        details[k] = v
        sq.add(("high", 0, q), v)

    _chan_forward(lambda j: fl[pl.ds(j, 8, stride=SEG), :], 96, _blocks(w, 0), 128, put_low, put_high)
    sums[0] = sq.total(rows, {("high", 0): None})
    for i in range(6):
        to_right, to_left = None, None
        for g in range(16):
            v = low0[6 * g + i]
            a = pltpu.roll(v, (8 * g - 118) % 128, 1)
            b = pltpu.roll(v, (8 * g + 6) % 128, 1)
            to_right = a if to_right is None else jnp.where(group == g, a, to_right)
            to_left = b if to_left is None else jnp.where(group == (g + 1) % 16, b, to_left)
        right[12 + i] = to_right
        left[12 + i] = to_left
    sq1 = _Squares()

    def put_low1(k, q, v):
        a1l[k] = v
        details[96 + k] = v
        sq1.add(("low", 0, q), v)
        if k >= 26:
            packed = jnp.where(lane < 64, a1l[k - 24], pltpu.roll(v, 64, 1))
            right[k - 6] = packed
            left[k - 6] = packed

    def put_high1(k, q, v):
        details[144 + k] = v
        sq1.add(("high", 0, q), v)

    get = _Forward(lambda j, n: low0[pl.ds(j, n)], _table(table, (256, 128), (0, 128)), y1, 24)
    _chan_forward(get, 48, _blocks(w, 1), 128, put_low1, put_high1)
    for k in (24, 25):
        packed = jnp.where(lane < 64, a1l[k - 24], pltpu.roll(a1l[k], 64, 1))
        right[k - 6] = packed
        left[k - 6] = packed
    sums[1] = sq1.total(rows, {("low", 0): _ones(_mask(lane, OWN_HIGH1, 0, 64)), ("high", 0): None})


def _bands(details):
    out, at = [], 0
    for n in (24, 48, 24, 12, 6, 3):
        out += [details.at[pl.ds(at, n)], details.at[pl.ds(at + n, n)]]
        at += 2 * n
    return out


def _aside_kernel(
    sc, fh, w, rim_all, back_all, coarse_all, rim_table, back_table, coarse_table, details, sums, sems
):
    copies = []
    mine = pl.multiple_of(512 + 16 * (sc[2] // 4), 16)
    for i in range(2):
        for src, dst, start, n in (
            (rim_all.at[sc[1], i], rim_table.at[i], 0, 448),
            (rim_all.at[sc[1], i], rim_table.at[i], 448, 448),
            (back_all.at[sc[1], i], back_table.at[i], 0, 896),
            (coarse_all.at[i], coarse_table.at[i], 0, 512),
        ):
            rows = pl.ds(start, n)
            copies.append(pltpu.make_async_copy(src.at[rows], dst.at[rows], sems.at[len(copies)]))
        src, dst = coarse_all.at[i, pl.ds(mine, 128)], coarse_table.at[i, pl.ds(512, 128)]
        copies.append(pltpu.make_async_copy(src, dst, sems.at[len(copies)]))
    for c in copies:
        c.start()
    rows = _own_rows(sc[0])
    sq = _Squares()

    def put_low(k, q, v):
        details[k] = v
        sq.add(("low", 0, q), v)

    def put_high(k, q, v):
        details[96 + k] = v
        sq.add(("high", 0, q), v)

    _chan_forward(lambda j: fh[pl.ds(j, 8, stride=SEG), :], 96, _blocks(w, 0), 128, put_low, put_high)
    sums[...] = sq.total(rows, {("low", 0): None, ("high", 0): None})
    for c in copies:
        c.wait()


def _rim_kernel(
    sc, right, left, from_left, from_right, low0, a1l, own_sums, more_sums, table, w,
    details, payload,
    rim, y0, y1, x2, y2, y3, y4, y5, l5, h5, flat,
):
    core = sc[0]
    rlow0, rhigh0, r1l, r1h, a2l, a2h, a3l, a3h, a4l, a4h, a5l, a5h = _bands(details)
    lane = _lane()
    rows = _own_rows(core)
    totals = []

    def level(l, load, n, t, y, step, lanes, low, high, own_low, own_high, pairs):
        quarters = l == 0
        weights = _blocks(w, l)
        place = lane % 32 if quarters else lane
        sq = _Squares()

        def put_low(k, q, value):
            low[k] = value
            sq.add(("low", 0, q), _tile(value, 0))

        def put_high(k, q, value):
            high[k] = value
            sq.add(("high", 0, q), _tile(value, 0))

        wrap = _QuarterWrap() if quarters else None
        weights = _quarters(weights) if quarters else weights
        get = y.__getitem__ if quarters else _Forward(load, t, y, step)
        _chan_forward(get, n, weights, lanes, put_low, put_high, wrap)
        is_high = _mask(place, own_high, 0, pairs)
        is_low = _mask(place, own_low, 0, pairs)
        total = sq.total(_quarters(rows) if quarters else rows, {("low", 0): _ones(is_high), ("high", 0): _ones(is_high | is_low)})
        totals.append(total + own_sums[l] if l < 2 else total)

    def pick(r, k, c, n):
        return _table(table, (r, k), (c, n))

    raw = pl.ds(0, 12)
    raw = jnp.concatenate([from_left[raw], left[raw], right[raw], from_right[raw]], axis=2)
    raw = _dot3(raw.reshape(96, 512), pick(384, 512, 0, 512))
    for h in range(4):
        y0[pl.ds(12 * h, 12)] = _tile(raw, h).reshape(12, 8, 128)
    level(0, None, 24, None, y0, 24, 128, rlow0, rhigh0, RIM_LOW0, RIM_HIGH0, 128)
    totals[0] = totals[0] + more_sums[...]
    for j in range(96):
        g, i = j // 24, j % 24
        mine = pltpu.roll(rlow0[i], 128 - 32 * g, 1) if g else rlow0[i]
        g, i = j // 6, 12 + j % 6
        theirs = jnp.where(lane // 8 == g, from_left[i], from_right[i])
        theirs = pltpu.roll(theirs, (32 - 8 * g) % 128, 1) if g != 4 else theirs
        rim[j] = jnp.where(lane < 32, mine, theirs)

    def load1(j, n):
        return jnp.concatenate([low0[pl.ds(j, n)], rim[pl.ds(j, n)]], axis=2)

    level(1, load1, 48, pick(0, 256, 0, 128), y1, 24, 128, r1l, r1h, RIM_LOW1, RIM_HIGH1, 64)
    for j in range(48):
        h, i = j // 24, 18 + j % 24
        b, a = from_left[i], from_right[i]
        if h == 0:
            a = pltpu.roll(a, 64, 1)
        else:
            b = pltpu.roll(b, 64, 1)
        x2[j, :, 0:128] = jnp.where(lane < 64, a1l[j], a)
        x2[j, :, 128:256] = jnp.where(lane < 64, b, r1l[j])
    level(2, lambda j, n: x2[pl.ds(j, n)], 24, pick(0, 256, 128, 128), y2, 24, 128, a2l, a2h, LOW2, HIGH2, 32)
    level(3, lambda j, n: a2l[pl.ds(j, n)], 12, pick(0, 128, 256, 128), y3, 24, 128, a3l, a3h, LOW3, HIGH3, 16)
    level(4, lambda j, n: a3l[pl.ds(j, n)], 6, pick(128, 128, 256, 128), y4, 12, 128, a4l, a4h, LOW4, HIGH4, 8)
    level(5, lambda j, n: a4l[pl.ds(j, n)], 3, pick(256, 128, 0, 256), y5, 6, 256, l5, h5, LOW5, HIGH5, 4)
    sub = _sublane(128)
    for j in range(3):
        a5l[j] = l5[j, :, 0:128]
        a5h[j] = h5[j, :, 0:128]
        flat[pl.ds(j, 8, stride=3), :] = jnp.where(lane % 16 < 7, l5[j, :, 128:256], h5[j, :, 128:256])
    sums = jnp.zeros((8, 128), F32)
    for l in range(LEVELS):
        sums = jnp.where(sub == l, jnp.sum(totals[l], axis=0, keepdims=True), sums)
    sums = jnp.where((lane == 16 * sub + 13) & (sub < LEVELS), jnp.sum(sums, axis=1, keepdims=True), 0.0)
    lines = []
    for h in range(2):
        mine = flat[pl.ds(pl.multiple_of(8 * core + 8 * h, 8), 8), :]
        mine = jnp.where(lane // 16 == sub, mine, 0.0)
        lines.append(jnp.sum(mine + sums if h == 0 else mine, axis=0, keepdims=True))
    block = jnp.where(sub % 2 == 0, lines[0], lines[1])
    for i in range(32):
        payload[pl.ds(8 * i, 8), :] = block


def _shrink(v, limit):
    return v - jnp.minimum(jnp.maximum(v, -limit), limit)


def _back_kernel(
    sc, mine, theirs, coarse_table, table, own_details, more_details, rim_details, w,
    out,
    both, gt, nears, cur, x5l, x5h, y5, y4, y3, y2, y1, c4, c3, c2, c1, c0, f0, f1, f2, yr, stage, sems,
):
    core, place = sc[0], sc[2]
    rlow0, rhigh0, r1l, r1h, a2l, a2h, a3l, a3h, a4l, a4h, a5l, a5h = _bands(rim_details)
    dhigh0, dlow0, dhigh1 = own_details.at[pl.ds(0, 96)], more_details.at[pl.ds(0, 96)], more_details.at[pl.ds(96, 96)]
    a1l, a1h = (own_details.at[pl.ds(96 + 48 * i, 48)] for i in range(2))
    lane = _lane()
    lane1 = _lane(1)
    sub = _sublane(128)
    both[0, 0:256, :] = mine[...]
    both[1, 0:256, :] = theirs[...]
    for h in range(2):
        halves = [both[g, pl.ds(h, NT, stride=2), :] for g in range(2)]
        if h == 0:
            total = jnp.sum(halves[0] + halves[1], axis=0, keepdims=True)
        for c in range(2):
            gt[c, h, 0:128, :] = jnp.transpose(jnp.where(core == c, halves[0], halves[1]))
    limits = []
    for l in range(LEVELS):
        entries = 3 * (C >> (l + 1)) * (S >> (l + 1))
        s = jnp.sum(jnp.where(lane1 == 16 * l + 13, total, 0.0), axis=1, keepdims=True)
        limits.append(jnp.sqrt(s * (1.0 / entries) + FLOOR))
    rows = [
        jnp.concatenate([gt[c, h, pl.ds(m, 8, stride=16), :] for m in range(4)], axis=1)
        for c in range(2)
        for h in range(2)
    ]
    coarse = _dot3(jnp.concatenate(rows, axis=0), lambda i: coarse_table[i, 0:512, :])
    highs = lax.broadcasted_iota(jnp.int32, (32, 512), 1) >= (S >> (LEVELS + COARSE))
    square = jnp.sum(jnp.where(highs, coarse * coarse, 0.0), axis=0, keepdims=True)
    square = jnp.sum(square, axis=1, keepdims=True)
    entries = (C >> LEVELS) * ((S >> LEVELS) - (S >> (LEVELS + COARSE)))
    limit = jnp.sqrt(square * (1.0 / entries) + FLOOR)
    coarse = jnp.where(highs, _shrink(coarse, limit), coarse)
    hi = coarse.astype(BF16)
    lo = (coarse - hi.astype(F32)).astype(BF16)
    for side, other in enumerate((jnp.maximum(place - 1, 0), jnp.minimum(place + 1, NT - 1))):
        for c in range(2):
            for h in range(2):
                row = pl.ds(2 * other + h, 1)
                line = jnp.broadcast_to(jnp.where(core == c, mine[row, :], theirs[row, :]), (8, 128))
                near = line
                for k in range(1, 8):
                    near = jnp.where(sub == k, pltpu.roll(line, 128 - 16 * k, 1), near)
                nears[side, pl.ds(16 * c + 8 * h, 8), :] = near
    for k in range(3):
        rows = pl.ds(8 * core + k, 8, stride=3)
        before, after = nears[0, rows, :], nears[1, rows, :]
        v = a5h[k]
        for at, near, shift in ((1, before, 122), (9, after, 2), (17, before, 7), (25, after, 15)):
            v = jnp.where((lane >= at) & (lane < at + 3), pltpu.roll(near, shift, 1), v)
        x5h[k] = v
        v = a5l[k]
        for at, near, shift in ((17, before, 13), (25, after, 21)):
            v = jnp.where((lane >= at) & (lane < at + 3), pltpu.roll(near, shift, 1), v)
        x5l[k] = v

    def nt(a, b):
        return lax.dot_general(a, b, (((1,), (1,)), ((), ())), preferred_element_type=F32)

    rows = pl.ds(512, 128)
    current = nt(hi, coarse_table[0, rows, :]) + nt(lo, coarse_table[0, rows, :]) + nt(hi, coarse_table[1, rows, :])
    cur[0:32, :] = pltpu.roll(current, (128 - 4 * (place % 4)) % 128, 1)

    def level(l, get_current, low, high, n, y, t, nxt, step, needed):
        tl = jnp.broadcast_to(limits[l] * (1.0 / KS), (8, 128))
        th = jnp.broadcast_to(limits[l] * KS, (8, 128))
        is_low = needed(lane)

        def get_low(k):
            return jnp.where(is_low, get_current(k), _shrink(low[k], tl))

        def store(j, m, value):
            nxt[pl.ds(j, m)] = value

        put = _Backward(y, t, store, step)
        _chan_inverse(get_low, lambda k: _shrink(high[k], th), n, _blocks(w, l), 128, put)

    def pick(r, k, c, n):
        return _table(table, (r, k), (c, n))

    level(
        5, lambda k: cur[pl.ds(8 * core + k, 8, stride=3), :], x5l, x5h, 3, y5, pick(768, 128, 0, 128), c4, 6, lambda i: i < 12
    )
    level(4, lambda k: c4[k], a4l, a4h, 6, y4, pick(640, 128, 128, 128), c3, 12, lambda i: i < 32)
    level(3, lambda k: c3[k], a3l, a3h, 12, y3, pick(640, 128, 0, 128), c2, 24, lambda i: i < 64)
    level(2, lambda k: c2[k], a2l, a2h, 24, y2, pick(512, 128, 0, 256), c1, 24, lambda i: i < 89)
    tl = jnp.broadcast_to(limits[1] * (1.0 / KS), (8, 256))
    th = jnp.broadcast_to(limits[1] * KS, (8, 256))
    lane2 = lax.broadcasted_iota(jnp.int32, (8, 256), 1)
    is_low1 = (lane2 < 64) | ((lane2 >= 192) & (lane2 < 208))

    def get_low1(k):
        v1 = jnp.concatenate([a1l[k], r1l[k]], axis=1)
        return jnp.where(is_low1, c1[k], _shrink(v1, tl))

    def get_high1(k):
        return _shrink(jnp.concatenate([a1h[k], r1h[k]], axis=1), th)

    def store1(j, m, value):
        c0[pl.ds(j, m)] = value

    put1 = _Backward(y1, pick(256, 256, 0, 256), store1, 24)
    _chan_inverse(get_low1, get_high1, 48, _blocks(w, 1), 256, put1)
    tl0 = jnp.broadcast_to(limits[0] * (1.0 / KS), (8, 128))
    th0 = jnp.broadcast_to(limits[0] * KS, (8, 256))
    group = lane // 32
    rim_low = lane % 32 < 8

    def get_low_rim(k):
        now = c0[k, :, 128:256]
        for q in range(1, 4):
            now = jnp.where(group == q, c0[24 * q + k, :, 128:256], now)
        return jnp.where(rim_low, now, _shrink(rlow0[k], tl0))

    def store_rim(j, m, value):
        for i in range(m):
            for q in range(4):
                v = pltpu.roll(value[i], 128 - 32 * q, 1) if q else value[i]
                f2[pl.ds(48 * q + j + i, 8, stride=SEG), :] = v

    put_rim = _Backward(yr, pick(768, 128, 128, 128), store_rim, 24)
    _chan_inverse(
        get_low_rim, lambda k: _shrink(rhigh0[k], th0[:, 0:128]), 24, _quarters(_blocks(w, 0)), 128, put_rim, _QuarterWrap()
    )

    def get_low0(k):
        return jnp.concatenate([c0[k, :, 0:128], _shrink(dlow0[k], tl0)], axis=1)

    def get_high0(k):
        return _shrink(jnp.concatenate([dhigh0[k], dhigh1[k]], axis=1), th0)

    def put0(j, value):
        for i, buf in enumerate((f0, f1)):
            buf[pl.ds(j, 8, stride=SEG), :] = _tile(value, i)

    _chan_inverse(get_low0, get_high0, 96, _blocks(w, 0), 256, put0)
    at_own = pl.multiple_of(core * HALO, 8)
    t = pick(0, 256, 0, 256)
    wide = _lane(128)
    copies = []
    for r in range(0, OWN, 128):
        rows = pl.ds(at_own + r, 128)
        done = pl.ds(r, 128)
        ends = f2[rows, :]
        v = _dot3(jnp.concatenate([f0[rows, :], f1[rows, :]], axis=1), t)
        stage[done, 0:128] = _tile(v, 0) + jnp.where(wide < 8, ends, 0.0)
        stage[done, 128:256] = _tile(v, 1) + jnp.where(wide >= 121, ends, 0.0)
        copies.append(pltpu.make_async_copy(stage.at[done], out.at[done], sems.at[r // 128]))
        copies[-1].start()
    for c in copies:
        c.wait()


VM = pl.BlockSpec(memory_space=pltpu.VMEM)
SM = pl.BlockSpec(memory_space=pltpu.SMEM)
HBM = pl.BlockSpec(memory_space=pltpu.HBM)
ROWS = (9 * SEG, 128)


def _call(kernel, name, limit, args, specs, outs, out_specs, scratch):
    args = [
        pltpu.with_memory_space_constraint(x, pltpu.HBM) if spec is HBM else x for x, spec in zip(args, specs)
    ]
    outs = [jax.ShapeDtypeStruct(s, F32) if isinstance(s, tuple) else s for s in outs]
    return pl.pallas_call(
        kernel,
        out_shape=[pltpu.HBM(s.shape, s.dtype) if spec is HBM else s for s, spec in zip(outs, out_specs)],
        in_specs=specs,
        out_specs=out_specs,
        scratch_shapes=[pltpu.VMEM(s, F32) if isinstance(s, tuple) else s for s in scratch],
        compiler_params=pltpu.CompilerParams(vmem_limit_bytes=limit << 20),
        name=name,
    )(*args)


def _shift(v, by):
    return lax.ppermute(v, "tm", [(i, (i + by) % NT) for i in range(NT)])


def shards(record, gauge_table, gauge_index):
    tables = _tables()
    core = lax.axis_index("chan")
    place = lax.axis_index("tm")
    variant = jnp.where(place == 0, 0, jnp.where(place == NT - 1, 2, 1))
    sc = jnp.stack([core, variant, place]).astype(jnp.int32)
    dma = pltpu.SemaphoreType.DMA
    recv = lax.ppermute(record, "chan", [(0, 1), (1, 0)])
    low, high, ends, own_table, w = _call(
        _load_kernel, "load", 12, (sc, record, gauge_table, gauge_index, tables["own"]),
        [SM] + [HBM] * 4,
        [(OWN, 128), (OWN, 128), (OWN, 128), jax.ShapeDtypeStruct((2, 384, 256), BF16), (LEVELS, 3, 8, 128)],
        [VM] * 5,
        [(OWN, 256), (LEVELS, GTAB), pltpu.VMEM((LEVELS, NBLK), jnp.int32), dma((7,))],
    )
    right, left, low0, a1l, fh, own_details, sums = _call(
        _own_kernel, "own", 12, (sc, recv, low, high, ends, own_table, w), [SM] + [VM] * 6,
        [(42, 8, 128), (42, 8, 128), (96, 8, 128), (48, 8, 128), ROWS, (192, 8, 128), (2, 8, 128)],
        [VM] * 7,
        [ROWS, ROWS, (96, 8, 128)],
    )
    from_left, from_right = _shift(right, 1), _shift(left, -1)
    rim_table, back_table, coarse_table, more_details, more_sums = _call(
        _aside_kernel, "aside", 6, (sc, fh, w, tables["rim"], tables["back"], tables["coarse"]),
        [SM, VM, VM, HBM, HBM, HBM],
        [jax.ShapeDtypeStruct((2, 896, 512), BF16), jax.ShapeDtypeStruct((2, 896, 256), BF16),
         jax.ShapeDtypeStruct((2, 640, 512), BF16), (192, 8, 128), (8, 128)],
        [VM] * 5,
        [dma((10,))],
    )
    rim_details, payload = _call(
        _rim_kernel, "rim", 16,
        (sc, right, left, from_left, from_right, low0, a1l, sums, more_sums, rim_table, w), [SM] + [VM] * 10,
        [(234, 8, 128), (256, 128)], [VM] * 2,
        [(96, 8, 128), (48, 8, 128), (96, 8, 128), (48, 8, 256), (48, 8, 128), (24, 8, 128), (12, 8, 128),
         (6, 8, 256), (3, 8, 256), (3, 8, 256), (32, 128)],
    )
    mine = lax.all_to_all(payload, "tm", split_axis=0, concat_axis=0, tiled=True)
    theirs = lax.ppermute(mine, "chan", [(0, 1), (1, 0)])
    (out,) = _call(
        _back_kernel, "back", 24, (sc, mine, theirs, coarse_table, back_table, own_details, more_details, rim_details, w),
        [SM] + [VM] * 8, [(OWN, 256)], [HBM],
        [
            (2, 264, 128), (2, 2, 144, 128), (2, 40, 128), (40, 128), (3, 8, 128), (3, 8, 128),
            (6, 8, 128), (12, 8, 128), (24, 8, 128), (48, 8, 128), (96, 8, 256),
            (6, 8, 128), (12, 8, 128), (24, 8, 128), (48, 8, 256), (96, 8, 256),
            ROWS, ROWS, ROWS, (48, 8, 128), (OWN, 256), dma((8,)),
        ],
    )
    return out


def solution(mesh):
    return jax.shard_map(
        shards,
        mesh=mesh,
        in_specs=(P("chan", "tm"), P(), P()),
        out_specs=P("chan", "tm"),
        check_vma=False,
    )
```

```python
import functools

import jax
import jax.numpy as jnp
import ml_dtypes
import numpy as np
from jax import lax
from jax.experimental import pallas as pl
from jax.experimental.pallas import tpu as pltpu
from jax.sharding import PartitionSpec as P

LEVELS = 6
COARSE = 6
GTAB = 8
NBLK = 32
C = 2048
S = 32768
NT = 128
OWN = 1024
HALO = 512
SEG = 192
A1 = -1.586134342059924
B1 = -0.052980118572961
A2 = 0.882911075530934
B2 = 0.443506852043971
KS = 1.149604398860241
FLOOR = 1e-06
F32 = jnp.float32
BF16 = jnp.bfloat16


def _next(e):
    return np.concatenate((e[1:], e[-1:]))


def _prev(o):
    return np.concatenate((o[:1], o[:-1]))


def _lift(x):
    e, o = x[0::2], x[1::2]
    o = o + A1 * (e + _next(e))
    e = e + B1 * (_prev(o) + o)
    o = o + A2 * (e + _next(e))
    e = e + B2 * (_prev(o) + o)
    return KS * e, o / KS


def _unlift(low, high):
    e, o = low / KS, high * KS
    e = e - B2 * (_prev(o) + o)
    o = o - A2 * (e + _next(e))
    e = e - B1 * (_prev(o) + o)
    o = o - A1 * (e + _next(e))
    return np.stack((e, o), axis=1).reshape((2 * e.shape[0],) + e.shape[1:])


def _forward(inputs, lows, highs, rows, cols, start, stop, scale):
    pairs = list(lows) + list(highs)
    a = max(2 * min(pairs) - 16, start)
    b = min(2 * max(pairs) + 16, stop)
    low, high = _lift(np.eye(b - a))
    out = np.zeros((rows, cols))
    for band, places in ((low, lows), (high, highs)):
        for pair, col in places.items():
            if a <= 2 * pair < b:
                line = band[pair - a // 2]
                for i in np.nonzero(line)[0]:
                    out[inputs[a + int(i)], col] += scale * line[i]
    return out


def _inverse(lows, highs, outputs, rows, cols, start, stop, scale):
    a = max(2 * (min(outputs) // 2) - 16, start) // 2
    b = min(2 * (max(outputs) // 2) + 18, stop) // 2
    n = b - a
    eye, zero = np.eye(n), np.zeros((n, n))
    from_low, from_high = _unlift(eye, zero), _unlift(zero, eye)
    out = np.zeros((rows, cols))
    for sample, col in outputs.items():
        if 2 * a <= sample < 2 * b:
            for lines, places in ((from_low, lows), (from_high, highs)):
                line = lines[sample - 2 * a]
                for i in np.nonzero(line)[0]:
                    out[places[a + int(i)], col] += scale * line[i]
    return out


def _pair(m):
    hi = m.astype(ml_dtypes.bfloat16)
    lo = (m - hi.astype(np.float64)).astype(ml_dtypes.bfloat16)
    return np.stack((hi, lo))


def _run(first, last, at):
    return {k: at + k - first for k in range(first, last)}


OWN_LOW0 = _run(2, 126, 2)
OWN_HIGH0 = _run(2, 126, 130)
RIM_LOW0 = {**_run(-2, 2, 0), **_run(126, 130, 4)}
RIM_HIGH0 = {**_run(-2, 2, 8), **_run(126, 130, 12)}
RIM_IN0 = {**_run(-8, 0, 120), **_run(0, 8, 128), **_run(248, 256, 376), **_run(256, 264, 384)}
OWN_LOW1 = _run(3, 61, 3)
OWN_HIGH1 = _run(2, 61, 66)
RIM_LOW1 = {**_run(-3, 3, 64), **_run(61, 67, 70)}
RIM_HIGH1 = {**_run(-3, 2, 80), **_run(61, 67, 85)}
IN1 = {**OWN_LOW0, **{k: 128 + v for k, v in RIM_LOW0.items()}, **_run(-10, -2, 160), **_run(130, 138, 168)}
IN2 = {
    **OWN_LOW1, **_run(67, 125, 67), **_run(-61, -3, 131), **{k: 128 + v for k, v in RIM_LOW1.items()}
}
LOW2 = _run(-28, 61, 0)
HIGH2 = _run(-3, 36, 89)
LOW3 = _run(-12, 29, 0)
HIGH3 = _run(-3, 20, 64)
LOW4 = _run(-4, 13, 0)
HIGH4 = _run(-3, 12, 32)
LOW5 = _run(-4, 8, 0)
HIGH5 = _run(-4, 8, 16)


def _part(places, first, last):
    return {k: places[k] for k in range(first, last)}


def _edges(width):
    far = 1 << 20
    return ((0, far), (-far, far), (-far, width))


def _bundle(parts, rows, cols):
    out = np.zeros((rows, cols))
    for r, c, m in parts:
        out[r : r + m.shape[0], c : c + m.shape[1]] = m
    return _pair(out)


@functools.cache
def _tables():
    fw, inv = _forward, _inverse
    far = 1 << 20
    out = {}
    out["own"] = _bundle(
        (
            (0, 0, fw(_run(0, 256, 0), OWN_LOW0, OWN_HIGH0, 256, 256, -far, far, 1.0)),
            (256, 0, fw(OWN_LOW0, OWN_LOW1, OWN_HIGH1, 128, 128, -far, far, KS)),
        ),
        384,
        256,
    )
    rim, back = [], []
    for v in range(3):
        a, b = zip(*(_edges(256 >> l)[v] for l in range(LEVELS)))
        t5 = fw(LOW4, _part(LOW5, 0, 5), _part(HIGH5, 0, 5), 128, 256, a[5], b[5], KS)
        lows, highs = t5[:, 4:8].copy(), t5[:, 20:24].copy()
        sixteen = np.concatenate([lows, highs[:, 1:], lows[:, 1:], highs[:, 1:], np.zeros((128, 3))], axis=1)
        t5[:, 128:] = np.tile(sixteen, (1, 8))
        one = fw(RIM_IN0, RIM_LOW0, RIM_HIGH0, 512, 128, a[0], b[0], 1.0)
        one = one.reshape(4, 128, 128)
        rim0 = [sum(np.roll(one, (8 * (4 * g + h), 32 * g), (1, 2)) for g in range(4)).reshape(512, 128) for h in range(4)]
        rim.append(
            _bundle(
                (
                    (0, 0, fw(IN1, RIM_LOW1, RIM_HIGH1, 256, 128, a[1], b[1], KS)),
                    (0, 128, fw(IN2, LOW2, HIGH2, 256, 128, a[2], b[2], KS)),
                    (0, 256, fw(LOW2, LOW3, HIGH3, 128, 128, a[3], b[3], KS)),
                    (128, 256, fw(LOW3, LOW4, HIGH4, 128, 128, a[4], b[4], KS)),
                    (256, 0, t5),
                    (384, 0, np.concatenate(rim0, axis=1)),
                ),
                896,
                512,
            )
        )
        low0 = {**OWN_LOW0, **{k: 256 + v for k, v in RIM_LOW0.items() if -2 <= k < 130}}
        high0 = {**OWN_HIGH0, **{k: 256 + v for k, v in RIM_HIGH0.items()}}
        low1 = {**OWN_LOW1, **{k: 128 + v for k, v in RIM_LOW1.items()}}
        high1 = {**OWN_HIGH1, **{k: 128 + v for k, v in RIM_HIGH1.items()}}
        full = inv(low0, high0, _run(0, 256, 0), 288, 256, a[0], b[0], 1.0)
        ends = np.zeros((128, 128))
        for i in range(32):
            for c in range(-7, 8):
                ends[i, c % 128] = full[256 + i, c % 256]
        ends = sum(np.roll(ends, (32 * g, 32 * g), (0, 1)) for g in range(4))
        s1 = inv(low1, high1, _part(IN1, -1, 130), 256, 256, a[1], b[1], 1.0 / KS)
        s1[:, 128:] = np.tile(s1[:, 128:160], (1, 4))
        back.append(
            _bundle(
                (
                    (0, 0, full[:256]),
                    (256, 0, s1),
                    (512, 0, inv(LOW2, HIGH2, _part(low1, -2, 67), 128, 256, a[2], b[2], 1.0 / KS)),
                    (640, 0, inv(LOW3, HIGH3, _part(LOW2, -2, 36), 128, 128, a[3], b[3], 1.0 / KS)),
                    (640, 128, inv(LOW4, HIGH4, _part(LOW3, -2, 20), 128, 128, a[4], b[4], 1.0 / KS)),
                    (768, 0, inv(LOW5, HIGH5, _part(LOW4, -2, 12), 128, 128, a[5], b[5], 1.0 / KS)),
                    (768, 128, ends),
                ),
                896,
                256,
            )
        )
    out["rim"], out["back"] = np.stack(rim), np.stack(back)
    n = S >> LEVELS
    bands = []
    current = np.eye(n)
    for _ in range(COARSE):
        current, high = _lift(current)
        bands.append(high)
    coarse = np.concatenate([current] + bands[::-1])
    order = (np.arange(n) % NT) * 4 + np.arange(n) // NT
    last = n >> COARSE
    current = np.eye(n)[:last]
    for step in range(COARSE):
        size = last << step
        current = _unlift(current, np.eye(n)[size : 2 * size])
    both = np.zeros((n + 640, n))
    both[:n] = (KS * coarse.T)[order]
    both[n + 4 : 2 * n + 4] = current / KS
    out["coarse"] = _pair(both)
    return out


def _mask(lane, places, first, last, base=0):
    lanes = sorted(v - base for k, v in places.items() if first <= k < last)
    out, i = None, 0
    while i < len(lanes):
        j = i
        while j + 1 < len(lanes) and lanes[j + 1] == lanes[j] + 1:
            j += 1
        hit = (lane >= lanes[i]) & (lane <= lanes[j])
        out = hit if out is None else out | hit
        i = j + 1
    return out


def _ones(hit):
    return jnp.where(hit, 1.0, 0.0)


def _dot3(x, t):
    hi = x.astype(BF16)
    lo = (x - hi.astype(F32)).astype(BF16)
    d = functools.partial(jnp.dot, preferred_element_type=F32)
    both = d(jnp.concatenate([hi, lo], axis=0), t(0))
    return both[: x.shape[0]] + both[x.shape[0] :] + d(hi, t(1))


def _time(load, t, y, step, j):
    x = load(j, step)
    y[pl.ds(j, step)] = _dot3(x.reshape(step * 8, x.shape[2]), t).reshape(step, 8, y.shape[2])


class _Forward:
    def __init__(self, load, t, y, step):
        self.load, self.t, self.y, self.step, self.done = load, t, y, step, 0

    def __call__(self, j):
        ahead = min(j + self.step, self.y.shape[0] - 1)
        while self.done <= ahead:
            _time(self.load, self.t, self.y, self.step, self.done)
            self.done += self.step
        return self.y[j]


class _Backward:
    def __init__(self, y, t, store, step):
        self.y, self.t, self.store, self.step, self.left = y, t, store, step, {}

    def __call__(self, j, value):
        self.y[j] = value
        chunk = j // self.step
        self.left[chunk] = self.left.get(chunk, self.step) - 1
        if not self.left[chunk]:
            x = self.y[pl.ds(chunk * self.step, self.step)]
            out = _dot3(x.reshape(self.step * 8, x.shape[2]), self.t)
            self.store(chunk * self.step, self.step, out.reshape(self.step, 8, out.shape[1]))


def _table(ref, rows, cols, *lead):
    r, c = pl.ds(*rows), pl.ds(*cols)
    return lambda i: ref[(*lead, i, r, c)]


def _sublane(lanes):
    return lax.broadcasted_iota(jnp.int32, (8, lanes), 0)


def _lane(rows=8):
    return lax.broadcasted_iota(jnp.int32, (rows, 128), 1)


def _wide(v, lanes):
    return v if lanes == 128 else jnp.concatenate([v] * (lanes // 128), axis=1)


class _QuarterWrap:
    def __init__(self):
        self.sub, self.group = _sublane(128), _lane() // 32

    def after(self, first, last):
        moved = pltpu.roll(first, 96, 1)
        moved = jnp.where(self.group == 3, pltpu.roll(moved, 7, 0), moved)
        return jnp.where((self.group == 3) & (self.sub == 7), last, moved)

    def before(self, last, first):
        moved = pltpu.roll(last, 32, 1)
        moved = jnp.where(self.group == 0, pltpu.roll(moved, 1, 0), moved)
        return jnp.where((self.group == 0) & (self.sub == 0), first, moved)


def _quarters(values):
    group = _lane() // 32
    out = []
    for c in range(3):
        v = values[0]
        for g in range(1, 4):
            v = jnp.where(group == g, values[(24 * g + 8 * c) // 32], v)
        out.append(v)
    return out


class _Wrap:
    def __init__(self, lanes):
        sub = _sublane(lanes)
        self.last, self.first = sub == 7, sub == 0

    def after(self, first, last):
        return jnp.where(self.last, last, pltpu.roll(first, 7, 0))

    def before(self, last, first):
        return jnp.where(self.first, first, pltpu.roll(last, 1, 0))


def _coefs(weights, lanes):
    return [[_wide(c * v, lanes) for v in weights] for c in (A1, B1, A2, B2)]


def _chan_forward(get, n, weights, lanes, put_low, put_high, wrap=None):
    wrap = wrap or _Wrap(lanes)
    ca, cb, cc, cd = _coefs(weights, lanes)
    per = n // 3
    first = get(0)
    e, o1, e1, o2 = {0: first}, {}, {}, {}

    def high(k, v):
        o2[k] = v
        put_high(k, k // per, v)

    def low(k):
        put_low(k, k // per, e1[k] + cd[k // per] * (o2[k - 1] + o2[k]))

    for k in range(n):
        q = k // per
        e[k + 1] = get(2 * k + 2) if k + 1 < n else wrap.after(first, e[k])
        o1[k] = get(2 * k + 1) + ca[q] * (e[k] + e[k + 1])
        if k >= 1:
            e1[k] = e[k] + cb[q] * (o1[k - 1] + o1[k])
        if k >= 2:
            high(k - 1, o1[k - 1] + cc[(k - 1) // per] * (e1[k - 1] + e1[k]))
        if k >= 3:
            low(k - 1)
    e1[0] = first + cb[0] * (wrap.before(o1[n - 1], o1[0]) + o1[0])
    high(0, o1[0] + cc[0] * (e1[0] + e1[1]))
    high(n - 1, o1[n - 1] + cc[2] * (e1[n - 1] + wrap.after(e1[0], e1[n - 1])))
    o2[-1] = wrap.before(o2[n - 1], o2[0])
    for k in (0, 1, n - 1):
        low(k)


def _chan_inverse(get_low, get_high, n, weights, lanes, put, wrap=None):
    wrap = wrap or _Wrap(lanes)
    ca, cb, cc, cd = _coefs(weights, lanes)
    per = n // 3
    o = {0: get_high(0)}
    o[-1] = wrap.before(get_high(n - 1), o[0])
    e1, o1, e2 = {}, {}, {}

    def even(k):
        e2[k] = e1[k] - cb[k // per] * (o1[k - 1] + o1[k])
        put(2 * k, e2[k])

    def odd(k):
        put(2 * k + 1, o1[k] - ca[k // per] * (e2[k] + e2[k + 1]))

    for k in range(n):
        q = k // per
        if k:
            o[k] = get_high(k)
        e1[k] = get_low(k) - cd[q] * (o[k - 1] + o[k])
        if k >= 1:
            o1[k - 1] = o[k - 1] - cc[(k - 1) // per] * (e1[k - 1] + e1[k])
        if k >= 2:
            even(k - 1)
        if k >= 3:
            odd(k - 2)
    o1[n - 1] = o[n - 1] - cc[2] * (e1[n - 1] + wrap.after(e1[0], e1[n - 1]))
    o1[-1] = wrap.before(o1[n - 1], o1[0])
    even(n - 1)
    if n > 2:
        odd(n - 2)
    even(0)
    odd(0)
    e2[n] = wrap.after(e2[0], e2[n - 1])
    odd(n - 1)


class _Squares:
    def __init__(self):
        self.acc = {}

    def add(self, key, v):
        self.acc[key] = v * v if key not in self.acc else self.acc[key] + v * v

    def total(self, rows, tiles):
        out = None
        for q in range(3):
            part = None
            for (band, tile), lanes in tiles.items():
                v = self.acc[(band, tile, q)] * (KS * KS if band == "low" else 1.0 / (KS * KS))
                v = v if lanes is None else v * lanes
                part = v if part is None else part + v
            part = part * rows[q]
            out = part if out is None else out + part
        return out


def _tile(v, i):
    return v[:, 128 * i : 128 * (i + 1)]


def _blocks(w, level):
    return [w[level, q] for q in range(3)]


def _own_rows(core):
    block = 3 * _sublane(128)
    return [
        jnp.where(core == 0, _ones(block + q < 16), _ones(block + q >= 8)) for q in range(3)
    ]


def _load_kernel(
    sc, x_all, gauge_table_all, gauge_index_all, own_all,
    low, high, ends, own_table, w,
    x, gauge_table, gauge_index, sems,
):
    core = sc[0]
    copies = [
        pltpu.make_async_copy(src, dst, sems.at[i])
        for i, (src, dst) in enumerate(
            (
                (gauge_index_all, gauge_index),
                (gauge_table_all, gauge_table),
                (own_all, own_table),
                *((x_all.at[pl.ds(256 * i, 256)], x.at[pl.ds(256 * i, 256)]) for i in range(4)),
            )
        )
    ]
    for c in copies:
        c.start()
    for c in copies[:2]:
        c.wait()
    index = gauge_index[...]
    table_rows = gauge_table[...]
    weights = jnp.zeros(index.shape, F32)
    for g in range(GTAB):
        weights = weights + jnp.where(index == g, table_rows[:, g : g + 1], 0.0)
    block = lax.broadcasted_iota(jnp.int32, (8, NBLK), 1) - 3 * lax.broadcasted_iota(jnp.int32, (8, NBLK), 0)
    block = block - 8 * core
    for l in range(LEVELS):
        for q in range(3):
            hit = jnp.where(block == q, weights[l : l + 1], 0.0)
            w[l, q] = jnp.broadcast_to(jnp.sum(hit, axis=1, keepdims=True), (8, 128))
    copies[2].wait()
    for c in copies[3:]:
        c.wait()
    _first(x, own_table, low, high, ends, 0, range(0, OWN, 128))


def _first(x, table, low, high, ends, at, blocks):
    lane = _lane(128)
    for r in blocks:
        v = x[pl.ds(r, 128), :]
        y = _dot3(v, _table(table, (0, 256), (0, 256)))
        rows = pl.ds(at + r, 128)
        low[rows, :] = y[:, 0:128]
        high[rows, :] = y[:, 128:256]
        ends[rows, :] = jnp.where(lane < 32, v[:, 0:128], v[:, 128:256])


def _own_kernel(
    sc, recv, own_low, own_high, own_ends, table, w,
    right, left, low0, a1l, fh, details, sums,
    fl, fe, y1,
):
    core = sc[0]
    at_own = pl.multiple_of(core * HALO, 8)
    at_recv = pl.multiple_of((1 - core) * OWN, 8)
    for src, dst in ((own_low, fl), (own_high, fh), (own_ends, fe)):
        for r in range(0, OWN, 128):
            dst[pl.ds(at_own + r, 128), :] = src[pl.ds(r, 128), :]
    theirs = recv.at[pl.ds(at_own, HALO)]
    _first(theirs, table, fl, fh, fe, at_recv, range(0, HALO, 128))
    lane = _lane()
    group = lane // 8
    for i in range(12):
        to_right, to_left = None, None
        for g in range(16):
            v = fe[pl.ds(12 * g + i, 8, stride=SEG), :]
            v = pltpu.roll(v, 8 * g, 1) if g else v
            to_left = v if to_left is None else jnp.where(group == g, v, to_left)
            to_right = v if to_right is None else jnp.where(group == (g + 15) % 16, v, to_right)
        right[i] = to_right
        left[i] = to_left
    rows = _own_rows(core)
    sq = _Squares()

    def put_low(k, q, v):
        low0[k] = v

    def put_high(k, q, v):
        details[k] = v
        sq.add(("high", 0, q), v)

    _chan_forward(lambda j: fl[pl.ds(j, 8, stride=SEG), :], 96, _blocks(w, 0), 128, put_low, put_high)
    sums[0] = sq.total(rows, {("high", 0): None})
    for i in range(6):
        to_right, to_left = None, None
        for g in range(16):
            v = low0[6 * g + i]
            a = pltpu.roll(v, (8 * g - 118) % 128, 1)
            b = pltpu.roll(v, (8 * g + 6) % 128, 1)
            to_right = a if to_right is None else jnp.where(group == g, a, to_right)
            to_left = b if to_left is None else jnp.where(group == (g + 1) % 16, b, to_left)
        right[12 + i] = to_right
        left[12 + i] = to_left
    sq1 = _Squares()

    def put_low1(k, q, v):
        a1l[k] = v
        details[96 + k] = v
        sq1.add(("low", 0, q), v)
        if k >= 26:
            packed = jnp.where(lane < 64, a1l[k - 24], pltpu.roll(v, 64, 1))
            right[k - 6] = packed
            left[k - 6] = packed

    def put_high1(k, q, v):
        details[144 + k] = v
        sq1.add(("high", 0, q), v)

    get = _Forward(lambda j, n: low0[pl.ds(j, n)], _table(table, (256, 128), (0, 128)), y1, 24)
    _chan_forward(get, 48, _blocks(w, 1), 128, put_low1, put_high1)
    for k in (24, 25):
        packed = jnp.where(lane < 64, a1l[k - 24], pltpu.roll(a1l[k], 64, 1))
        right[k - 6] = packed
        left[k - 6] = packed
    sums[1] = sq1.total(rows, {("low", 0): _ones(_mask(lane, OWN_HIGH1, 0, 64)), ("high", 0): None})


def _bands(details):
    out, at = [], 0
    for n in (24, 48, 24, 12, 6, 3):
        out += [details.at[pl.ds(at, n)], details.at[pl.ds(at + n, n)]]
        at += 2 * n
    return out


def _aside_kernel(
    sc, fh, w, rim_all, back_all, coarse_all, rim_table, back_table, coarse_table, details, sums, sems
):
    copies = []
    mine = pl.multiple_of(512 + 16 * (sc[2] // 4), 16)
    for i in range(2):
        for src, dst, start, n in (
            (rim_all.at[sc[1], i], rim_table.at[i], 0, 448),
            (rim_all.at[sc[1], i], rim_table.at[i], 448, 448),
            (back_all.at[sc[1], i], back_table.at[i], 0, 896),
            (coarse_all.at[i], coarse_table.at[i], 0, 512),
        ):
            rows = pl.ds(start, n)
            copies.append(pltpu.make_async_copy(src.at[rows], dst.at[rows], sems.at[len(copies)]))
        src, dst = coarse_all.at[i, pl.ds(mine, 128)], coarse_table.at[i, pl.ds(512, 128)]
        copies.append(pltpu.make_async_copy(src, dst, sems.at[len(copies)]))
    for c in copies:
        c.start()
    rows = _own_rows(sc[0])
    sq = _Squares()

    def put_low(k, q, v):
        details[k] = v
        sq.add(("low", 0, q), v)

    def put_high(k, q, v):
        details[96 + k] = v
        sq.add(("high", 0, q), v)

    _chan_forward(lambda j: fh[pl.ds(j, 8, stride=SEG), :], 96, _blocks(w, 0), 128, put_low, put_high)
    sums[...] = sq.total(rows, {("low", 0): None, ("high", 0): None})
    for c in copies:
        c.wait()


def _rim_kernel(
    sc, right, left, from_left, from_right, low0, a1l, own_sums, more_sums, table, w,
    details, payload,
    rim, y0, y1, x2, y2, y3, y4, y5, l5, h5, flat,
):
    core = sc[0]
    rlow0, rhigh0, r1l, r1h, a2l, a2h, a3l, a3h, a4l, a4h, a5l, a5h = _bands(details)
    lane = _lane()
    rows = _own_rows(core)
    totals = []

    def level(l, load, n, t, y, step, lanes, low, high, own_low, own_high, pairs):
        quarters = l == 0
        weights = _blocks(w, l)
        place = lane % 32 if quarters else lane
        sq = _Squares()

        def put_low(k, q, value):
            low[k] = value
            sq.add(("low", 0, q), _tile(value, 0))

        def put_high(k, q, value):
            high[k] = value
            sq.add(("high", 0, q), _tile(value, 0))

        wrap = _QuarterWrap() if quarters else None
        weights = _quarters(weights) if quarters else weights
        get = y.__getitem__ if quarters else _Forward(load, t, y, step)
        _chan_forward(get, n, weights, lanes, put_low, put_high, wrap)
        is_high = _mask(place, own_high, 0, pairs)
        is_low = _mask(place, own_low, 0, pairs)
        total = sq.total(_quarters(rows) if quarters else rows, {("low", 0): _ones(is_high), ("high", 0): _ones(is_high | is_low)})
        totals.append(total + own_sums[l] if l < 2 else total)

    def pick(r, k, c, n):
        return _table(table, (r, k), (c, n))

    raw = pl.ds(0, 12)
    raw = jnp.concatenate([from_left[raw], left[raw], right[raw], from_right[raw]], axis=2)
    raw = _dot3(raw.reshape(96, 512), pick(384, 512, 0, 512))
    for h in range(4):
        y0[pl.ds(12 * h, 12)] = _tile(raw, h).reshape(12, 8, 128)
    level(0, None, 24, None, y0, 24, 128, rlow0, rhigh0, RIM_LOW0, RIM_HIGH0, 128)
    totals[0] = totals[0] + more_sums[...]
    for j in range(96):
        g, i = j // 24, j % 24
        mine = pltpu.roll(rlow0[i], 128 - 32 * g, 1) if g else rlow0[i]
        g, i = j // 6, 12 + j % 6
        theirs = jnp.where(lane // 8 == g, from_left[i], from_right[i])
        theirs = pltpu.roll(theirs, (32 - 8 * g) % 128, 1) if g != 4 else theirs
        rim[j] = jnp.where(lane < 32, mine, theirs)

    def load1(j, n):
        return jnp.concatenate([low0[pl.ds(j, n)], rim[pl.ds(j, n)]], axis=2)

    level(1, load1, 48, pick(0, 256, 0, 128), y1, 24, 128, r1l, r1h, RIM_LOW1, RIM_HIGH1, 64)
    for j in range(48):
        h, i = j // 24, 18 + j % 24
        b, a = from_left[i], from_right[i]
        if h == 0:
            a = pltpu.roll(a, 64, 1)
        else:
            b = pltpu.roll(b, 64, 1)
        x2[j, :, 0:128] = jnp.where(lane < 64, a1l[j], a)
        x2[j, :, 128:256] = jnp.where(lane < 64, b, r1l[j])
    level(2, lambda j, n: x2[pl.ds(j, n)], 24, pick(0, 256, 128, 128), y2, 24, 128, a2l, a2h, LOW2, HIGH2, 32)
    level(3, lambda j, n: a2l[pl.ds(j, n)], 12, pick(0, 128, 256, 128), y3, 24, 128, a3l, a3h, LOW3, HIGH3, 16)
    level(4, lambda j, n: a3l[pl.ds(j, n)], 6, pick(128, 128, 256, 128), y4, 12, 128, a4l, a4h, LOW4, HIGH4, 8)
    level(5, lambda j, n: a4l[pl.ds(j, n)], 3, pick(256, 128, 0, 256), y5, 6, 256, l5, h5, LOW5, HIGH5, 4)
    sub = _sublane(128)
    for j in range(3):
        a5l[j] = l5[j, :, 0:128]
        a5h[j] = h5[j, :, 0:128]
        flat[pl.ds(j, 8, stride=3), :] = jnp.where(lane % 16 < 7, l5[j, :, 128:256], h5[j, :, 128:256])
    sums = jnp.zeros((8, 128), F32)
    for l in range(LEVELS):
        sums = jnp.where(sub == l, jnp.sum(totals[l], axis=0, keepdims=True), sums)
    sums = jnp.where((lane == 16 * sub + 13) & (sub < LEVELS), jnp.sum(sums, axis=1, keepdims=True), 0.0)
    lines = []
    for h in range(2):
        mine = flat[pl.ds(pl.multiple_of(8 * core + 8 * h, 8), 8), :]
        mine = jnp.where(lane // 16 == sub, mine, 0.0)
        lines.append(jnp.sum(mine + sums if h == 0 else mine, axis=0, keepdims=True))
    block = jnp.where(sub % 2 == 0, lines[0], lines[1])
    for i in range(32):
        payload[pl.ds(8 * i, 8), :] = block


def _shrink(v, limit):
    return v - jnp.minimum(jnp.maximum(v, -limit), limit)


def _back_kernel(
    sc, mine, theirs, coarse_table, table, own_details, more_details, rim_details, w,
    out,
    both, gt, nears, cur, x5l, x5h, y5, y4, y3, y2, y1, c4, c3, c2, c1, c0, f0, f1, f2, yr, stage, sems,
):
    core, place = sc[0], sc[2]
    rlow0, rhigh0, r1l, r1h, a2l, a2h, a3l, a3h, a4l, a4h, a5l, a5h = _bands(rim_details)
    dhigh0, dlow0, dhigh1 = own_details.at[pl.ds(0, 96)], more_details.at[pl.ds(0, 96)], more_details.at[pl.ds(96, 96)]
    a1l, a1h = (own_details.at[pl.ds(96 + 48 * i, 48)] for i in range(2))
    lane = _lane()
    lane1 = _lane(1)
    sub = _sublane(128)
    both[0, 0:256, :] = mine[...]
    both[1, 0:256, :] = theirs[...]
    for h in range(2):
        halves = [both[g, pl.ds(h, NT, stride=2), :] for g in range(2)]
        if h == 0:
            total = jnp.sum(halves[0] + halves[1], axis=0, keepdims=True)
        for c in range(2):
            gt[c, h, 0:128, :] = jnp.transpose(jnp.where(core == c, halves[0], halves[1]))
    limits = []
    for l in range(LEVELS):
        entries = 3 * (C >> (l + 1)) * (S >> (l + 1))
        s = jnp.sum(jnp.where(lane1 == 16 * l + 13, total, 0.0), axis=1, keepdims=True)
        limits.append(jnp.sqrt(s * (1.0 / entries) + FLOOR))
    rows = [
        jnp.concatenate([gt[c, h, pl.ds(m, 8, stride=16), :] for m in range(4)], axis=1)
        for c in range(2)
        for h in range(2)
    ]
    coarse = _dot3(jnp.concatenate(rows, axis=0), lambda i: coarse_table[i, 0:512, :])
    highs = lax.broadcasted_iota(jnp.int32, (32, 512), 1) >= (S >> (LEVELS + COARSE))
    square = jnp.sum(jnp.where(highs, coarse * coarse, 0.0), axis=0, keepdims=True)
    square = jnp.sum(square, axis=1, keepdims=True)
    entries = (C >> LEVELS) * ((S >> LEVELS) - (S >> (LEVELS + COARSE)))
    limit = jnp.sqrt(square * (1.0 / entries) + FLOOR)
    coarse = jnp.where(highs, _shrink(coarse, limit), coarse)
    hi = coarse.astype(BF16)
    lo = (coarse - hi.astype(F32)).astype(BF16)
    for side, other in enumerate((jnp.maximum(place - 1, 0), jnp.minimum(place + 1, NT - 1))):
        for c in range(2):
            for h in range(2):
                row = pl.ds(2 * other + h, 1)
                line = jnp.broadcast_to(jnp.where(core == c, mine[row, :], theirs[row, :]), (8, 128))
                near = line
                for k in range(1, 8):
                    near = jnp.where(sub == k, pltpu.roll(line, 128 - 16 * k, 1), near)
                nears[side, pl.ds(16 * c + 8 * h, 8), :] = near
    for k in range(3):
        rows = pl.ds(8 * core + k, 8, stride=3)
        before, after = nears[0, rows, :], nears[1, rows, :]
        v = a5h[k]
        for at, near, shift in ((1, before, 122), (9, after, 2), (17, before, 7), (25, after, 15)):
            v = jnp.where((lane >= at) & (lane < at + 3), pltpu.roll(near, shift, 1), v)
        x5h[k] = v
        v = a5l[k]
        for at, near, shift in ((17, before, 13), (25, after, 21)):
            v = jnp.where((lane >= at) & (lane < at + 3), pltpu.roll(near, shift, 1), v)
        x5l[k] = v

    def nt(a, b):
        return lax.dot_general(a, b, (((1,), (1,)), ((), ())), preferred_element_type=F32)

    rows = pl.ds(512, 128)
    current = nt(hi, coarse_table[0, rows, :]) + nt(lo, coarse_table[0, rows, :]) + nt(hi, coarse_table[1, rows, :])
    cur[0:32, :] = pltpu.roll(current, (128 - 4 * (place % 4)) % 128, 1)

    def level(l, get_current, low, high, n, y, t, nxt, step, needed):
        tl = jnp.broadcast_to(limits[l] * (1.0 / KS), (8, 128))
        th = jnp.broadcast_to(limits[l] * KS, (8, 128))
        is_low = needed(lane)

        def get_low(k):
            return jnp.where(is_low, get_current(k), _shrink(low[k], tl))

        def store(j, m, value):
            nxt[pl.ds(j, m)] = value

        put = _Backward(y, t, store, step)
        _chan_inverse(get_low, lambda k: _shrink(high[k], th), n, _blocks(w, l), 128, put)

    def pick(r, k, c, n):
        return _table(table, (r, k), (c, n))

    level(
        5, lambda k: cur[pl.ds(8 * core + k, 8, stride=3), :], x5l, x5h, 3, y5, pick(768, 128, 0, 128), c4, 6, lambda i: i < 12
    )
    level(4, lambda k: c4[k], a4l, a4h, 6, y4, pick(640, 128, 128, 128), c3, 12, lambda i: i < 32)
    level(3, lambda k: c3[k], a3l, a3h, 12, y3, pick(640, 128, 0, 128), c2, 24, lambda i: i < 64)
    level(2, lambda k: c2[k], a2l, a2h, 24, y2, pick(512, 128, 0, 256), c1, 24, lambda i: i < 89)
    tl = jnp.broadcast_to(limits[1] * (1.0 / KS), (8, 256))
    th = jnp.broadcast_to(limits[1] * KS, (8, 256))
    lane2 = lax.broadcasted_iota(jnp.int32, (8, 256), 1)
    is_low1 = (lane2 < 64) | ((lane2 >= 192) & (lane2 < 208))

    def get_low1(k):
        v1 = jnp.concatenate([a1l[k], r1l[k]], axis=1)
        return jnp.where(is_low1, c1[k], _shrink(v1, tl))

    def get_high1(k):
        return _shrink(jnp.concatenate([a1h[k], r1h[k]], axis=1), th)

    def store1(j, m, value):
        c0[pl.ds(j, m)] = value

    put1 = _Backward(y1, pick(256, 256, 0, 256), store1, 24)
    _chan_inverse(get_low1, get_high1, 48, _blocks(w, 1), 256, put1)
    tl0 = jnp.broadcast_to(limits[0] * (1.0 / KS), (8, 128))
    th0 = jnp.broadcast_to(limits[0] * KS, (8, 256))
    group = lane // 32
    rim_low = lane % 32 < 8

    def get_low_rim(k):
        now = c0[k, :, 128:256]
        for q in range(1, 4):
            now = jnp.where(group == q, c0[24 * q + k, :, 128:256], now)
        return jnp.where(rim_low, now, _shrink(rlow0[k], tl0))

    def store_rim(j, m, value):
        for i in range(m):
            for q in range(4):
                v = pltpu.roll(value[i], 128 - 32 * q, 1) if q else value[i]
                f2[pl.ds(48 * q + j + i, 8, stride=SEG), :] = v

    put_rim = _Backward(yr, pick(768, 128, 128, 128), store_rim, 24)
    _chan_inverse(
        get_low_rim, lambda k: _shrink(rhigh0[k], th0[:, 0:128]), 24, _quarters(_blocks(w, 0)), 128, put_rim, _QuarterWrap()
    )

    def get_low0(k):
        return jnp.concatenate([c0[k, :, 0:128], _shrink(dlow0[k], tl0)], axis=1)

    def get_high0(k):
        return _shrink(jnp.concatenate([dhigh0[k], dhigh1[k]], axis=1), th0)

    def put0(j, value):
        for i, buf in enumerate((f0, f1)):
            buf[pl.ds(j, 8, stride=SEG), :] = _tile(value, i)

    _chan_inverse(get_low0, get_high0, 96, _blocks(w, 0), 256, put0)
    at_own = pl.multiple_of(core * HALO, 8)
    t = pick(0, 256, 0, 256)
    wide = _lane(128)
    copies = []
    for r in range(0, OWN, 128):
        rows = pl.ds(at_own + r, 128)
        done = pl.ds(r, 128)
        ends = f2[rows, :]
        v = _dot3(jnp.concatenate([f0[rows, :], f1[rows, :]], axis=1), t)
        stage[done, 0:128] = _tile(v, 0) + jnp.where(wide < 8, ends, 0.0)
        stage[done, 128:256] = _tile(v, 1) + jnp.where(wide >= 121, ends, 0.0)
        copies.append(pltpu.make_async_copy(stage.at[done], out.at[done], sems.at[r // 128]))
        copies[-1].start()
    for c in copies:
        c.wait()


VM = pl.BlockSpec(memory_space=pltpu.VMEM)
SM = pl.BlockSpec(memory_space=pltpu.SMEM)
HBM = pl.BlockSpec(memory_space=pltpu.HBM)
ROWS = (9 * SEG, 128)


def _call(kernel, name, limit, args, specs, outs, out_specs, scratch):
    args = [
        pltpu.with_memory_space_constraint(x, pltpu.HBM) if spec is HBM else x for x, spec in zip(args, specs)
    ]
    outs = [jax.ShapeDtypeStruct(s, F32) if isinstance(s, tuple) else s for s in outs]
    return pl.pallas_call(
        kernel,
        out_shape=[pltpu.HBM(s.shape, s.dtype) if spec is HBM else s for s, spec in zip(outs, out_specs)],
        in_specs=specs,
        out_specs=out_specs,
        scratch_shapes=[pltpu.VMEM(s, F32) if isinstance(s, tuple) else s for s in scratch],
        compiler_params=pltpu.CompilerParams(vmem_limit_bytes=limit << 20),
        name=name,
    )(*args)


def _shift(v, by):
    return lax.ppermute(v, "tm", [(i, (i + by) % NT) for i in range(NT)])


def shards(record, gauge_table, gauge_index):
    tables = _tables()
    core = lax.axis_index("chan")
    place = lax.axis_index("tm")
    variant = jnp.where(place == 0, 0, jnp.where(place == NT - 1, 2, 1))
    sc = jnp.stack([core, variant, place]).astype(jnp.int32)
    dma = pltpu.SemaphoreType.DMA
    recv = lax.ppermute(record, "chan", [(0, 1), (1, 0)])
    low, high, ends, own_table, w = _call(
        _load_kernel, "load", 12, (sc, record, gauge_table, gauge_index, tables["own"]),
        [SM] + [HBM] * 4,
        [(OWN, 128), (OWN, 128), (OWN, 128), jax.ShapeDtypeStruct((2, 384, 256), BF16), (LEVELS, 3, 8, 128)],
        [VM] * 5,
        [(OWN, 256), (LEVELS, GTAB), pltpu.VMEM((LEVELS, NBLK), jnp.int32), dma((7,))],
    )
    right, left, low0, a1l, fh, own_details, sums = _call(
        _own_kernel, "own", 12, (sc, recv, low, high, ends, own_table, w), [SM] + [VM] * 6,
        [(42, 8, 128), (42, 8, 128), (96, 8, 128), (48, 8, 128), ROWS, (192, 8, 128), (2, 8, 128)],
        [VM] * 7,
        [ROWS, ROWS, (96, 8, 128)],
    )
    from_left, from_right = _shift(right, 1), _shift(left, -1)
    rim_table, back_table, coarse_table, more_details, more_sums = _call(
        _aside_kernel, "aside", 6, (sc, fh, w, tables["rim"], tables["back"], tables["coarse"]),
        [SM, VM, VM, HBM, HBM, HBM],
        [jax.ShapeDtypeStruct((2, 896, 512), BF16), jax.ShapeDtypeStruct((2, 896, 256), BF16),
         jax.ShapeDtypeStruct((2, 640, 512), BF16), (192, 8, 128), (8, 128)],
        [VM] * 5,
        [dma((10,))],
    )
    rim_details, payload = _call(
        _rim_kernel, "rim", 16,
        (sc, right, left, from_left, from_right, low0, a1l, sums, more_sums, rim_table, w), [SM] + [VM] * 10,
        [(234, 8, 128), (256, 128)], [VM] * 2,
        [(96, 8, 128), (48, 8, 128), (96, 8, 128), (48, 8, 256), (48, 8, 128), (24, 8, 128), (12, 8, 128),
         (6, 8, 256), (3, 8, 256), (3, 8, 256), (32, 128)],
    )
    mine = lax.all_to_all(payload, "tm", split_axis=0, concat_axis=0, tiled=True)
    theirs = lax.ppermute(mine, "chan", [(0, 1), (1, 0)])
    (out,) = _call(
        _back_kernel, "back", 24, (sc, mine, theirs, coarse_table, back_table, own_details, more_details, rim_details, w),
        [SM] + [VM] * 8, [(OWN, 256)], [HBM],
        [
            (2, 264, 128), (2, 2, 144, 128), (2, 40, 128), (40, 128), (3, 8, 128), (3, 8, 128),
            (6, 8, 128), (12, 8, 128), (24, 8, 128), (48, 8, 128), (96, 8, 256),
            (6, 8, 128), (12, 8, 128), (24, 8, 128), (48, 8, 256), (96, 8, 256),
            ROWS, ROWS, ROWS, (48, 8, 128), (OWN, 256), dma((8,)),
        ],
    )
    return out


def solution(mesh):
    return jax.shard_map(
        shards,
        mesh=mesh,
        in_specs=(P("chan", "tm"), P(), P()),
        out_specs=P("chan", "tm"),
        check_vma=False,
    )
```
